32 devices in a mesh: seq: 8 (over y, x, core), tensor: 4 (over z).
Axes of the slice: x: 2, y: 2, z: 4, core: 2. Of those that a mesh axis runs over, the one named last changes fastest.
Arguments:
- byte_states: bfloat16 [8192, 1024], P('seq'), may hold values from -6 to 6
- byte_patch: int32 [8192], P('seq'), may hold values from 0 to 1023, as said below
- patch_len: int32 [1024], replicated, may hold values from 1 to 1024, as said below
- cross_query: bfloat16 [1024, 4096], P('seq', 'tensor'), may hold values from -0.75 to 0.75
- cross_key: bfloat16 [1024, 4096], P('seq', 'tensor'), may hold values from -0.375 to 0.375
- cross_value: bfloat16 [1024, 4096], P('seq', 'tensor'), may hold values from -0.1875 to 0.1875
- cross_out: bfloat16 [4096, 4096], P('tensor', 'seq'), may hold values from -0.09375 to 0.09375
- norm_gain: float32 [4096], replicated, may hold values from 0.5 to 1.5
- latent_query: bfloat16 [4096, 4096], P('seq', 'tensor'), may hold values from -0.1875 to 0.1875
- latent_key: bfloat16 [4096, 4096], P('seq', 'tensor'), may hold values from -0.1875 to 0.1875
- latent_value: bfloat16 [4096, 4096], P('seq', 'tensor'), may hold values from -0.09375 to 0.09375
- latent_out: bfloat16 [4096, 4096], P('tensor', 'seq'), may hold values from -0.09375 to 0.09375
Outputs:
- patch_latent: bfloat16 [1024, 4096], P('seq', 'tensor')
The draws below stay inside these ranges and needn't reach their ends.
Inputs may be any that keep to these rules, and one draw needn't show every extreme that they name: `byte_patch`: within each aligned block of 1024 bytes the numbers never fall and rise by at most one from byte to byte, and the block's first byte starts a new patch, so no patch spans two blocks. Block k begins with patch number k * 128 + r with -64 <= r < 64; the first block begins with 0 and the last ends with 1023. A block holds 1 to 255 patches; some block holds exactly 255 and the block after it exactly one. patch_len[p] is the number of bytes b with byte_patch[b] = p.
All inputs are finite; a program needn't handle non-finite values.
Results may differ from the reference program's by a relative error of at most 0.028.
Values may be sent and summed in bfloat16 or wider, within the bound.
No kernel may reach another device: no remote copies, remote signals or barrier semaphores. Data moves between devices by JAX's collectives and lax.ppermute only.
A program may use at most 128 MiB of HBM per device.

```python
import math
import jax
import jax.numpy as jnp
from jax import lax

DB = 1024
D = 4096
HEADS = 32
HEAD_DIM = 128
PATCH_DEV = 128
BYTE_DEV = 1024
BYTES = 8192
PATCHES = 1024


def patch_layout(key):
    folded = jax.random.fold_in(key, 7)
    shards = BYTES // BYTE_DEV
    half_width = PATCH_DEV // 2
    drift_key, pick_key, cut_key = jax.random.split(folded, 3)
    interior = jax.random.randint(drift_key, (shards + 1,), -half_width, half_width)
    forced = 1 + jax.random.randint(pick_key, (), 0, shards - 3)
    places = jnp.arange(shards + 1)
    drifts = jnp.where(places == forced, -half_width, interior)
    drifts = jnp.where(places == forced + 1, half_width - 1, drifts)
    drifts = jnp.where(places == forced + 2, -half_width, drifts)
    drifts = jnp.where((places == 0) | (places == shards), 0, drifts)
    counts = PATCH_DEV + drifts[1:] - drifts[:-1]
    firsts = jnp.arange(shards) * PATCH_DEV + drifts[:-1]
    shard_keys = jax.random.split(cut_key, shards)
    orders = jax.vmap(lambda single: jax.random.permutation(single, BYTE_DEV - 1))(shard_keys)
    cut_mask = orders < (counts - 1)[:, None]
    starts = jnp.concatenate([jnp.ones((shards, 1), jnp.int32), cut_mask.astype(jnp.int32)], axis=1)
    local_rank = jnp.cumsum(starts, axis=1) - 1
    return (firsts[:, None] + local_rank).reshape(BYTES).astype(jnp.int32)


def draw_byte_patch(key, part):
    return patch_layout(key)


def draw_patch_len(key, part):
    patches = patch_layout(key)
    return jax.ops.segment_sum(jnp.ones((BYTES,), jnp.int32), patches, num_segments=PATCHES).astype(jnp.int32)


def block_levels(stream_key, dims, pieces, smallest, largest):
    def one(dim, blocks):
        heights = jax.random.uniform(jax.random.fold_in(jax.random.fold_in(stream_key, 6), dim), (blocks,), jnp.float32, smallest / len(pieces), largest / len(pieces))
        return jnp.repeat(jnp.exp(heights), dims[dim] // blocks).reshape((-1,) + (1,) * (len(dims) - dim - 1))

    level = one(*pieces[0])
    for cut in pieces[1:]:
        level = level * one(*cut)
    return level


def noise(key, shape, spread, bound, pieces=(), held_as=jnp.bfloat16):
    factor_of = block_levels(key, shape, pieces, -0.22, 0.18) if pieces else 1.0
    result = jax.random.normal(key, shape, jnp.float32) * spread * factor_of
    return jnp.minimum(jnp.maximum(result, -bound), bound).astype(held_as)


def setup_inputs(seed: int = 0) -> dict:
    keys = jax.random.split(jax.random.key(seed), 13)
    return {
        "byte_states": noise(keys[0], (BYTES, DB), 1.0, 6.0, ((0, 8),)),
        "byte_patch": draw_byte_patch(jax.random.fold_in(keys[12], 71), 0),
        "patch_len": draw_patch_len(jax.random.fold_in(keys[12], 71), 0),
        "cross_query": noise(keys[3], (DB, HEADS * HEAD_DIM), (DB // 16) ** -0.5, 0.75, ((0, 8), (1, 4))),
        "cross_key": noise(keys[4], (DB, HEADS * HEAD_DIM), (DB // 4) ** -0.5, 0.375, ((0, 8), (1, 4))),
        "cross_value": noise(keys[5], (DB, HEADS * HEAD_DIM), DB ** -0.5, 0.1875, ((0, 8), (1, 4))),
        "cross_out": noise(keys[6], (HEADS * HEAD_DIM, D), (HEADS * HEAD_DIM) ** -0.5, 0.09375, ((0, 4), (1, 8))),
        "norm_gain": jnp.clip(1.0 + 0.1 * jax.random.normal(keys[7], (D,), jnp.float32), 0.5, 1.5),
        "latent_query": noise(keys[8], (D, HEADS * HEAD_DIM), (D // 4) ** -0.5, 0.1875, ((0, 8), (1, 4))),
        "latent_key": noise(keys[9], (D, HEADS * HEAD_DIM), (D // 4) ** -0.5, 0.1875, ((0, 8), (1, 4))),
        "latent_value": noise(keys[10], (D, HEADS * HEAD_DIM), D ** -0.5, 0.09375, ((0, 8), (1, 4))),
        "latent_out": noise(keys[11], (HEADS * HEAD_DIM, D), (HEADS * HEAD_DIM) ** -0.5, 0.09375, ((0, 4), (1, 8))),
    }


score_cap = 30.0
norm_eps = 1e-05

def capped_exp(scores):
    return jnp.exp(score_cap * jnp.tanh(scores / score_cap))

def rounded(value):
    return lax.optimization_barrier(value.astype(jnp.bfloat16))

def reference(byte_states, byte_patch, patch_len, cross_query, cross_key, cross_value, cross_out, norm_gain, latent_query, latent_key, latent_value, latent_out):
    inner_width = HEADS * HEAD_DIM
    byte_sums = jax.ops.segment_sum(byte_states.astype(jnp.float32), byte_patch, num_segments=PATCHES)
    pooled = rounded(byte_sums / patch_len.astype(jnp.float32)[:, None])
    cross_q = rounded(jnp.dot(pooled, cross_query, preferred_element_type=jnp.float32))
    cross_k = rounded(jnp.dot(byte_states, cross_key, preferred_element_type=jnp.float32))
    cross_v = rounded(jnp.dot(byte_states, cross_value, preferred_element_type=jnp.float32))
    query_bytes = jnp.take(cross_q, byte_patch, axis=0).astype(jnp.float32)
    scores = (query_bytes * cross_k.astype(jnp.float32)).reshape(BYTES, HEADS, HEAD_DIM).sum(axis=2) / math.sqrt(HEAD_DIM)
    byte_raw = capped_exp(scores)
    byte_total = jax.ops.segment_sum(byte_raw, byte_patch, num_segments=PATCHES)
    byte_weight = rounded(byte_raw / jnp.take(byte_total, byte_patch, axis=0))
    weighted = byte_weight.astype(jnp.float32)[:, :, None] * cross_v.astype(jnp.float32).reshape(BYTES, HEADS, HEAD_DIM)
    cross_heads = rounded(jax.ops.segment_sum(weighted.reshape(BYTES, inner_width), byte_patch, num_segments=PATCHES))
    latent_in = rounded(jnp.dot(cross_heads, cross_out, preferred_element_type=jnp.float32))
    hidden = latent_in.astype(jnp.float32)
    mean_square = lax.optimization_barrier(jnp.mean(hidden * hidden, axis=1, keepdims=True))
    normed = rounded(hidden * lax.rsqrt(mean_square + norm_eps) * norm_gain[None, :])
    latent_q = rounded(jnp.dot(normed, latent_query, preferred_element_type=jnp.float32))
    latent_k = rounded(jnp.dot(normed, latent_key, preferred_element_type=jnp.float32))
    latent_v = rounded(jnp.dot(normed, latent_value, preferred_element_type=jnp.float32))

    def split_heads(matrix):
        return matrix.reshape(PATCHES, HEADS, HEAD_DIM).transpose(1, 0, 2)
    positions = jnp.arange(PATCHES, dtype=jnp.int32)
    allowed = positions[None, :] <= positions[:, None]

    def head_attention(operands):
        head_q, head_k, head_v = operands
        head_scores = jnp.dot(head_q.astype(jnp.float32), head_k.astype(jnp.float32).T, preferred_element_type=jnp.float32) / math.sqrt(HEAD_DIM)
        attn_raw = jnp.where(allowed, capped_exp(head_scores), jnp.zeros_like(head_scores))
        attn_total = lax.optimization_barrier(jnp.sum(attn_raw, axis=1, keepdims=True))
        attn_weight = rounded(attn_raw)
        summed = jnp.dot(attn_weight.astype(jnp.float32), head_v.astype(jnp.float32), preferred_element_type=jnp.float32)
        return (summed / attn_total).astype(jnp.bfloat16)
    per_head = lax.map(head_attention, (split_heads(latent_q), split_heads(latent_k), split_heads(latent_v)))
    attended = per_head.transpose(1, 0, 2).reshape(PATCHES, inner_width)
    projected = jnp.dot(attended, latent_out, preferred_element_type=jnp.float32)
    return (hidden + projected).astype(jnp.bfloat16)
```

```python
import math

import jax
import jax.numpy as jnp
from jax import lax
from jax.sharding import PartitionSpec as P

HEAD_DIM = 128
PATCH_DEV = 128


score_cap = 30.0
norm_eps = 1e-05


def shifted(block, axis, distance):
    devices = range(lax.axis_size(axis))
    route = [(i - distance, i) for i in devices if i - distance in devices]
    return lax.ppermute(block, axis, route)


def capped_exp(scores):
    return jnp.exp(score_cap * jnp.tanh(scores / score_cap))


def contract_rows(left, right):
    return lax.dot_general(
        left,
        right,
        (((0,), (0,)), ((), ())),
        precision=lax.Precision.HIGHEST,
        preferred_element_type=jnp.float32,
    )


def per_device_gathered(
    byte_states,
    byte_patch,
    patch_len,
    cross_query,
    cross_key,
    cross_value,
    cross_out,
    norm_gain,
    latent_query,
    latent_key,
    latent_value,
    latent_out,
):
    seq_index = lax.axis_index("seq")
    tensor_count = lax.axis_size("tensor")
    (
        cross_query,
        cross_key,
        cross_value,
        latent_query,
        latent_key,
        latent_value,
        cross_out,
        latent_out,
    ) = (
        lax.all_gather(cross_query, "seq", axis=0, tiled=True),
        lax.all_gather(cross_key, "seq", axis=0, tiled=True),
        lax.all_gather(cross_value, "seq", axis=0, tiled=True),
        lax.all_gather(latent_query, "seq", axis=0, tiled=True),
        lax.all_gather(latent_key, "seq", axis=0, tiled=True),
        lax.all_gather(latent_value, "seq", axis=0, tiled=True),
        lax.all_gather(cross_out, "seq", axis=1, tiled=True),
        lax.all_gather(latent_out, "seq", axis=1, tiled=True),
    )
    latent_width = cross_out.shape[1]
    local_width = cross_out.shape[0]
    head_count = local_width // HEAD_DIM
    slot_count = 2 * PATCH_DEV
    byte_count = byte_states.shape[0]
    first_patch = byte_patch[0]
    slot_of = byte_patch - first_patch
    onehot_mask = slot_of[:, None] == jnp.arange(slot_count, dtype=jnp.int32)[None, :]
    onehot = onehot_mask.astype(jnp.bfloat16)
    onehot_float = onehot_mask.astype(jnp.float32)
    byte_sums = lax.dot_general(
        onehot, byte_states, (((0,), (0,)), ((), ())), preferred_element_type=jnp.float32
    )
    lengths_all = jnp.concatenate([patch_len, jnp.ones((slot_count,), jnp.int32)])
    lengths = lax.dynamic_slice_in_dim(lengths_all, first_patch, slot_count)
    pooled = (byte_sums / lengths.astype(jnp.float32)[:, None]).astype(jnp.bfloat16)
    query_slots = jnp.dot(pooled, cross_query, preferred_element_type=jnp.float32).astype(
        jnp.bfloat16
    )
    byte_keys = jnp.dot(byte_states, cross_key, preferred_element_type=jnp.float32).astype(
        jnp.bfloat16
    )
    byte_values = jnp.dot(byte_states, cross_value, preferred_element_type=jnp.float32).astype(
        jnp.bfloat16
    )
    query_bytes = jnp.dot(onehot, query_slots, preferred_element_type=jnp.float32)
    scores = (query_bytes * byte_keys.astype(jnp.float32)).reshape(
        byte_count, head_count, HEAD_DIM
    ).sum(axis=2) / math.sqrt(HEAD_DIM)
    byte_raw = capped_exp(scores)
    totals = contract_rows(onehot_float, byte_raw)
    totals = jnp.where(totals > 0.0, totals, 1.0)
    totals_bytes = jnp.dot(
        onehot_float, totals, precision=lax.Precision.HIGHEST, preferred_element_type=jnp.float32
    )
    byte_weight = (byte_raw / totals_bytes).astype(jnp.bfloat16)
    weighted = (
        byte_weight.astype(jnp.float32)[:, :, None]
        * byte_values.astype(jnp.float32).reshape(byte_count, head_count, HEAD_DIM)
    ).reshape(byte_count, local_width)
    cross_heads = contract_rows(onehot_float, weighted).astype(jnp.bfloat16)
    padding = jnp.zeros((2 * PATCH_DEV, cross_heads.shape[1]), cross_heads.dtype)
    padded = jnp.concatenate([padding, cross_heads, padding], axis=0)
    offset = seq_index * PATCH_DEV - first_patch + 2 * PATCH_DEV
    padded, offset = (padded, offset)
    owned_heads = lax.dynamic_slice_in_dim(padded, offset, PATCH_DEV, 0)
    for offset_step in (-1, 1):
        window = lax.dynamic_slice_in_dim(padded, offset + offset_step * PATCH_DEV, PATCH_DEV, 0)
        owned_heads = owned_heads + shifted(window, "seq", offset_step)
    partial_value = jnp.dot(owned_heads, cross_out, preferred_element_type=jnp.float32)
    latent_in = lax.psum(partial_value, "tensor").astype(jnp.bfloat16)
    hidden = latent_in.astype(jnp.float32)
    mean_square = jnp.mean(hidden * hidden, axis=1, keepdims=True)
    normed = (hidden * lax.rsqrt(mean_square + norm_eps) * norm_gain[None, :]).astype(jnp.bfloat16)
    query = (
        jnp.dot(normed, latent_query, preferred_element_type=jnp.float32)
        .astype(jnp.bfloat16)
        .reshape(PATCH_DEV, head_count, HEAD_DIM)
    )
    key_rows = jnp.dot(normed, latent_key, preferred_element_type=jnp.float32).astype(jnp.bfloat16)
    value_rows = jnp.dot(normed, latent_value, preferred_element_type=jnp.float32).astype(
        jnp.bfloat16
    )
    positions = seq_index * PATCH_DEV + jnp.arange(PATCH_DEV, dtype=jnp.int32)
    key_piece = lax.all_gather(key_rows, "seq", axis=0, tiled=True)
    value_piece = lax.all_gather(value_rows, "seq", axis=0, tiled=True)
    piece_rows = key_piece.shape[0]
    key_piece = key_piece.reshape(piece_rows, head_count, HEAD_DIM)
    value_piece = value_piece.reshape(piece_rows, head_count, HEAD_DIM)
    piece_scores = jnp.einsum(
        "qhd,khd->hqk", query, key_piece, preferred_element_type=jnp.float32
    ) / math.sqrt(HEAD_DIM)
    key_positions = jnp.arange(piece_rows, dtype=jnp.int32)
    allowed = key_positions[None, :] <= positions[:, None]
    exp_scores = jnp.where(allowed[None, :, :], capped_exp(piece_scores), 0.0)
    denominator = jnp.sum(exp_scores, axis=2)
    numerator = jnp.einsum(
        "hqk,khd->hqd",
        exp_scores.astype(jnp.bfloat16),
        value_piece,
        preferred_element_type=jnp.float32,
    )
    numerator, denominator = (numerator, denominator)
    attended = (numerator / denominator[:, :, None]).astype(jnp.bfloat16)
    attended = attended.transpose(1, 0, 2).reshape(PATCH_DEV, local_width)
    projected = jnp.dot(attended, latent_out, preferred_element_type=jnp.float32)
    mixed_sum = lax.psum_scatter(projected, "tensor", scatter_dimension=1, tiled=True)
    column_width = latent_width // tensor_count
    residual = lax.dynamic_slice_in_dim(
        hidden, lax.axis_index("tensor") * column_width, column_width, 1
    )
    return (residual + mixed_sum).astype(jnp.bfloat16)


def dot(left, right):
    return jnp.dot(left, right, preferred_element_type=jnp.float32)


def exchanged(block, axis, distance):
    route = [(i, i ^ distance) for i in range(lax.axis_size(axis))]
    return lax.ppermute(block, axis, route)


def core_swapped(block):
    return exchanged(block, "seq", 1)


def columns(matrix, index, width):
    return lax.dynamic_slice_in_dim(matrix, index * width, width, 1)


def rows(matrix, index, height):
    return lax.dynamic_slice_in_dim(matrix, index * height, height, 0)


def per_device(
    byte_states,
    byte_patch,
    patch_len,
    cross_query,
    cross_key,
    cross_value,
    cross_out,
    norm_gain,
    latent_query,
    latent_key,
    latent_value,
    latent_out,
):
    seq = lax.axis_index("seq")
    tensor = lax.axis_index("tensor")
    seq_count = lax.axis_size("seq")
    tensor_count = lax.axis_size("tensor")
    chip_count = seq_count // 2
    chip, core = seq // 2, seq % 2
    other = 1 - core
    patch_count = patch_len.shape[0]
    patch_dev = patch_count // seq_count
    chip_patches = 2 * patch_dev
    spill = patch_dev // 2
    slot_count = chip_patches + 2 * spill
    local_width = cross_query.shape[1]
    half_width = local_width // 2
    half_heads = half_width // HEAD_DIM
    key_rows = cross_query.shape[0]
    out_width = cross_out.shape[1]
    bf16 = jnp.bfloat16

    cross_weights = []
    for weight in (cross_query, cross_key, cross_value):
        received = core_swapped(columns(weight, other, half_width))
        block = jnp.concatenate([columns(weight, core, half_width), received], axis=0)
        cross_weights.append(
            jnp.concatenate(
                [block] + [exchanged(block, "seq", 2 * d) for d in range(1, chip_count)], axis=0
            )
        )
    states = jnp.concatenate([byte_states, core_swapped(byte_states)], axis=0)
    patches = jnp.concatenate([byte_patch, core_swapped(byte_patch)], axis=0)
    states = jnp.concatenate(
        [
            columns(states, 2 * (chip ^ d) + (core ^ e), key_rows)
            for d in range(chip_count)
            for e in range(2)
        ],
        axis=1,
    )

    cross_out = jnp.concatenate(
        [rows(cross_out, core, half_width), rows(cross_out, other, half_width)], axis=0
    )
    latent_out = jnp.concatenate(
        [
            rows(latent_out, half_heads * e + (chip ^ d), HEAD_DIM)
            for e in (core, other)
            for d in range(chip_count)
        ],
        axis=0,
    )
    paired = []
    for weight in (latent_query, latent_key, latent_value):
        received = core_swapped(columns(weight, other, half_width))
        paired.append(jnp.concatenate([columns(weight, core, half_width), received], axis=0))
    head_weights = [
        jnp.concatenate([columns(weight, chip ^ d, HEAD_DIM) for weight in paired], axis=1)
        for d in range(chip_count)
    ]
    gain_own = lax.dynamic_slice_in_dim(norm_gain, seq * out_width, out_width)
    gain_other = lax.dynamic_slice_in_dim(norm_gain, (seq ^ 1) * out_width, out_width)

    slot_of = patches - (chip * chip_patches - spill)
    onehot = (slot_of[:, None] == jnp.arange(slot_count, dtype=jnp.int32)[None, :]).astype(bf16)
    edge = jnp.ones((spill,), jnp.int32)
    lengths = lax.dynamic_slice_in_dim(
        jnp.concatenate([edge, patch_len, edge]), chip * chip_patches, slot_count
    )
    byte_sums = lax.dot_general(
        onehot, states, (((0,), (0,)), ((), ())), preferred_element_type=jnp.float32
    )
    pooled = (byte_sums / lengths.astype(jnp.float32)[:, None]).astype(bf16)
    query_slots = dot(pooled, cross_weights[0]).astype(bf16)
    byte_keys = dot(states, cross_weights[1]).astype(bf16)
    byte_values = dot(states, cross_weights[2]).astype(bf16)
    byte_count = states.shape[0]
    query_bytes = dot(onehot, query_slots)
    scores = (query_bytes * byte_keys.astype(jnp.float32)).reshape(
        byte_count, half_heads, HEAD_DIM
    ).sum(axis=2) / math.sqrt(HEAD_DIM)
    byte_raw = capped_exp(scores)
    totals = contract_rows(onehot.astype(jnp.float32), byte_raw)
    totals = jnp.where(totals > 0.0, totals, 1.0)
    weighted = (
        byte_raw[:, :, None]
        * byte_values.astype(jnp.float32).reshape(byte_count, half_heads, HEAD_DIM)
    ).reshape(byte_count, half_width)
    summed = lax.dot_general(
        onehot, weighted.astype(bf16), (((0,), (0,)), ((), ())), preferred_element_type=jnp.float32
    )
    heads = (
        summed.reshape(slot_count, half_heads, HEAD_DIM) / totals[:, :, None]
    ).reshape(slot_count, half_width).astype(bf16)

    own_heads = heads[spill : spill + chip_patches]
    from_above = shifted(heads[:spill], "seq", -2)
    from_below = shifted(heads[spill + chip_patches :], "seq", 2)
    own_heads = own_heads + jnp.concatenate(
        [from_below, jnp.zeros((chip_patches - 2 * spill, half_width), bf16), from_above], axis=0
    )

    partial = []
    for d in range(chip_count):
        block = exchanged(own_heads, "seq", 2 * d) if d else own_heads
        block = jnp.concatenate([block, core_swapped(block)], axis=1)
        partial.append(dot(block, cross_out))
    partial = jnp.stack(partial)

    def quarter(stack, index):
        return lax.dynamic_index_in_dim(stack, index, 0, keepdims=False)

    total = quarter(partial, chip ^ tensor)
    partial = partial.astype(bf16)
    for r in range(1, tensor_count):
        total = total + exchanged(quarter(partial, chip ^ tensor ^ r), "tensor", r).astype(
            jnp.float32
        )
    latent_in = total.astype(bf16)

    projected = []
    squares = []
    for r in range(tensor_count):
        block = exchanged(latent_in, "tensor", r) if r else latent_in
        pair = jnp.concatenate([block, core_swapped(block)], axis=1).astype(jnp.float32)
        squares.append(jnp.sum(pair * pair, axis=1))
        scaled = (pair * jnp.concatenate([gain_own, gain_other])[None, :]).astype(bf16)
        share = dot(scaled, head_weights[0])
        for d in range(1, chip_count):
            share = share + exchanged(
                dot(scaled, head_weights[d]).astype(bf16), "seq", 2 * d
            ).astype(jnp.float32)
        projected.append(share)
    squares = jnp.stack(squares)
    mean_square = squares
    for d in range(1, chip_count):
        mean_square = mean_square + exchanged(squares, "seq", 2 * d)
    mean_square = mean_square / (out_width * seq_count)
    projected = jnp.stack(projected) * lax.rsqrt(mean_square + norm_eps)[:, :, None]
    projected = jnp.concatenate(
        [quarter(projected, tensor ^ a) for a in range(tensor_count)], axis=0
    ).astype(bf16)
    query, key, value = jnp.split(projected, 3, axis=1)

    attn_scores = lax.dot_general(
        query, key, (((1,), (1,)), ((), ())), preferred_element_type=jnp.float32
    ) / math.sqrt(HEAD_DIM)
    positions = jnp.arange(patch_count, dtype=jnp.int32)
    raw = jnp.where(positions[None, :] <= positions[:, None], capped_exp(attn_scores), 0.0)
    attended = (dot(raw.astype(bf16), value) / jnp.sum(raw, axis=1, keepdims=True)).astype(bf16)

    arrived = [attended] + [exchanged(attended, "seq", 2 * d) for d in range(1, chip_count)]
    arrived = jnp.concatenate(arrived, axis=1)
    arrived = jnp.concatenate([arrived, core_swapped(arrived)], axis=1)
    mixed = dot(arrived, latent_out).reshape(tensor_count, -1, out_width)
    result = latent_in.astype(jnp.float32) + quarter(mixed, tensor)
    mixed = mixed.astype(bf16)
    for r in range(1, tensor_count):
        result = result + exchanged(quarter(mixed, tensor ^ r), "tensor", r).astype(jnp.float32)
    result = result.astype(bf16)

    pieces = []
    for flip in range(2):
        route = [
            (s * tensor_count + t, (2 * t + ((s % 2) ^ flip)) * tensor_count + s // 2)
            for s in range(seq_count)
            for t in range(tensor_count)
        ]
        pieces.append(lax.ppermute(rows(result, core ^ flip, patch_dev), ("seq", "tensor"), route))
    same, crossed = pieces
    return jnp.concatenate(
        [jnp.where(core == 0, same, crossed), jnp.where(core == 0, crossed, same)], axis=1
    )


def head_per_device(mesh, heads):
    seq_count, tensor_count = mesh.shape["seq"], mesh.shape["tensor"]
    return (
        heads == seq_count * tensor_count
        and seq_count == 2 * tensor_count
        and tensor_count & (tensor_count - 1) == 0
    )


def solution(mesh):
    specs = (
        P("seq", None),
        P("seq"),
        P(),
        P("seq", "tensor"),
        P("seq", "tensor"),
        P("seq", "tensor"),
        P("tensor", "seq"),
        P(),
        P("seq", "tensor"),
        P("seq", "tensor"),
        P("seq", "tensor"),
        P("tensor", "seq"),
    )

    def whole(*arrays):
        chosen = (
            per_device
            if head_per_device(mesh, arrays[3].shape[1] // HEAD_DIM)
            else per_device_gathered
        )
        return jax.shard_map(
            chosen, mesh=mesh, in_specs=specs, out_specs=P("seq", "tensor"), check_vma=False
        )(*arrays)

    return whole
```

```python
import functools
import math

import jax
import jax.numpy as jnp
from jax import lax
from jax.experimental import pallas as pl
from jax.experimental.pallas import tpu as pltpu
from jax.sharding import PartitionSpec as P

HEAD_DIM = 128
PATCH_DEV = 128


score_cap = 30.0
norm_eps = 1e-05


def shifted(block, axis, distance):
    devices = range(lax.axis_size(axis))
    route = [(i - distance, i) for i in devices if i - distance in devices]
    return lax.ppermute(block, axis, route)


def capped_exp(scores):
    return jnp.exp(score_cap * jnp.tanh(scores / score_cap))


def contract_rows(left, right):
    return lax.dot_general(
        left,
        right,
        (((0,), (0,)), ((), ())),
        precision=lax.Precision.HIGHEST,
        preferred_element_type=jnp.float32,
    )


def per_device_gathered(
    byte_states,
    byte_patch,
    patch_len,
    cross_query,
    cross_key,
    cross_value,
    cross_out,
    norm_gain,
    latent_query,
    latent_key,
    latent_value,
    latent_out,
):
    seq_index = lax.axis_index("seq")
    tensor_count = lax.axis_size("tensor")
    (
        cross_query,
        cross_key,
        cross_value,
        latent_query,
        latent_key,
        latent_value,
        cross_out,
        latent_out,
    ) = (
        lax.all_gather(cross_query, "seq", axis=0, tiled=True),
        lax.all_gather(cross_key, "seq", axis=0, tiled=True),
        lax.all_gather(cross_value, "seq", axis=0, tiled=True),
        lax.all_gather(latent_query, "seq", axis=0, tiled=True),
        lax.all_gather(latent_key, "seq", axis=0, tiled=True),
        lax.all_gather(latent_value, "seq", axis=0, tiled=True),
        lax.all_gather(cross_out, "seq", axis=1, tiled=True),
        lax.all_gather(latent_out, "seq", axis=1, tiled=True),
    )
    latent_width = cross_out.shape[1]
    local_width = cross_out.shape[0]
    head_count = local_width // HEAD_DIM
    slot_count = 2 * PATCH_DEV
    byte_count = byte_states.shape[0]
    first_patch = byte_patch[0]
    slot_of = byte_patch - first_patch
    onehot_mask = slot_of[:, None] == jnp.arange(slot_count, dtype=jnp.int32)[None, :]
    onehot = onehot_mask.astype(jnp.bfloat16)
    onehot_float = onehot_mask.astype(jnp.float32)
    byte_sums = lax.dot_general(
        onehot, byte_states, (((0,), (0,)), ((), ())), preferred_element_type=jnp.float32
    )
    lengths_all = jnp.concatenate([patch_len, jnp.ones((slot_count,), jnp.int32)])
    lengths = lax.dynamic_slice_in_dim(lengths_all, first_patch, slot_count)
    pooled = (byte_sums / lengths.astype(jnp.float32)[:, None]).astype(jnp.bfloat16)
    query_slots = jnp.dot(pooled, cross_query, preferred_element_type=jnp.float32).astype(
        jnp.bfloat16
    )
    byte_keys = jnp.dot(byte_states, cross_key, preferred_element_type=jnp.float32).astype(
        jnp.bfloat16
    )
    byte_values = jnp.dot(byte_states, cross_value, preferred_element_type=jnp.float32).astype(
        jnp.bfloat16
    )
    query_bytes = jnp.dot(onehot, query_slots, preferred_element_type=jnp.float32)
    scores = (query_bytes * byte_keys.astype(jnp.float32)).reshape(
        byte_count, head_count, HEAD_DIM
    ).sum(axis=2) / math.sqrt(HEAD_DIM)
    byte_raw = capped_exp(scores)
    totals = contract_rows(onehot_float, byte_raw)
    totals = jnp.where(totals > 0.0, totals, 1.0)
    totals_bytes = jnp.dot(
        onehot_float, totals, precision=lax.Precision.HIGHEST, preferred_element_type=jnp.float32
    )
    byte_weight = (byte_raw / totals_bytes).astype(jnp.bfloat16)
    weighted = (
        byte_weight.astype(jnp.float32)[:, :, None]
        * byte_values.astype(jnp.float32).reshape(byte_count, head_count, HEAD_DIM)
    ).reshape(byte_count, local_width)
    cross_heads = contract_rows(onehot_float, weighted).astype(jnp.bfloat16)
    padding = jnp.zeros((2 * PATCH_DEV, cross_heads.shape[1]), cross_heads.dtype)
    padded = jnp.concatenate([padding, cross_heads, padding], axis=0)
    offset = seq_index * PATCH_DEV - first_patch + 2 * PATCH_DEV
    padded, offset = (padded, offset)
    owned_heads = lax.dynamic_slice_in_dim(padded, offset, PATCH_DEV, 0)
    for offset_step in (-1, 1):
        window = lax.dynamic_slice_in_dim(padded, offset + offset_step * PATCH_DEV, PATCH_DEV, 0)
        owned_heads = owned_heads + shifted(window, "seq", offset_step)
    partial_value = jnp.dot(owned_heads, cross_out, preferred_element_type=jnp.float32)
    latent_in = lax.psum(partial_value, "tensor").astype(jnp.bfloat16)
    hidden = latent_in.astype(jnp.float32)
    mean_square = jnp.mean(hidden * hidden, axis=1, keepdims=True)
    normed = (hidden * lax.rsqrt(mean_square + norm_eps) * norm_gain[None, :]).astype(jnp.bfloat16)
    query = (
        jnp.dot(normed, latent_query, preferred_element_type=jnp.float32)
        .astype(jnp.bfloat16)
        .reshape(PATCH_DEV, head_count, HEAD_DIM)
    )
    key_rows = jnp.dot(normed, latent_key, preferred_element_type=jnp.float32).astype(jnp.bfloat16)
    value_rows = jnp.dot(normed, latent_value, preferred_element_type=jnp.float32).astype(
        jnp.bfloat16
    )
    positions = seq_index * PATCH_DEV + jnp.arange(PATCH_DEV, dtype=jnp.int32)
    key_piece = lax.all_gather(key_rows, "seq", axis=0, tiled=True)
    value_piece = lax.all_gather(value_rows, "seq", axis=0, tiled=True)
    piece_rows = key_piece.shape[0]
    key_piece = key_piece.reshape(piece_rows, head_count, HEAD_DIM)
    value_piece = value_piece.reshape(piece_rows, head_count, HEAD_DIM)
    piece_scores = jnp.einsum(
        "qhd,khd->hqk", query, key_piece, preferred_element_type=jnp.float32
    ) / math.sqrt(HEAD_DIM)
    key_positions = jnp.arange(piece_rows, dtype=jnp.int32)
    allowed = key_positions[None, :] <= positions[:, None]
    exp_scores = jnp.where(allowed[None, :, :], capped_exp(piece_scores), 0.0)
    denominator = jnp.sum(exp_scores, axis=2)
    numerator = jnp.einsum(
        "hqk,khd->hqd",
        exp_scores.astype(jnp.bfloat16),
        value_piece,
        preferred_element_type=jnp.float32,
    )
    numerator, denominator = (numerator, denominator)
    attended = (numerator / denominator[:, :, None]).astype(jnp.bfloat16)
    attended = attended.transpose(1, 0, 2).reshape(PATCH_DEV, local_width)
    projected = jnp.dot(attended, latent_out, preferred_element_type=jnp.float32)
    mixed_sum = lax.psum_scatter(projected, "tensor", scatter_dimension=1, tiled=True)
    column_width = latent_width // tensor_count
    residual = lax.dynamic_slice_in_dim(
        hidden, lax.axis_index("tensor") * column_width, column_width, 1
    )
    return (residual + mixed_sum).astype(jnp.bfloat16)


def dot(left, right):
    return jnp.dot(left, right, preferred_element_type=jnp.float32)


def exchanged(block, axis, distance):
    route = [(i, i ^ distance) for i in range(lax.axis_size(axis))]
    return lax.ppermute(block, axis, route)


def core_swapped(block):
    return exchanged(block, "seq", 1)


def after(value, *earlier):
    return lax.optimization_barrier((value, *earlier))[0]


def place():
    seq = lax.axis_index("seq")
    return seq // 2, lax.rem(seq, 2), lax.axis_index("tensor")


def aligned(index, size):
    return pl.ds(pl.multiple_of(index * size, size), size)


def call(kernel, outs, *operands, scratch=(), flops=0):
    shapes = [jax.ShapeDtypeStruct(shape, dtype) for shape, dtype in outs]
    moved = sum(o.size * o.dtype.itemsize for o in [*operands, *shapes])
    return pl.pallas_call(
        kernel,
        out_shape=shapes,
        in_specs=[pl.BlockSpec(memory_space=pltpu.VMEM)] * len(operands),
        out_specs=[pl.BlockSpec(memory_space=pltpu.VMEM)] * len(outs),
        scratch_shapes=list(scratch),
        compiler_params=pltpu.CompilerParams(vmem_limit_bytes=28 * 1024 * 1024),
        cost_estimate=pl.CostEstimate(flops=flops, bytes_accessed=moved, transcendentals=0),
    )(*operands)


def assemble(pieces, whole):
    chip, core, _ = place()
    for n, piece in enumerate(pieces):
        index = 2 * (chip ^ (n // 2)) + (core ^ (n % 2))
        whole[aligned(index, piece.shape[0]), :] = piece[...]


def query_kernel(count, states, slot_row, lengths, *refs):
    pieces, query, whole = refs[:count], refs[count], refs[count + 1]
    slots, byte_count = query.shape[0], states.shape[0]
    assemble(pieces, whole)
    index = lax.broadcasted_iota(jnp.int32, (slots, byte_count), 0)
    onehot = (index == slot_row[...]).astype(jnp.bfloat16)
    pooled = (dot(onehot, states[...]) / lengths[...]).astype(jnp.bfloat16)
    query[...] = dot(pooled, whole[...]).astype(jnp.bfloat16)


def score_kernel(count, tile, states, slot_row, slot_column, query, *refs):
    pieces, (raw, totals, whole) = refs[:count], refs[count:]
    slots, width = query.shape
    head_count = width // HEAD_DIM
    assemble(pieces, whole)
    totals[...] = jnp.zeros_like(totals)

    @pl.loop(0, states.shape[0] // tile)
    def _(step):
        span = aligned(step, tile)
        keys = dot(states[span, :], whole[...]).astype(jnp.bfloat16).astype(jnp.float32)
        slot = lax.broadcasted_iota(jnp.int32, (tile, slots), 1)
        onehot = (slot == slot_column[span, :]).astype(jnp.bfloat16)
        product = dot(onehot, query[...]) * keys
        lane = lax.broadcasted_iota(jnp.int32, (tile, HEAD_DIM), 1)
        scores = jnp.zeros((tile, HEAD_DIM), jnp.float32)
        for head in range(head_count):
            summed = jnp.sum(
                product[:, head * HEAD_DIM : (head + 1) * HEAD_DIM], axis=1, keepdims=True
            )
            scores = jnp.where(lane == head, summed, scores)
        values = capped_exp(scores / math.sqrt(HEAD_DIM))
        raw[span, :] = values
        high = values.astype(jnp.bfloat16)
        low = (values - high.astype(jnp.float32)).astype(jnp.bfloat16)
        index = lax.broadcasted_iota(jnp.int32, (slots, tile), 0)
        turned = (index == slot_row[:, span]).astype(jnp.bfloat16)
        totals[...] += dot(turned, high) + dot(turned, low)


def value_kernel(tile, states, slot_row, weight, raw, totals, own, above, below, summed):
    slots = totals.shape[0]
    spill = above.shape[0]
    head_count = weight.shape[1] // HEAD_DIM
    summed[...] = jnp.zeros_like(summed)

    @pl.loop(0, states.shape[0] // tile)
    def _(step):
        span = aligned(step, tile)
        values = dot(states[span, :], weight[...]).astype(jnp.bfloat16).astype(jnp.float32)
        factors = raw[span, :]
        weighted = jnp.concatenate(
            [
                (values[:, h * HEAD_DIM : (h + 1) * HEAD_DIM] * factors[:, h : h + 1]).astype(
                    jnp.bfloat16
                )
                for h in range(head_count)
            ],
            axis=1,
        )
        index = lax.broadcasted_iota(jnp.int32, (slots, tile), 0)
        turned = (index == slot_row[:, span]).astype(jnp.bfloat16)
        summed[...] += dot(turned, weighted)

    total = totals[...]
    inverse = 1.0 / jnp.where(total > 0.0, total, 1.0)
    for h in range(head_count):
        part = slice(h * HEAD_DIM, (h + 1) * HEAD_DIM)
        heads = (summed[:, part] * inverse[:, h : h + 1]).astype(jnp.bfloat16)
        above[:, part] = heads[:spill]
        own[:, part] = heads[spill : slots - spill]
        below[:, part] = heads[slots - spill :]


def quarters(left, weight, outs):
    _, _, tensor = place()
    height = outs[0].shape[0]
    for r, out in enumerate(outs):
        block = left[aligned(tensor ^ r, height), :]
        out[...] = dot(block, weight[...]).astype(out.dtype)


def cross_out_kernel(count, weight, *refs):
    pieces, outs, whole = refs[:count], refs[count:-1], refs[-1]
    assemble(pieces, whole)
    quarters(whole, weight, outs)


def latent_out_kernel(count, weight, *refs):
    pieces, outs, whole = refs[:count], refs[count:-1], refs[-1]
    chip, core, _ = place()
    for n, piece in enumerate(pieces):
        index = (count // 2) * (core ^ (n % 2)) + (chip ^ (n // 2))
        whole[:, aligned(index, HEAD_DIM)] = piece[...]
    quarters(whole, weight, outs)


def project_kernel(rows_own, rows_other, gain, *refs):
    weights, (stats, *outs), (left, right) = refs[:6], refs[6:-2], refs[-2:]
    chip, core, _ = place()
    seq = lax.axis_index("seq")
    width = rows_own.shape[1]
    total = jnp.zeros((8, rows_own.shape[0]), jnp.float32)
    for n, block in enumerate((rows_own, rows_other)):
        hidden = block[...].astype(jnp.float32)
        total += lax.dot_general(
            jnp.ones((8, width), jnp.float32),
            hidden * hidden,
            (((1,), (1,)), ((), ())),
            precision=lax.Precision.HIGHEST,
            preferred_element_type=jnp.float32,
        )
        left[:, n * width : (n + 1) * width] = (
            hidden * gain[:, aligned(seq ^ n, width)]
        ).astype(jnp.bfloat16)
    stats[...] = total
    for d, out in enumerate(outs):
        head = len(outs) * core + (chip ^ d)
        for m in range(3):
            for n in range(2):
                right[n * width : (n + 1) * width, m * HEAD_DIM : (m + 1) * HEAD_DIM] = weights[
                    2 * m + n
                ][:, aligned(head, HEAD_DIM)]
        out[...] = dot(left[...], right[...]).astype(out.dtype)


def attention_kernel(parts, chips, depth, stats, *refs):
    shares, attended, (query, key, value) = refs[: parts * chips], refs[-4], refs[-3:]
    _, _, tensor = place()
    height = shares[0].shape[0]
    diagonal = lax.broadcasted_iota(jnp.int32, (height, height), 0) == lax.broadcasted_iota(
        jnp.int32, (height, height), 1
    )
    for r in range(parts):
        total = shares[r * chips][...]
        for d in range(1, chips):
            total += shares[r * chips + d][...].astype(jnp.float32)
        row = stats[r * 8 : r * 8 + 1, :]
        column = jnp.sum(jnp.where(diagonal, row, 0.0), axis=1, keepdims=True)
        total = (total * lax.rsqrt(column / depth + norm_eps)).astype(jnp.bfloat16)
        span = aligned(tensor ^ r, height)
        for m, kept in enumerate((query, key, value)):
            kept[span, :] = total[:, m * HEAD_DIM : (m + 1) * HEAD_DIM]
    causal = lax.broadcasted_iota(jnp.int32, (height, height), 0) >= lax.broadcasted_iota(
        jnp.int32, (height, height), 1
    )
    for i in range(parts):
        block = query[i * height : (i + 1) * height, :]
        numerator = jnp.zeros((height, HEAD_DIM), jnp.float32)
        denominator = jnp.zeros((height, 1), jnp.float32)
        for j in range(i + 1):
            span = slice(j * height, (j + 1) * height)
            scores = lax.dot_general(
                block, key[span, :], (((1,), (1,)), ((), ())), preferred_element_type=jnp.float32
            )
            raw = capped_exp(scores / math.sqrt(HEAD_DIM))
            if i == j:
                raw = jnp.where(causal, raw, 0.0)
            denominator += jnp.sum(raw, axis=1, keepdims=True)
            numerator += dot(raw.astype(jnp.bfloat16), value[span, :])
        attended[i * height : (i + 1) * height, :] = (numerator / denominator).astype(jnp.bfloat16)


def final_kernel(own, hidden, *refs):
    received, outs, whole = refs[:-3], refs[-3:-1], refs[-1]
    _, core, _ = place()
    total = own[...] + hidden[...].astype(jnp.float32)
    for block in received:
        total += block[...].astype(jnp.float32)
    whole[...] = total
    height = outs[0].shape[0]
    for flip, out in enumerate(outs):
        out[...] = whole[aligned(core ^ flip, height), :].astype(jnp.bfloat16)


def per_device(
    byte_states,
    byte_patch,
    patch_len,
    cross_query,
    cross_key,
    cross_value,
    cross_out,
    norm_gain,
    latent_query,
    latent_key,
    latent_value,
    latent_out,
):
    seq = lax.axis_index("seq")
    core = lax.rem(seq, 2)
    seq_count = lax.axis_size("seq")
    tensor_count = lax.axis_size("tensor")
    chip_count = seq_count // 2
    patch_count = patch_len.shape[0]
    patch_dev = patch_count // seq_count
    spill = patch_dev // 2
    slot_count = patch_dev + 2 * spill
    byte_count, byte_width = byte_states.shape
    local_width = cross_query.shape[1]
    out_width = cross_out.shape[1]
    quarter = patch_count // tensor_count
    bf16, f32 = jnp.bfloat16, jnp.float32
    tile = min(256, byte_count)

    def over_plane(block):
        pieces = []
        for d in range(chip_count):
            moved = exchanged(block, "seq", 2 * d) if d else block
            pieces += [moved, core_swapped(moved)]
        return pieces

    value_weight = lax.all_gather(cross_value, "seq", axis=0, tiled=True)
    slot_of = byte_patch - (seq * patch_dev - spill)
    slot_row, slot_column = slot_of[None, :], slot_of[:, None]
    edge = jnp.ones((spill,), jnp.int32)
    lengths = lax.dynamic_slice_in_dim(
        jnp.concatenate([edge, patch_len, edge]), seq * patch_dev, slot_count
    ).astype(f32)[:, None]
    query_pieces = over_plane(cross_query)
    key_pieces = over_plane(cross_key)
    (query_slots,) = call(
        functools.partial(query_kernel, seq_count),
        [((slot_count, local_width), bf16)],
        byte_states,
        slot_row,
        lengths,
        *query_pieces,
        scratch=[pltpu.VMEM((byte_width, local_width), bf16)],
        flops=2 * slot_count * byte_width * (byte_count + local_width),
    )
    raw, totals = call(
        functools.partial(score_kernel, seq_count, tile),
        [((byte_count, HEAD_DIM), f32), ((slot_count, HEAD_DIM), f32)],
        byte_states,
        slot_row,
        slot_column,
        query_slots,
        *key_pieces,
        scratch=[pltpu.VMEM((byte_width, local_width), bf16)],
        flops=2 * byte_count * local_width * (byte_width + 2 * slot_count),
    )
    weights = []
    for weight in (latent_query, latent_key, latent_value):
        weights += [weight, core_swapped(after(weight, query_slots))]
    raw, *weights = lax.optimization_barrier((raw, *weights))
    own, above, below = call(
        functools.partial(value_kernel, tile),
        [((rows, local_width), bf16) for rows in (patch_dev, spill, spill)],
        byte_states,
        slot_row,
        value_weight,
        raw,
        totals,
        scratch=[pltpu.VMEM((slot_count, local_width), f32)],
        flops=2 * byte_count * local_width * (byte_width + slot_count),
    )

    own = own + jnp.concatenate([shifted(below, "seq", 1), shifted(above, "seq", -1)], axis=0)

    total, *sent = call(
        functools.partial(cross_out_kernel, seq_count),
        [((quarter, out_width), f32 if r == 0 else bf16) for r in range(tensor_count)],
        cross_out,
        *over_plane(own),
        scratch=[pltpu.VMEM((patch_count, local_width), bf16)],
        flops=2 * patch_count * local_width * out_width,
    )
    for r, block in enumerate(sent, 1):
        total = total + exchanged(block, "tensor", r).astype(f32)
    latent_in = total.astype(bf16)

    gain = norm_gain[None, :]
    blocks = [latent_in]
    for r in range(1, tensor_count):
        blocks.append(exchanged(after(latent_in, *blocks[r - 2 : r - 1]), "tensor", r))
    shares, squares = [], []
    for block in blocks:
        square, share, *sent = call(
            project_kernel,
            [((8, quarter), f32)]
            + [((quarter, 3 * HEAD_DIM), f32 if d == 0 else bf16) for d in range(chip_count)],
            block,
            core_swapped(block),
            gain,
            *weights,
            scratch=[
                pltpu.VMEM((quarter, 2 * out_width), bf16),
                pltpu.VMEM((2 * out_width, 3 * HEAD_DIM), bf16),
            ],
            flops=2 * quarter * 2 * out_width * 3 * HEAD_DIM * chip_count,
        )
        squares.append(square)
        shares += [share] + [exchanged(part, "seq", 2 * d) for d, part in enumerate(sent, 1)]
    squares = jnp.concatenate(squares, axis=0)
    square_sum = squares
    for d in range(1, chip_count):
        square_sum = square_sum + exchanged(squares, "seq", 2 * d)
    (attended,) = call(
        functools.partial(attention_kernel, tensor_count, chip_count, out_width * seq_count),
        [((patch_count, HEAD_DIM), bf16)],
        square_sum,
        *shares,
        scratch=[pltpu.VMEM((patch_count, HEAD_DIM), bf16)] * 3,
        flops=2 * patch_count * patch_count * HEAD_DIM,
    )

    total, *sent = call(
        functools.partial(latent_out_kernel, seq_count),
        [((quarter, out_width), f32 if r == 0 else bf16) for r in range(tensor_count)],
        latent_out,
        *over_plane(attended),
        scratch=[pltpu.VMEM((patch_count, local_width), bf16)],
        flops=2 * patch_count * local_width * out_width,
    )
    pieces = call(
        final_kernel,
        [((patch_dev, out_width), bf16)] * 2,
        total,
        latent_in,
        *[exchanged(block, "tensor", r) for r, block in enumerate(sent, 1)],
        scratch=[pltpu.VMEM((quarter, out_width), f32)],
    )

    moved = []
    for flip in range(2):
        route = [
            (s * tensor_count + t, (2 * t + ((s % 2) ^ flip)) * tensor_count + s // 2)
            for s in range(seq_count)
            for t in range(tensor_count)
        ]
        moved.append(lax.ppermute(pieces[flip], ("seq", "tensor"), route))
    same, crossed = moved
    return jnp.concatenate(
        [jnp.where(core == 0, same, crossed), jnp.where(core == 0, crossed, same)], axis=1
    )


def head_per_device(mesh, heads):
    seq_count, tensor_count = mesh.shape["seq"], mesh.shape["tensor"]
    return (
        heads == seq_count * tensor_count
        and seq_count == 2 * tensor_count
        and tensor_count & (tensor_count - 1) == 0
    )


def solution(mesh):
    specs = (
        P("seq", None),
        P("seq"),
        P(),
        P("seq", "tensor"),
        P("seq", "tensor"),
        P("seq", "tensor"),
        P("tensor", "seq"),
        P(),
        P("seq", "tensor"),
        P("seq", "tensor"),
        P("seq", "tensor"),
        P("tensor", "seq"),
    )

    def whole(*arrays):
        chosen = (
            per_device
            if head_per_device(mesh, arrays[3].shape[1] // HEAD_DIM)
            else per_device_gathered
        )
        return jax.shard_map(
            chosen, mesh=mesh, in_specs=specs, out_specs=P("seq", "tensor"), check_vma=False
        )(*arrays)

    return whole
```

```python
import functools
import math

import jax
import jax.numpy as jnp
from jax import lax
from jax.experimental import pallas as pl
from jax.experimental.pallas import tpu as pltpu
from jax.sharding import PartitionSpec as P

HEAD_DIM = 128
PATCH_DEV = 128


score_cap = 30.0
norm_eps = 1e-05


def shifted(block, axis, distance):
    devices = range(lax.axis_size(axis))
    route = [(i - distance, i) for i in devices if i - distance in devices]
    return lax.ppermute(block, axis, route)


def capped_exp(scores):
    return jnp.exp(score_cap * jnp.tanh(scores / score_cap))


def contract_rows(left, right):
    return lax.dot_general(
        left,
        right,
        (((0,), (0,)), ((), ())),
        precision=lax.Precision.HIGHEST,
        preferred_element_type=jnp.float32,
    )


def per_device_gathered(
    byte_states,
    byte_patch,
    patch_len,
    cross_query,
    cross_key,
    cross_value,
    cross_out,
    norm_gain,
    latent_query,
    latent_key,
    latent_value,
    latent_out,
):
    seq_index = lax.axis_index("seq")
    tensor_count = lax.axis_size("tensor")
    (
        cross_query,
        cross_key,
        cross_value,
        latent_query,
        latent_key,
        latent_value,
        cross_out,
        latent_out,
    ) = (
        lax.all_gather(cross_query, "seq", axis=0, tiled=True),
        lax.all_gather(cross_key, "seq", axis=0, tiled=True),
        lax.all_gather(cross_value, "seq", axis=0, tiled=True),
        lax.all_gather(latent_query, "seq", axis=0, tiled=True),
        lax.all_gather(latent_key, "seq", axis=0, tiled=True),
        lax.all_gather(latent_value, "seq", axis=0, tiled=True),
        lax.all_gather(cross_out, "seq", axis=1, tiled=True),
        lax.all_gather(latent_out, "seq", axis=1, tiled=True),
    )
    latent_width = cross_out.shape[1]
    local_width = cross_out.shape[0]
    head_count = local_width // HEAD_DIM
    slot_count = 2 * PATCH_DEV
    byte_count = byte_states.shape[0]
    first_patch = byte_patch[0]
    slot_of = byte_patch - first_patch
    onehot_mask = slot_of[:, None] == jnp.arange(slot_count, dtype=jnp.int32)[None, :]
    onehot = onehot_mask.astype(jnp.bfloat16)
    onehot_float = onehot_mask.astype(jnp.float32)
    byte_sums = lax.dot_general(
        onehot, byte_states, (((0,), (0,)), ((), ())), preferred_element_type=jnp.float32
    )
    lengths_all = jnp.concatenate([patch_len, jnp.ones((slot_count,), jnp.int32)])
    lengths = lax.dynamic_slice_in_dim(lengths_all, first_patch, slot_count)
    pooled = (byte_sums / lengths.astype(jnp.float32)[:, None]).astype(jnp.bfloat16)
    query_slots = jnp.dot(pooled, cross_query, preferred_element_type=jnp.float32).astype(
        jnp.bfloat16
    )
    byte_keys = jnp.dot(byte_states, cross_key, preferred_element_type=jnp.float32).astype(
        jnp.bfloat16
    )
    byte_values = jnp.dot(byte_states, cross_value, preferred_element_type=jnp.float32).astype(
        jnp.bfloat16
    )
    query_bytes = jnp.dot(onehot, query_slots, preferred_element_type=jnp.float32)
    scores = (query_bytes * byte_keys.astype(jnp.float32)).reshape(
        byte_count, head_count, HEAD_DIM
    ).sum(axis=2) / math.sqrt(HEAD_DIM)
    byte_raw = capped_exp(scores)
    totals = contract_rows(onehot_float, byte_raw)
    totals = jnp.where(totals > 0.0, totals, 1.0)
    totals_bytes = jnp.dot(
        onehot_float, totals, precision=lax.Precision.HIGHEST, preferred_element_type=jnp.float32
    )
    byte_weight = (byte_raw / totals_bytes).astype(jnp.bfloat16)
    weighted = (
        byte_weight.astype(jnp.float32)[:, :, None]
        * byte_values.astype(jnp.float32).reshape(byte_count, head_count, HEAD_DIM)
    ).reshape(byte_count, local_width)
    cross_heads = contract_rows(onehot_float, weighted).astype(jnp.bfloat16)
    padding = jnp.zeros((2 * PATCH_DEV, cross_heads.shape[1]), cross_heads.dtype)
    padded = jnp.concatenate([padding, cross_heads, padding], axis=0)
    offset = seq_index * PATCH_DEV - first_patch + 2 * PATCH_DEV
    padded, offset = (padded, offset)
    owned_heads = lax.dynamic_slice_in_dim(padded, offset, PATCH_DEV, 0)
    for offset_step in (-1, 1):
        window = lax.dynamic_slice_in_dim(padded, offset + offset_step * PATCH_DEV, PATCH_DEV, 0)
        owned_heads = owned_heads + shifted(window, "seq", offset_step)
    partial_value = jnp.dot(owned_heads, cross_out, preferred_element_type=jnp.float32)
    latent_in = lax.psum(partial_value, "tensor").astype(jnp.bfloat16)
    hidden = latent_in.astype(jnp.float32)
    mean_square = jnp.mean(hidden * hidden, axis=1, keepdims=True)
    normed = (hidden * lax.rsqrt(mean_square + norm_eps) * norm_gain[None, :]).astype(jnp.bfloat16)
    query = (
        jnp.dot(normed, latent_query, preferred_element_type=jnp.float32)
        .astype(jnp.bfloat16)
        .reshape(PATCH_DEV, head_count, HEAD_DIM)
    )
    key_rows = jnp.dot(normed, latent_key, preferred_element_type=jnp.float32).astype(jnp.bfloat16)
    value_rows = jnp.dot(normed, latent_value, preferred_element_type=jnp.float32).astype(
        jnp.bfloat16
    )
    positions = seq_index * PATCH_DEV + jnp.arange(PATCH_DEV, dtype=jnp.int32)
    key_piece = lax.all_gather(key_rows, "seq", axis=0, tiled=True)
    value_piece = lax.all_gather(value_rows, "seq", axis=0, tiled=True)
    piece_rows = key_piece.shape[0]
    key_piece = key_piece.reshape(piece_rows, head_count, HEAD_DIM)
    value_piece = value_piece.reshape(piece_rows, head_count, HEAD_DIM)
    piece_scores = jnp.einsum(
        "qhd,khd->hqk", query, key_piece, preferred_element_type=jnp.float32
    ) / math.sqrt(HEAD_DIM)
    key_positions = jnp.arange(piece_rows, dtype=jnp.int32)
    allowed = key_positions[None, :] <= positions[:, None]
    exp_scores = jnp.where(allowed[None, :, :], capped_exp(piece_scores), 0.0)
    denominator = jnp.sum(exp_scores, axis=2)
    numerator = jnp.einsum(
        "hqk,khd->hqd",
        exp_scores.astype(jnp.bfloat16),
        value_piece,
        preferred_element_type=jnp.float32,
    )
    numerator, denominator = (numerator, denominator)
    attended = (numerator / denominator[:, :, None]).astype(jnp.bfloat16)
    attended = attended.transpose(1, 0, 2).reshape(PATCH_DEV, local_width)
    projected = jnp.dot(attended, latent_out, preferred_element_type=jnp.float32)
    mixed_sum = lax.psum_scatter(projected, "tensor", scatter_dimension=1, tiled=True)
    column_width = latent_width // tensor_count
    residual = lax.dynamic_slice_in_dim(
        hidden, lax.axis_index("tensor") * column_width, column_width, 1
    )
    return (residual + mixed_sum).astype(jnp.bfloat16)


def dot(left, right):
    return jnp.dot(left, right, preferred_element_type=jnp.float32)


def exchanged(block, axis, distance):
    route = [(i, i ^ distance) for i in range(lax.axis_size(axis))]
    return lax.ppermute(block, axis, route)


def core_swapped(block):
    return exchanged(block, "seq", 1)


def after(value, *earlier):
    return lax.optimization_barrier((value, *earlier))[0]


def place():
    seq = lax.axis_index("seq")
    return seq // 2, lax.rem(seq, 2), lax.axis_index("tensor")


def aligned(index, size):
    return pl.ds(pl.multiple_of(index * size, size), size)


def fetched(pairs, semaphores):
    copies = [
        pltpu.make_async_copy(source, target, semaphores.at[n])
        for n, (source, target) in enumerate(pairs)
    ]
    for copy in copies:
        copy.start()
    return copies


def call(kernel, outs, *operands, far=0, scratch=(), flops=0):
    shapes = [jax.ShapeDtypeStruct(shape, dtype) for shape, dtype in outs]
    moved = sum(o.size * o.dtype.itemsize for o in [*operands, *shapes])
    return pl.pallas_call(
        kernel,
        out_shape=shapes,
        in_specs=[pl.BlockSpec(memory_space=pltpu.VMEM)] * (len(operands) - far)
        + [pl.BlockSpec(memory_space=pl.ANY)] * far,
        out_specs=[pl.BlockSpec(memory_space=pltpu.VMEM)] * len(outs),
        scratch_shapes=list(scratch),
        compiler_params=pltpu.CompilerParams(vmem_limit_bytes=28 * 1024 * 1024),
        cost_estimate=pl.CostEstimate(flops=flops, bytes_accessed=moved, transcendentals=0),
    )(*operands)


def assemble(pieces, whole):
    chip, core, _ = place()
    for n, piece in enumerate(pieces):
        index = 2 * (chip ^ (n // 2)) + (core ^ (n % 2))
        whole[aligned(index, piece.shape[0]), :] = piece[...]


def plane_rows(pieces, whole):
    chip, core, _ = place()
    return [
        (piece, whole.at[aligned(2 * (chip ^ (n // 2)) + (core ^ (n % 2)), piece.shape[0]), :])
        for n, piece in enumerate(pieces)
    ]


def query_kernel(count, slot_row, lengths, states, *refs):
    pieces, (query, held, whole, semaphores) = refs[:count], refs[count:]
    slots, byte_count = query.shape[0], states.shape[0]
    copies = fetched([(states, held), *plane_rows(pieces, whole)], semaphores)
    index = lax.broadcasted_iota(jnp.int32, (slots, byte_count), 0)
    onehot = (index == slot_row[...]).astype(jnp.bfloat16)
    copies[0].wait()
    pooled = (dot(onehot, held[...]) / lengths[...]).astype(jnp.bfloat16)
    for copy in copies[1:]:
        copy.wait()
    query[...] = dot(pooled, whole[...]).astype(jnp.bfloat16)


def score_kernel(count, tile, slot_row, query, states, *refs):
    pieces, (raw, totals, held, whole, semaphores) = refs[:count], refs[count:]
    slots, width = query.shape
    head_count = width // HEAD_DIM
    copies = fetched([(states, held), *plane_rows(pieces, whole)], semaphores)
    totals[...] = jnp.zeros_like(totals)
    for copy in copies:
        copy.wait()

    @pl.loop(0, states.shape[0] // tile)
    def _(step):
        span = aligned(step, tile)
        keys = dot(held[span, :], whole[...]).astype(jnp.bfloat16).astype(jnp.float32)
        index = lax.broadcasted_iota(jnp.int32, (slots, tile), 0)
        turned = (index == slot_row[:, span]).astype(jnp.bfloat16)
        product = keys * lax.dot_general(
            turned, query[...], (((0,), (0,)), ((), ())), preferred_element_type=jnp.float32
        )
        lane = lax.broadcasted_iota(jnp.int32, (tile, HEAD_DIM), 1)
        scores = jnp.zeros((tile, HEAD_DIM), jnp.float32)
        for head in range(head_count):
            summed = jnp.sum(
                product[:, head * HEAD_DIM : (head + 1) * HEAD_DIM], axis=1, keepdims=True
            )
            scores = jnp.where(lane == head, summed, scores)
        values = capped_exp(scores / math.sqrt(HEAD_DIM))
        raw[span, :] = values
        high = values.astype(jnp.bfloat16)
        low = (values - high.astype(jnp.float32)).astype(jnp.bfloat16)
        totals[...] += dot(turned, high) + dot(turned, low)


def value_kernel(tile, slot_row, raw, totals, states, weight, *refs):
    own, above, below, held, whole, summed, semaphores = refs
    slots = totals.shape[0]
    copies = fetched([(states, held), (weight, whole)], semaphores)
    spill = above.shape[0]
    head_count = weight.shape[1] // HEAD_DIM
    summed[...] = jnp.zeros_like(summed)
    for copy in copies:
        copy.wait()

    @pl.loop(0, states.shape[0] // tile)
    def _(step):
        span = aligned(step, tile)
        values = dot(held[span, :], whole[...]).astype(jnp.bfloat16).astype(jnp.float32)
        factors = raw[span, :]
        weighted = jnp.concatenate(
            [
                (values[:, h * HEAD_DIM : (h + 1) * HEAD_DIM] * factors[:, h : h + 1]).astype(
                    jnp.bfloat16
                )
                for h in range(head_count)
            ],
            axis=1,
        )
        index = lax.broadcasted_iota(jnp.int32, (slots, tile), 0)
        turned = (index == slot_row[:, span]).astype(jnp.bfloat16)
        summed[...] += dot(turned, weighted)

    total = totals[...]
    inverse = 1.0 / jnp.where(total > 0.0, total, 1.0)
    for h in range(head_count):
        part = slice(h * HEAD_DIM, (h + 1) * HEAD_DIM)
        heads = (summed[:, part] * inverse[:, h : h + 1]).astype(jnp.bfloat16)
        above[:, part] = heads[:spill]
        own[:, part] = heads[spill : slots - spill]
        below[:, part] = heads[slots - spill :]


def quarters(left, weight, outs):
    _, _, tensor = place()
    height = outs[0].shape[0]
    for r, out in enumerate(outs):
        block = left[aligned(tensor ^ r, height), :]
        out[...] = dot(block, weight[...]).astype(out.dtype)


def cross_out_kernel(count, weight, *refs):
    pieces, outs, whole = refs[:count], refs[count:-1], refs[-1]
    assemble(pieces, whole)
    quarters(whole, weight, outs)


def latent_out_kernel(count, weight, *refs):
    pieces, outs, whole = refs[:count], refs[count:-1], refs[-1]
    chip, core, _ = place()
    for n, piece in enumerate(pieces):
        index = (count // 2) * (core ^ (n % 2)) + (chip ^ (n // 2))
        whole[:, aligned(index, HEAD_DIM)] = piece[...]
    quarters(whole, weight, outs)


def arrange_kernel(*refs):
    weights, outs, semaphores = refs[:6], refs[6:-1], refs[-1]
    chip, core, _ = place()
    height = weights[0].shape[0]
    copies = fetched(
        [
            (
                weights[2 * m + n].at[:, aligned(len(outs) * core + (chip ^ d), HEAD_DIM)],
                out.at[n * height : (n + 1) * height, m * HEAD_DIM : (m + 1) * HEAD_DIM],
            )
            for d, out in enumerate(outs)
            for m in range(3)
            for n in range(2)
        ],
        semaphores,
    )
    for copy in copies:
        copy.wait()


def diagonal(size):
    return lax.broadcasted_iota(jnp.int32, (size, size), 0) == lax.broadcasted_iota(
        jnp.int32, (size, size), 1
    )


def project_kernel(rows_own, rows_other, gain, *refs):
    chips = (len(refs) - 1) // 2
    weights, outs, left = refs[:chips], refs[chips:-1], refs[-1]
    seq = lax.axis_index("seq")
    height, width = rows_own.shape
    total = jnp.zeros((height, 1), jnp.float32)
    for n, block in enumerate((rows_own, rows_other)):
        hidden = block[...].astype(jnp.float32)
        total += jnp.sum(hidden * hidden, axis=1, keepdims=True)
        left[:, n * width : (n + 1) * width] = (
            hidden * gain[:, aligned(seq ^ n, width)]
        ).astype(jnp.bfloat16)
    for weight, out in reversed(list(zip(weights, outs))):
        out[:height, :] = dot(left[...], weight[...]).astype(out.dtype)
    row = jnp.sum(jnp.where(diagonal(height), total, 0.0), axis=0, keepdims=True)
    outs[0][height:, :height] = jnp.broadcast_to(row, (outs[0].shape[0] - height, height))
    high = row.astype(jnp.bfloat16).astype(jnp.float32)
    middle = (row - high).astype(jnp.bfloat16).astype(jnp.float32)
    low = row - high - middle
    index = lax.broadcasted_iota(jnp.int32, (outs[1].shape[0] - height, height), 0)
    terms = jnp.where(index == 0, high, jnp.where(index == 1, middle, low)).astype(jnp.bfloat16)
    for out in outs[1:]:
        out[height:, :height] = terms


def attention_kernel(parts, chips, depth, *refs):
    shares, attended, (query, key, value) = refs[: parts * chips], refs[-4], refs[-3:]
    _, _, tensor = place()
    height = attended.shape[0] // parts
    own_place = diagonal(height)
    for r in range(parts):
        total = shares[r * chips][:height, :]
        row = shares[r * chips][height : height + 1, :height]
        for d in range(1, chips):
            share = shares[r * chips + d]
            total += share[:height, :].astype(jnp.float32)
            terms = share[height:, :height].astype(jnp.float32)
            row += terms[0:1] + terms[1:2] + terms[2:3]
        column = jnp.sum(jnp.where(own_place, row, 0.0), axis=1, keepdims=True)
        total = (total * lax.rsqrt(column / depth + norm_eps)).astype(jnp.bfloat16)
        span = aligned(tensor ^ r, height)
        for m, kept in enumerate((query, key, value)):
            kept[span, :] = total[:, m * HEAD_DIM : (m + 1) * HEAD_DIM]
    causal = lax.broadcasted_iota(jnp.int32, (height, height), 0) >= lax.broadcasted_iota(
        jnp.int32, (height, height), 1
    )
    for i in range(parts):
        block = query[i * height : (i + 1) * height, :]
        numerator = jnp.zeros((height, HEAD_DIM), jnp.float32)
        denominator = jnp.zeros((height, 1), jnp.float32)
        for j in range(i + 1):
            span = slice(j * height, (j + 1) * height)
            scores = lax.dot_general(
                block, key[span, :], (((1,), (1,)), ((), ())), preferred_element_type=jnp.float32
            )
            raw = capped_exp(scores / math.sqrt(HEAD_DIM))
            if i == j:
                raw = jnp.where(causal, raw, 0.0)
            denominator += jnp.sum(raw, axis=1, keepdims=True)
            numerator += dot(raw.astype(jnp.bfloat16), value[span, :])
        attended[i * height : (i + 1) * height, :] = (numerator / denominator).astype(jnp.bfloat16)


def final_kernel(own, hidden, *refs):
    received, outs, whole = refs[:-3], refs[-3:-1], refs[-1]
    _, core, _ = place()
    total = own[...] + hidden[...].astype(jnp.float32)
    for block in received:
        total += block[...].astype(jnp.float32)
    whole[...] = total
    height = outs[0].shape[0]
    for flip, out in enumerate(outs):
        out[...] = whole[aligned(core ^ flip, height), :].astype(jnp.bfloat16)


def per_device(
    byte_states,
    byte_patch,
    patch_len,
    cross_query,
    cross_key,
    cross_value,
    cross_out,
    norm_gain,
    latent_query,
    latent_key,
    latent_value,
    latent_out,
):
    seq = lax.axis_index("seq")
    core = lax.rem(seq, 2)
    seq_count = lax.axis_size("seq")
    tensor_count = lax.axis_size("tensor")
    chip_count = seq_count // 2
    patch_count = patch_len.shape[0]
    patch_dev = patch_count // seq_count
    spill = patch_dev // 2
    slot_count = patch_dev + 2 * spill
    byte_count, byte_width = byte_states.shape
    local_width = cross_query.shape[1]
    out_width = cross_out.shape[1]
    quarter = patch_count // tensor_count
    bf16, f32 = jnp.bfloat16, jnp.float32
    tile = min(256, byte_count)

    def over_plane(block):
        pieces = []
        for d in range(chip_count):
            moved = exchanged(block, "seq", 2 * d) if d else block
            pieces += [moved, core_swapped(moved)]
        return pieces

    value_weight = lax.all_gather(cross_value, "seq", axis=0, tiled=True)
    slot_of = byte_patch - (seq * patch_dev - spill)
    slot_row = slot_of[None, :]
    edge = jnp.ones((spill,), jnp.int32)
    lengths = lax.dynamic_slice_in_dim(
        jnp.concatenate([edge, patch_len, edge]), seq * patch_dev, slot_count
    ).astype(f32)[:, None]
    query_pieces = over_plane(cross_query)
    key_pieces = over_plane(cross_key)
    (query_slots,) = call(
        functools.partial(query_kernel, seq_count),
        [((slot_count, local_width), bf16)],
        slot_row,
        lengths,
        byte_states,
        *query_pieces,
        far=1 + seq_count,
        scratch=[
            pltpu.VMEM((byte_count, byte_width), bf16),
            pltpu.VMEM((byte_width, local_width), bf16),
            pltpu.SemaphoreType.DMA((1 + seq_count,)),
        ],
        flops=2 * slot_count * byte_width * (byte_count + local_width),
    )
    raw, totals = call(
        functools.partial(score_kernel, seq_count, tile),
        [((byte_count, HEAD_DIM), f32), ((slot_count, HEAD_DIM), f32)],
        slot_row,
        query_slots,
        byte_states,
        *key_pieces,
        far=1 + seq_count,
        scratch=[
            pltpu.VMEM((byte_count, byte_width), bf16),
            pltpu.VMEM((byte_width, local_width), bf16),
            pltpu.SemaphoreType.DMA((1 + seq_count,)),
        ],
        flops=2 * byte_count * local_width * (byte_width + 2 * slot_count),
    )
    weights = []
    for weight in (latent_query, latent_key, latent_value):
        weights += [weight, core_swapped(after(weight, query_slots))]
    head_weights = call(
        arrange_kernel,
        [((2 * out_width, 3 * HEAD_DIM), bf16)] * chip_count,
        *weights,
        far=6,
        scratch=[pltpu.SemaphoreType.DMA((6 * chip_count,))],
    )
    raw, *head_weights = lax.optimization_barrier((raw, *head_weights))
    own, above, below = call(
        functools.partial(value_kernel, tile),
        [((rows, local_width), bf16) for rows in (patch_dev, spill, spill)],
        slot_row,
        raw,
        totals,
        byte_states,
        value_weight,
        far=2,
        scratch=[
            pltpu.VMEM((byte_count, byte_width), bf16),
            pltpu.VMEM((byte_width, local_width), bf16),
            pltpu.VMEM((slot_count, local_width), f32),
            pltpu.SemaphoreType.DMA((2,)),
        ],
        flops=2 * byte_count * local_width * (byte_width + slot_count),
    )

    own = own + jnp.concatenate([shifted(below, "seq", 1), shifted(above, "seq", -1)], axis=0)

    total, *sent = call(
        functools.partial(cross_out_kernel, seq_count),
        [((quarter, out_width), f32 if r == 0 else bf16) for r in range(tensor_count)],
        cross_out,
        *over_plane(own),
        scratch=[pltpu.VMEM((patch_count, local_width), bf16)],
        flops=2 * patch_count * local_width * out_width,
    )
    for r, block in enumerate(sent, 1):
        total = total + exchanged(block, "tensor", r).astype(f32)
    latent_in = total.astype(bf16)

    gain = norm_gain[None, :]
    shares, blocks = [], [latent_in]
    for r in range(tensor_count):
        if r == 1:
            near = [exchanged(latent_in, "tensor", d) for d in (1, 2)]
            blocks += [after(block, shares[0]) for block in near]
        elif r > 2:
            earlier = shares[: (r - 2) * chip_count]
            blocks.append(exchanged(after(latent_in, blocks[r - 2], *earlier), "tensor", r))
        swapped = core_swapped(blocks[r])
        if r > 2:
            blocks[r] = after(blocks[r], *shares[(r - 2) * chip_count :])
        share, *sent = call(
            project_kernel,
            [((quarter + 8, 3 * HEAD_DIM), f32)]
            + [((quarter + 16, 3 * HEAD_DIM), bf16)] * (chip_count - 1),
            blocks[r],
            swapped,
            gain,
            *head_weights,
            scratch=[pltpu.VMEM((quarter, 2 * out_width), bf16)],
            flops=2 * quarter * 2 * out_width * 3 * HEAD_DIM * chip_count,
        )
        shares += [share] + [exchanged(part, "seq", 2 * d) for d, part in enumerate(sent, 1)]
    (attended,) = call(
        functools.partial(attention_kernel, tensor_count, chip_count, out_width * seq_count),
        [((patch_count, HEAD_DIM), bf16)],
        *shares,
        scratch=[pltpu.VMEM((patch_count, HEAD_DIM), bf16)] * 3,
        flops=2 * patch_count * patch_count * HEAD_DIM,
    )

    total, *sent = call(
        functools.partial(latent_out_kernel, seq_count),
        [((quarter, out_width), f32 if r == 0 else bf16) for r in range(tensor_count)],
        latent_out,
        *over_plane(attended),
        scratch=[pltpu.VMEM((patch_count, local_width), bf16)],
        flops=2 * patch_count * local_width * out_width,
    )
    pieces = call(
        final_kernel,
        [((patch_dev, out_width), bf16)] * 2,
        total,
        latent_in,
        *[exchanged(block, "tensor", r) for r, block in enumerate(sent, 1)],
        scratch=[pltpu.VMEM((quarter, out_width), f32)],
    )

    moved = []
    for flip in range(2):
        route = [
            (s * tensor_count + t, (2 * t + ((s % 2) ^ flip)) * tensor_count + s // 2)
            for s in range(seq_count)
            for t in range(tensor_count)
        ]
        moved.append(lax.ppermute(pieces[flip], ("seq", "tensor"), route))
    same, crossed = moved
    return jnp.concatenate(
        [jnp.where(core == 0, same, crossed), jnp.where(core == 0, crossed, same)], axis=1
    )


def head_per_device(mesh, heads):
    seq_count, tensor_count = mesh.shape["seq"], mesh.shape["tensor"]
    return (
        heads == seq_count * tensor_count
        and seq_count == 2 * tensor_count
        and tensor_count & (tensor_count - 1) == 0
    )


def solution(mesh):
    specs = (
        P("seq", None),
        P("seq"),
        P(),
        P("seq", "tensor"),
        P("seq", "tensor"),
        P("seq", "tensor"),
        P("tensor", "seq"),
        P(),
        P("seq", "tensor"),
        P("seq", "tensor"),
        P("seq", "tensor"),
        P("tensor", "seq"),
    )

    def whole(*arrays):
        chosen = (
            per_device
            if head_per_device(mesh, arrays[3].shape[1] // HEAD_DIM)
            else per_device_gathered
        )
        return jax.shard_map(
            chosen, mesh=mesh, in_specs=specs, out_specs=P("seq", "tensor"), check_vma=False
        )(*arrays)

    return whole
```

```python
import functools
import math

import jax
import jax.numpy as jnp
from jax import lax
from jax.experimental import pallas as pl
from jax.experimental.pallas import tpu as pltpu
from jax.sharding import PartitionSpec as P

HEAD_DIM = 128
PATCH_DEV = 128


score_cap = 30.0
norm_eps = 1e-05


def shifted(block, axis, distance):
    devices = range(lax.axis_size(axis))
    route = [(i - distance, i) for i in devices if i - distance in devices]
    return lax.ppermute(block, axis, route)


def capped_exp(scores):
    return jnp.exp(score_cap * jnp.tanh(scores / score_cap))


def contract_rows(left, right):
    return lax.dot_general(
        left,
        right,
        (((0,), (0,)), ((), ())),
        precision=lax.Precision.HIGHEST,
        preferred_element_type=jnp.float32,
    )


def per_device_gathered(
    byte_states,
    byte_patch,
    patch_len,
    cross_query,
    cross_key,
    cross_value,
    cross_out,
    norm_gain,
    latent_query,
    latent_key,
    latent_value,
    latent_out,
):
    seq_index = lax.axis_index("seq")
    tensor_count = lax.axis_size("tensor")
    (
        cross_query,
        cross_key,
        cross_value,
        latent_query,
        latent_key,
        latent_value,
        cross_out,
        latent_out,
    ) = (
        lax.all_gather(cross_query, "seq", axis=0, tiled=True),
        lax.all_gather(cross_key, "seq", axis=0, tiled=True),
        lax.all_gather(cross_value, "seq", axis=0, tiled=True),
        lax.all_gather(latent_query, "seq", axis=0, tiled=True),
        lax.all_gather(latent_key, "seq", axis=0, tiled=True),
        lax.all_gather(latent_value, "seq", axis=0, tiled=True),
        lax.all_gather(cross_out, "seq", axis=1, tiled=True),
        lax.all_gather(latent_out, "seq", axis=1, tiled=True),
    )
    latent_width = cross_out.shape[1]
    local_width = cross_out.shape[0]
    head_count = local_width // HEAD_DIM
    slot_count = 2 * PATCH_DEV
    byte_count = byte_states.shape[0]
    first_patch = byte_patch[0]
    slot_of = byte_patch - first_patch
    onehot_mask = slot_of[:, None] == jnp.arange(slot_count, dtype=jnp.int32)[None, :]
    onehot = onehot_mask.astype(jnp.bfloat16)
    onehot_float = onehot_mask.astype(jnp.float32)
    byte_sums = lax.dot_general(
        onehot, byte_states, (((0,), (0,)), ((), ())), preferred_element_type=jnp.float32
    )
    lengths_all = jnp.concatenate([patch_len, jnp.ones((slot_count,), jnp.int32)])
    lengths = lax.dynamic_slice_in_dim(lengths_all, first_patch, slot_count)
    pooled = (byte_sums / lengths.astype(jnp.float32)[:, None]).astype(jnp.bfloat16)
    query_slots = jnp.dot(pooled, cross_query, preferred_element_type=jnp.float32).astype(
        jnp.bfloat16
    )
    byte_keys = jnp.dot(byte_states, cross_key, preferred_element_type=jnp.float32).astype(
        jnp.bfloat16
    )
    byte_values = jnp.dot(byte_states, cross_value, preferred_element_type=jnp.float32).astype(
        jnp.bfloat16
    )
    query_bytes = jnp.dot(onehot, query_slots, preferred_element_type=jnp.float32)
    scores = (query_bytes * byte_keys.astype(jnp.float32)).reshape(
        byte_count, head_count, HEAD_DIM
    ).sum(axis=2) / math.sqrt(HEAD_DIM)
    byte_raw = capped_exp(scores)
    totals = contract_rows(onehot_float, byte_raw)
    totals = jnp.where(totals > 0.0, totals, 1.0)
    totals_bytes = jnp.dot(
        onehot_float, totals, precision=lax.Precision.HIGHEST, preferred_element_type=jnp.float32
    )
    byte_weight = (byte_raw / totals_bytes).astype(jnp.bfloat16)
    weighted = (
        byte_weight.astype(jnp.float32)[:, :, None]
        * byte_values.astype(jnp.float32).reshape(byte_count, head_count, HEAD_DIM)
    ).reshape(byte_count, local_width)
    cross_heads = contract_rows(onehot_float, weighted).astype(jnp.bfloat16)
    padding = jnp.zeros((2 * PATCH_DEV, cross_heads.shape[1]), cross_heads.dtype)
    padded = jnp.concatenate([padding, cross_heads, padding], axis=0)
    offset = seq_index * PATCH_DEV - first_patch + 2 * PATCH_DEV
    padded, offset = (padded, offset)
    owned_heads = lax.dynamic_slice_in_dim(padded, offset, PATCH_DEV, 0)
    for offset_step in (-1, 1):
        window = lax.dynamic_slice_in_dim(padded, offset + offset_step * PATCH_DEV, PATCH_DEV, 0)
        owned_heads = owned_heads + shifted(window, "seq", offset_step)
    partial_value = jnp.dot(owned_heads, cross_out, preferred_element_type=jnp.float32)
    latent_in = lax.psum(partial_value, "tensor").astype(jnp.bfloat16)
    hidden = latent_in.astype(jnp.float32)
    mean_square = jnp.mean(hidden * hidden, axis=1, keepdims=True)
    normed = (hidden * lax.rsqrt(mean_square + norm_eps) * norm_gain[None, :]).astype(jnp.bfloat16)
    query = (
        jnp.dot(normed, latent_query, preferred_element_type=jnp.float32)
        .astype(jnp.bfloat16)
        .reshape(PATCH_DEV, head_count, HEAD_DIM)
    )
    key_rows = jnp.dot(normed, latent_key, preferred_element_type=jnp.float32).astype(jnp.bfloat16)
    value_rows = jnp.dot(normed, latent_value, preferred_element_type=jnp.float32).astype(
        jnp.bfloat16
    )
    positions = seq_index * PATCH_DEV + jnp.arange(PATCH_DEV, dtype=jnp.int32)
    key_piece = lax.all_gather(key_rows, "seq", axis=0, tiled=True)
    value_piece = lax.all_gather(value_rows, "seq", axis=0, tiled=True)
    piece_rows = key_piece.shape[0]
    key_piece = key_piece.reshape(piece_rows, head_count, HEAD_DIM)
    value_piece = value_piece.reshape(piece_rows, head_count, HEAD_DIM)
    piece_scores = jnp.einsum(
        "qhd,khd->hqk", query, key_piece, preferred_element_type=jnp.float32
    ) / math.sqrt(HEAD_DIM)
    key_positions = jnp.arange(piece_rows, dtype=jnp.int32)
    allowed = key_positions[None, :] <= positions[:, None]
    exp_scores = jnp.where(allowed[None, :, :], capped_exp(piece_scores), 0.0)
    denominator = jnp.sum(exp_scores, axis=2)
    numerator = jnp.einsum(
        "hqk,khd->hqd",
        exp_scores.astype(jnp.bfloat16),
        value_piece,
        preferred_element_type=jnp.float32,
    )
    numerator, denominator = (numerator, denominator)
    attended = (numerator / denominator[:, :, None]).astype(jnp.bfloat16)
    attended = attended.transpose(1, 0, 2).reshape(PATCH_DEV, local_width)
    projected = jnp.dot(attended, latent_out, preferred_element_type=jnp.float32)
    mixed_sum = lax.psum_scatter(projected, "tensor", scatter_dimension=1, tiled=True)
    column_width = latent_width // tensor_count
    residual = lax.dynamic_slice_in_dim(
        hidden, lax.axis_index("tensor") * column_width, column_width, 1
    )
    return (residual + mixed_sum).astype(jnp.bfloat16)


def dot(left, right):
    return jnp.dot(left, right, preferred_element_type=jnp.float32)


def exchanged(block, axis, distance):
    route = [(i, i ^ distance) for i in range(lax.axis_size(axis))]
    return lax.ppermute(block, axis, route)


def core_swapped(block):
    return exchanged(block, "seq", 1)


def after(value, *earlier):
    return lax.optimization_barrier((value, *earlier))[0]


def place():
    seq = lax.axis_index("seq")
    return seq // 2, lax.rem(seq, 2), lax.axis_index("tensor")


def aligned(index, size):
    return pl.ds(pl.multiple_of(index * size, size), size)


def fetched(pairs, semaphores):
    copies = [
        pltpu.make_async_copy(source, target, semaphores.at[n])
        for n, (source, target) in enumerate(pairs)
    ]
    for copy in copies:
        copy.start()
    return copies


def call(kernel, outs, *operands, far=0, scratch=(), flops=0):
    shapes = [jax.ShapeDtypeStruct(shape, dtype) for shape, dtype in outs]
    moved = sum(o.size * o.dtype.itemsize for o in [*operands, *shapes])
    return pl.pallas_call(
        kernel,
        out_shape=shapes,
        in_specs=[pl.BlockSpec(memory_space=pltpu.VMEM)] * (len(operands) - far)
        + [pl.BlockSpec(memory_space=pl.ANY)] * far,
        out_specs=[pl.BlockSpec(memory_space=pltpu.VMEM)] * len(outs),
        scratch_shapes=list(scratch),
        compiler_params=pltpu.CompilerParams(vmem_limit_bytes=28 * 1024 * 1024),
        cost_estimate=pl.CostEstimate(flops=flops, bytes_accessed=moved, transcendentals=0),
    )(*operands)


def assemble(pieces, whole):
    chip, core, _ = place()
    for n, piece in enumerate(pieces):
        index = 2 * (chip ^ (n // 2)) + (core ^ (n % 2))
        whole[aligned(index, piece.shape[0]), :] = piece[...]


def plane_rows(pieces, whole):
    chip, core, _ = place()
    return [
        (piece, whole.at[aligned(2 * (chip ^ (n // 2)) + (core ^ (n % 2)), piece.shape[0]), :])
        for n, piece in enumerate(pieces)
    ]


def query_kernel(count, slot_row, lengths, states, *refs):
    pieces, (query, held, whole, semaphores) = refs[:count], refs[count:]
    slots, byte_count = query.shape[0], states.shape[0]
    copies = fetched([(states, held), *plane_rows(pieces, whole)], semaphores)
    index = lax.broadcasted_iota(jnp.int32, (slots, byte_count), 0)
    onehot = (index == slot_row[...]).astype(jnp.bfloat16)
    copies[0].wait()
    pooled = (dot(onehot, held[...]) / lengths[...]).astype(jnp.bfloat16)
    for copy in copies[1:]:
        copy.wait()
    query[...] = dot(pooled, whole[...]).astype(jnp.bfloat16)


def score_kernel(count, tile, slot_row, query, states, *refs):
    pieces, (raw, totals, held, whole, semaphores) = refs[:count], refs[count:]
    slots, width = query.shape
    head_count = width // HEAD_DIM
    copies = fetched([(states, held), *plane_rows(pieces, whole)], semaphores)
    totals[...] = jnp.zeros_like(totals)
    for copy in copies:
        copy.wait()

    @pl.loop(0, states.shape[0] // tile)
    def _(step):
        span = aligned(step, tile)
        keys = dot(held[span, :], whole[...]).astype(jnp.bfloat16).astype(jnp.float32)
        index = lax.broadcasted_iota(jnp.int32, (slots, tile), 0)
        turned = (index == slot_row[:, span]).astype(jnp.bfloat16)
        product = keys * lax.dot_general(
            turned, query[...], (((0,), (0,)), ((), ())), preferred_element_type=jnp.float32
        )
        lane = lax.broadcasted_iota(jnp.int32, (tile, HEAD_DIM), 1)
        scores = jnp.zeros((tile, HEAD_DIM), jnp.float32)
        for head in range(head_count):
            summed = jnp.sum(
                product[:, head * HEAD_DIM : (head + 1) * HEAD_DIM], axis=1, keepdims=True
            )
            scores = jnp.where(lane == head, summed, scores)
        values = capped_exp(scores / math.sqrt(HEAD_DIM))
        raw[span, :] = values
        high = values.astype(jnp.bfloat16)
        low = (values - high.astype(jnp.float32)).astype(jnp.bfloat16)
        totals[...] += dot(turned, high) + dot(turned, low)


def value_kernel(count, tile, slot_row, raw, totals, states, *refs):
    pieces, (own, above, below, held, whole, summed, semaphores) = refs[:count], refs[count:]
    slots = totals.shape[0]
    copies = fetched([(states, held), *plane_rows(pieces, whole)], semaphores)
    spill = above.shape[0]
    head_count = whole.shape[1] // HEAD_DIM
    summed[...] = jnp.zeros_like(summed)
    for copy in copies:
        copy.wait()

    @pl.loop(0, states.shape[0] // tile)
    def _(step):
        span = aligned(step, tile)
        values = dot(held[span, :], whole[...]).astype(jnp.bfloat16).astype(jnp.float32)
        factors = raw[span, :]
        weighted = jnp.concatenate(
            [
                (values[:, h * HEAD_DIM : (h + 1) * HEAD_DIM] * factors[:, h : h + 1]).astype(
                    jnp.bfloat16
                )
                for h in range(head_count)
            ],
            axis=1,
        )
        index = lax.broadcasted_iota(jnp.int32, (slots, tile), 0)
        turned = (index == slot_row[:, span]).astype(jnp.bfloat16)
        summed[...] += dot(turned, weighted)

    total = totals[...]
    inverse = 1.0 / jnp.where(total > 0.0, total, 1.0)
    for h in range(head_count):
        part = slice(h * HEAD_DIM, (h + 1) * HEAD_DIM)
        heads = (summed[:, part] * inverse[:, h : h + 1]).astype(jnp.bfloat16)
        above[:, part] = heads[:spill]
        own[:, part] = heads[spill : slots - spill]
        below[:, part] = heads[slots - spill :]


def quarters(left, weight, outs):
    _, _, tensor = place()
    height = outs[0].shape[0]
    for r, out in enumerate(outs):
        block = left[aligned(tensor ^ r, height), :]
        out[...] = dot(block, weight[...]).astype(out.dtype)


def cross_out_kernel(count, weight, *refs):
    pieces, outs, whole = refs[:count], refs[count:-1], refs[-1]
    assemble(pieces, whole)
    quarters(whole, weight, outs)


def latent_out_kernel(count, weight, *refs):
    pieces, outs, whole = refs[:count], refs[count:-1], refs[-1]
    chip, core, _ = place()
    for n, piece in enumerate(pieces):
        index = (count // 2) * (core ^ (n % 2)) + (chip ^ (n // 2))
        whole[:, aligned(index, HEAD_DIM)] = piece[...]
    quarters(whole, weight, outs)


def arrange_kernel(*refs):
    weights, outs, semaphores = refs[:6], refs[6:-1], refs[-1]
    chip, core, _ = place()
    height = weights[0].shape[0]
    copies = fetched(
        [
            (
                weights[2 * m + n].at[:, aligned(len(outs) * core + (chip ^ d), HEAD_DIM)],
                out.at[n * height : (n + 1) * height, m * HEAD_DIM : (m + 1) * HEAD_DIM],
            )
            for d, out in enumerate(outs)
            for m in range(3)
            for n in range(2)
        ],
        semaphores,
    )
    for copy in copies:
        copy.wait()


def diagonal(size):
    return lax.broadcasted_iota(jnp.int32, (size, size), 0) == lax.broadcasted_iota(
        jnp.int32, (size, size), 1
    )


def project_kernel(rows_own, rows_other, gain, *refs):
    chips = (len(refs) - 1) // 2
    weights, outs, left = refs[:chips], refs[chips:-1], refs[-1]
    seq = lax.axis_index("seq")
    height, width = rows_own.shape
    total = jnp.zeros((height, 1), jnp.float32)
    for n, block in enumerate((rows_own, rows_other)):
        hidden = block[...].astype(jnp.float32)
        total += jnp.sum(hidden * hidden, axis=1, keepdims=True)
        left[:, n * width : (n + 1) * width] = (
            hidden * gain[:, aligned(seq ^ n, width)]
        ).astype(jnp.bfloat16)
    for weight, out in reversed(list(zip(weights, outs))):
        out[:height, :] = dot(left[...], weight[...]).astype(out.dtype)
    row = jnp.sum(jnp.where(diagonal(height), total, 0.0), axis=0, keepdims=True)
    outs[0][height:, :height] = jnp.broadcast_to(row, (outs[0].shape[0] - height, height))
    high = row.astype(jnp.bfloat16).astype(jnp.float32)
    middle = (row - high).astype(jnp.bfloat16).astype(jnp.float32)
    low = row - high - middle
    index = lax.broadcasted_iota(jnp.int32, (outs[1].shape[0] - height, height), 0)
    terms = jnp.where(index == 0, high, jnp.where(index == 1, middle, low)).astype(jnp.bfloat16)
    for out in outs[1:]:
        out[height:, :height] = terms


def attention_kernel(parts, chips, depth, *refs):
    shares, attended, (query, key, value) = refs[: parts * chips], refs[-4], refs[-3:]
    _, _, tensor = place()
    height = attended.shape[0] // parts
    own_place = diagonal(height)
    for r in range(parts):
        total = shares[r * chips][:height, :]
        row = shares[r * chips][height : height + 1, :height]
        for d in range(1, chips):
            share = shares[r * chips + d]
            total += share[:height, :].astype(jnp.float32)
            terms = share[height:, :height].astype(jnp.float32)
            row += terms[0:1] + terms[1:2] + terms[2:3]
        column = jnp.sum(jnp.where(own_place, row, 0.0), axis=1, keepdims=True)
        total = (total * lax.rsqrt(column / depth + norm_eps)).astype(jnp.bfloat16)
        span = aligned(tensor ^ r, height)
        for m, kept in enumerate((query, key, value)):
            kept[span, :] = total[:, m * HEAD_DIM : (m + 1) * HEAD_DIM]
    causal = lax.broadcasted_iota(jnp.int32, (height, height), 0) >= lax.broadcasted_iota(
        jnp.int32, (height, height), 1
    )
    for i in range(parts):
        block = query[i * height : (i + 1) * height, :]
        numerator = jnp.zeros((height, HEAD_DIM), jnp.float32)
        denominator = jnp.zeros((height, 1), jnp.float32)
        for j in range(i + 1):
            span = slice(j * height, (j + 1) * height)
            scores = lax.dot_general(
                block, key[span, :], (((1,), (1,)), ((), ())), preferred_element_type=jnp.float32
            )
            raw = capped_exp(scores / math.sqrt(HEAD_DIM))
            if i == j:
                raw = jnp.where(causal, raw, 0.0)
            denominator += jnp.sum(raw, axis=1, keepdims=True)
            numerator += dot(raw.astype(jnp.bfloat16), value[span, :])
        attended[i * height : (i + 1) * height, :] = (numerator / denominator).astype(jnp.bfloat16)


def final_kernel(own, hidden, *refs):
    received, outs, whole = refs[:-3], refs[-3:-1], refs[-1]
    _, core, _ = place()
    total = own[...] + hidden[...].astype(jnp.float32)
    for block in received:
        total += block[...].astype(jnp.float32)
    whole[...] = total
    height = outs[0].shape[0]
    for flip, out in enumerate(outs):
        out[...] = whole[aligned(core ^ flip, height), :].astype(jnp.bfloat16)


def per_device(
    byte_states,
    byte_patch,
    patch_len,
    cross_query,
    cross_key,
    cross_value,
    cross_out,
    norm_gain,
    latent_query,
    latent_key,
    latent_value,
    latent_out,
):
    seq = lax.axis_index("seq")
    core = lax.rem(seq, 2)
    seq_count = lax.axis_size("seq")
    tensor_count = lax.axis_size("tensor")
    chip_count = seq_count // 2
    patch_count = patch_len.shape[0]
    patch_dev = patch_count // seq_count
    spill = patch_dev // 2
    slot_count = patch_dev + 2 * spill
    byte_count, byte_width = byte_states.shape
    local_width = cross_query.shape[1]
    out_width = cross_out.shape[1]
    quarter = patch_count // tensor_count
    bf16, f32 = jnp.bfloat16, jnp.float32
    tile = min(256, byte_count)

    def over_plane(block):
        pieces = []
        for d in range(chip_count):
            moved = exchanged(block, "seq", 2 * d) if d else block
            pieces += [moved, core_swapped(moved)]
        return pieces

    slot_of = byte_patch - (seq * patch_dev - spill)
    slot_row = slot_of[None, :]
    edge = jnp.ones((spill,), jnp.int32)
    lengths = lax.dynamic_slice_in_dim(
        jnp.concatenate([edge, patch_len, edge]), seq * patch_dev, slot_count
    ).astype(f32)[:, None]
    query_pieces = over_plane(cross_query)
    key_pieces = over_plane(cross_key)
    value_pieces = over_plane(cross_value)
    (query_slots,) = call(
        functools.partial(query_kernel, seq_count),
        [((slot_count, local_width), bf16)],
        slot_row,
        lengths,
        byte_states,
        *query_pieces,
        far=1 + seq_count,
        scratch=[
            pltpu.VMEM((byte_count, byte_width), bf16),
            pltpu.VMEM((byte_width, local_width), bf16),
            pltpu.SemaphoreType.DMA((1 + seq_count,)),
        ],
        flops=2 * slot_count * byte_width * (byte_count + local_width),
    )
    raw, totals = call(
        functools.partial(score_kernel, seq_count, tile),
        [((byte_count, HEAD_DIM), f32), ((slot_count, HEAD_DIM), f32)],
        slot_row,
        query_slots,
        byte_states,
        *key_pieces,
        far=1 + seq_count,
        scratch=[
            pltpu.VMEM((byte_count, byte_width), bf16),
            pltpu.VMEM((byte_width, local_width), bf16),
            pltpu.SemaphoreType.DMA((1 + seq_count,)),
        ],
        flops=2 * byte_count * local_width * (byte_width + 2 * slot_count),
    )
    weights = []
    for weight in (latent_query, latent_key, latent_value):
        weights += [weight, core_swapped(after(weight, query_slots))]
    head_weights = call(
        arrange_kernel,
        [((2 * out_width, 3 * HEAD_DIM), bf16)] * chip_count,
        *weights,
        far=6,
        scratch=[pltpu.SemaphoreType.DMA((6 * chip_count,))],
    )
    raw, *head_weights = lax.optimization_barrier((raw, *head_weights))
    own, above, below = call(
        functools.partial(value_kernel, seq_count, tile),
        [((rows, local_width), bf16) for rows in (patch_dev, spill, spill)],
        slot_row,
        raw,
        totals,
        byte_states,
        *value_pieces,
        far=1 + seq_count,
        scratch=[
            pltpu.VMEM((byte_count, byte_width), bf16),
            pltpu.VMEM((byte_width, local_width), bf16),
            pltpu.VMEM((slot_count, local_width), f32),
            pltpu.SemaphoreType.DMA((1 + seq_count,)),
        ],
        flops=2 * byte_count * local_width * (byte_width + slot_count),
    )

    own = own + jnp.concatenate([shifted(below, "seq", 1), shifted(above, "seq", -1)], axis=0)

    total, *sent = call(
        functools.partial(cross_out_kernel, seq_count),
        [((quarter, out_width), f32 if r == 0 else bf16) for r in range(tensor_count)],
        cross_out,
        *over_plane(own),
        scratch=[pltpu.VMEM((patch_count, local_width), bf16)],
        flops=2 * patch_count * local_width * out_width,
    )
    for r, block in enumerate(sent, 1):
        total = total + exchanged(block, "tensor", r).astype(f32)
    latent_in = total.astype(bf16)

    gain = norm_gain[None, :]
    shares, block = [], latent_in
    for r in range(tensor_count):
        if r:
            done = shares[(r - 2) * chip_count] if r > 1 else block
            block = exchanged(after(latent_in, block, done), "tensor", r)
        ready = block
        if r == 1:
            ready = after(block, shares[0])
        swapped = core_swapped(ready)
        if r > 1:
            ready = after(block, *shares[(r - 2) * chip_count : (r - 1) * chip_count + 2])
        share, *sent = call(
            project_kernel,
            [((quarter + 8, 3 * HEAD_DIM), f32)]
            + [((quarter + 16, 3 * HEAD_DIM), bf16)] * (chip_count - 1),
            ready,
            swapped,
            gain,
            *head_weights,
            scratch=[pltpu.VMEM((quarter, 2 * out_width), bf16)],
            flops=2 * quarter * 2 * out_width * 3 * HEAD_DIM * chip_count,
        )
        shares += [share] + [exchanged(part, "seq", 2 * d) for d, part in enumerate(sent, 1)]
    (attended,) = call(
        functools.partial(attention_kernel, tensor_count, chip_count, out_width * seq_count),
        [((patch_count, HEAD_DIM), bf16)],
        *shares,
        scratch=[pltpu.VMEM((patch_count, HEAD_DIM), bf16)] * 3,
        flops=2 * patch_count * patch_count * HEAD_DIM,
    )

    total, *sent = call(
        functools.partial(latent_out_kernel, seq_count),
        [((quarter, out_width), f32 if r == 0 else bf16) for r in range(tensor_count)],
        latent_out,
        *over_plane(attended),
        scratch=[pltpu.VMEM((patch_count, local_width), bf16)],
        flops=2 * patch_count * local_width * out_width,
    )
    pieces = call(
        final_kernel,
        [((patch_dev, out_width), bf16)] * 2,
        total,
        latent_in,
        *[exchanged(block, "tensor", r) for r, block in enumerate(sent, 1)],
        scratch=[pltpu.VMEM((quarter, out_width), f32)],
    )

    moved = []
    for flip in range(2):
        route = [
            (s * tensor_count + t, (2 * t + ((s % 2) ^ flip)) * tensor_count + s // 2)
            for s in range(seq_count)
            for t in range(tensor_count)
        ]
        moved.append(lax.ppermute(pieces[flip], ("seq", "tensor"), route))
    same, crossed = moved
    return jnp.concatenate(
        [jnp.where(core == 0, same, crossed), jnp.where(core == 0, crossed, same)], axis=1
    )


def head_per_device(mesh, heads):
    seq_count, tensor_count = mesh.shape["seq"], mesh.shape["tensor"]
    return (
        heads == seq_count * tensor_count
        and seq_count == 2 * tensor_count
        and tensor_count & (tensor_count - 1) == 0
    )


def solution(mesh):
    specs = (
        P("seq", None),
        P("seq"),
        P(),
        P("seq", "tensor"),
        P("seq", "tensor"),
        P("seq", "tensor"),
        P("tensor", "seq"),
        P(),
        P("seq", "tensor"),
        P("seq", "tensor"),
        P("seq", "tensor"),
        P("tensor", "seq"),
    )

    def whole(*arrays):
        chosen = (
            per_device
            if head_per_device(mesh, arrays[3].shape[1] // HEAD_DIM)
            else per_device_gathered
        )
        return jax.shard_map(
            chosen, mesh=mesh, in_specs=specs, out_specs=P("seq", "tensor"), check_vma=False
        )(*arrays)

    return whole
```

```python
import functools
import math

import jax
import jax.numpy as jnp
from jax import lax
from jax.experimental import pallas as pl
from jax.experimental.pallas import tpu as pltpu
from jax.sharding import PartitionSpec as P

HEAD_DIM = 128
PATCH_DEV = 128


score_cap = 30.0
norm_eps = 1e-05


def shifted(block, axis, distance):
    devices = range(lax.axis_size(axis))
    route = [(i - distance, i) for i in devices if i - distance in devices]
    return lax.ppermute(block, axis, route)


def capped_exp(scores):
    return jnp.exp(score_cap * jnp.tanh(scores / score_cap))


def contract_rows(left, right):
    return lax.dot_general(
        left,
        right,
        (((0,), (0,)), ((), ())),
        precision=lax.Precision.HIGHEST,
        preferred_element_type=jnp.float32,
    )


def per_device_gathered(
    byte_states,
    byte_patch,
    patch_len,
    cross_query,
    cross_key,
    cross_value,
    cross_out,
    norm_gain,
    latent_query,
    latent_key,
    latent_value,
    latent_out,
):
    seq_index = lax.axis_index("seq")
    tensor_count = lax.axis_size("tensor")
    (
        cross_query,
        cross_key,
        cross_value,
        latent_query,
        latent_key,
        latent_value,
        cross_out,
        latent_out,
    ) = (
        lax.all_gather(cross_query, "seq", axis=0, tiled=True),
        lax.all_gather(cross_key, "seq", axis=0, tiled=True),
        lax.all_gather(cross_value, "seq", axis=0, tiled=True),
        lax.all_gather(latent_query, "seq", axis=0, tiled=True),
        lax.all_gather(latent_key, "seq", axis=0, tiled=True),
        lax.all_gather(latent_value, "seq", axis=0, tiled=True),
        lax.all_gather(cross_out, "seq", axis=1, tiled=True),
        lax.all_gather(latent_out, "seq", axis=1, tiled=True),
    )
    latent_width = cross_out.shape[1]
    local_width = cross_out.shape[0]
    head_count = local_width // HEAD_DIM
    slot_count = 2 * PATCH_DEV
    byte_count = byte_states.shape[0]
    first_patch = byte_patch[0]
    slot_of = byte_patch - first_patch
    onehot_mask = slot_of[:, None] == jnp.arange(slot_count, dtype=jnp.int32)[None, :]
    onehot = onehot_mask.astype(jnp.bfloat16)
    onehot_float = onehot_mask.astype(jnp.float32)
    byte_sums = lax.dot_general(
        onehot, byte_states, (((0,), (0,)), ((), ())), preferred_element_type=jnp.float32
    )
    lengths_all = jnp.concatenate([patch_len, jnp.ones((slot_count,), jnp.int32)])
    lengths = lax.dynamic_slice_in_dim(lengths_all, first_patch, slot_count)
    pooled = (byte_sums / lengths.astype(jnp.float32)[:, None]).astype(jnp.bfloat16)
    query_slots = jnp.dot(pooled, cross_query, preferred_element_type=jnp.float32).astype(
        jnp.bfloat16
    )
    byte_keys = jnp.dot(byte_states, cross_key, preferred_element_type=jnp.float32).astype(
        jnp.bfloat16
    )
    byte_values = jnp.dot(byte_states, cross_value, preferred_element_type=jnp.float32).astype(
        jnp.bfloat16
    )
    query_bytes = jnp.dot(onehot, query_slots, preferred_element_type=jnp.float32)
    scores = (query_bytes * byte_keys.astype(jnp.float32)).reshape(
        byte_count, head_count, HEAD_DIM
    ).sum(axis=2) / math.sqrt(HEAD_DIM)
    byte_raw = capped_exp(scores)
    totals = contract_rows(onehot_float, byte_raw)
    totals = jnp.where(totals > 0.0, totals, 1.0)
    totals_bytes = jnp.dot(
        onehot_float, totals, precision=lax.Precision.HIGHEST, preferred_element_type=jnp.float32
    )
    byte_weight = (byte_raw / totals_bytes).astype(jnp.bfloat16)
    weighted = (
        byte_weight.astype(jnp.float32)[:, :, None]
        * byte_values.astype(jnp.float32).reshape(byte_count, head_count, HEAD_DIM)
    ).reshape(byte_count, local_width)
    cross_heads = contract_rows(onehot_float, weighted).astype(jnp.bfloat16)
    padding = jnp.zeros((2 * PATCH_DEV, cross_heads.shape[1]), cross_heads.dtype)
    padded = jnp.concatenate([padding, cross_heads, padding], axis=0)
    offset = seq_index * PATCH_DEV - first_patch + 2 * PATCH_DEV
    padded, offset = (padded, offset)
    owned_heads = lax.dynamic_slice_in_dim(padded, offset, PATCH_DEV, 0)
    for offset_step in (-1, 1):
        window = lax.dynamic_slice_in_dim(padded, offset + offset_step * PATCH_DEV, PATCH_DEV, 0)
        owned_heads = owned_heads + shifted(window, "seq", offset_step)
    partial_value = jnp.dot(owned_heads, cross_out, preferred_element_type=jnp.float32)
    latent_in = lax.psum(partial_value, "tensor").astype(jnp.bfloat16)
    hidden = latent_in.astype(jnp.float32)
    mean_square = jnp.mean(hidden * hidden, axis=1, keepdims=True)
    normed = (hidden * lax.rsqrt(mean_square + norm_eps) * norm_gain[None, :]).astype(jnp.bfloat16)
    query = (
        jnp.dot(normed, latent_query, preferred_element_type=jnp.float32)
        .astype(jnp.bfloat16)
        .reshape(PATCH_DEV, head_count, HEAD_DIM)
    )
    key_rows = jnp.dot(normed, latent_key, preferred_element_type=jnp.float32).astype(jnp.bfloat16)
    value_rows = jnp.dot(normed, latent_value, preferred_element_type=jnp.float32).astype(
        jnp.bfloat16
    )
    positions = seq_index * PATCH_DEV + jnp.arange(PATCH_DEV, dtype=jnp.int32)
    key_piece = lax.all_gather(key_rows, "seq", axis=0, tiled=True)
    value_piece = lax.all_gather(value_rows, "seq", axis=0, tiled=True)
    piece_rows = key_piece.shape[0]
    key_piece = key_piece.reshape(piece_rows, head_count, HEAD_DIM)
    value_piece = value_piece.reshape(piece_rows, head_count, HEAD_DIM)
    piece_scores = jnp.einsum(
        "qhd,khd->hqk", query, key_piece, preferred_element_type=jnp.float32
    ) / math.sqrt(HEAD_DIM)
    key_positions = jnp.arange(piece_rows, dtype=jnp.int32)
    allowed = key_positions[None, :] <= positions[:, None]
    exp_scores = jnp.where(allowed[None, :, :], capped_exp(piece_scores), 0.0)
    denominator = jnp.sum(exp_scores, axis=2)
    numerator = jnp.einsum(
        "hqk,khd->hqd",
        exp_scores.astype(jnp.bfloat16),
        value_piece,
        preferred_element_type=jnp.float32,
    )
    numerator, denominator = (numerator, denominator)
    attended = (numerator / denominator[:, :, None]).astype(jnp.bfloat16)
    attended = attended.transpose(1, 0, 2).reshape(PATCH_DEV, local_width)
    projected = jnp.dot(attended, latent_out, preferred_element_type=jnp.float32)
    mixed_sum = lax.psum_scatter(projected, "tensor", scatter_dimension=1, tiled=True)
    column_width = latent_width // tensor_count
    residual = lax.dynamic_slice_in_dim(
        hidden, lax.axis_index("tensor") * column_width, column_width, 1
    )
    return (residual + mixed_sum).astype(jnp.bfloat16)


def dot(left, right):
    return jnp.dot(left, right, preferred_element_type=jnp.float32)


def exchanged(block, axis, distance):
    route = [(i, i ^ distance) for i in range(lax.axis_size(axis))]
    return lax.ppermute(block, axis, route)


def core_swapped(block):
    return exchanged(block, "seq", 1)


def after(value, *earlier):
    return lax.optimization_barrier((value, *earlier))[0]


def place():
    seq = lax.axis_index("seq")
    return seq // 2, lax.rem(seq, 2), lax.axis_index("tensor")


def aligned(index, size):
    return pl.ds(pl.multiple_of(index * size, size), size)


def fetched(pairs, semaphores):
    copies = [
        pltpu.make_async_copy(source, target, semaphores.at[n])
        for n, (source, target) in enumerate(pairs)
    ]
    for copy in copies:
        copy.start()
    return copies


def call(kernel, outs, *operands, far=0, scratch=(), flops=0):
    shapes = [jax.ShapeDtypeStruct(shape, dtype) for shape, dtype in outs]
    moved = sum(o.size * o.dtype.itemsize for o in [*operands, *shapes])
    return pl.pallas_call(
        kernel,
        out_shape=shapes,
        in_specs=[pl.BlockSpec(memory_space=pltpu.VMEM)] * (len(operands) - far)
        + [pl.BlockSpec(memory_space=pl.ANY)] * far,
        out_specs=[pl.BlockSpec(memory_space=pltpu.VMEM)] * len(outs),
        scratch_shapes=list(scratch),
        compiler_params=pltpu.CompilerParams(vmem_limit_bytes=28 * 1024 * 1024),
        cost_estimate=pl.CostEstimate(flops=flops, bytes_accessed=moved, transcendentals=0),
    )(*operands)


def assemble(pieces, whole):
    chip, core, _ = place()
    for n, piece in enumerate(pieces):
        index = 2 * (chip ^ (n // 2)) + (core ^ (n % 2))
        whole[aligned(index, piece.shape[0]), :] = piece[...]


def stack_kernel(*refs):
    sources, stacked, semaphores = refs[:-2], refs[-2], refs[-1]
    height = sources[0].shape[0]
    copies = fetched(
        [(s, stacked.at[n * height : (n + 1) * height, :]) for n, s in enumerate(sources)],
        semaphores,
    )
    for copy in copies:
        copy.wait()


def plane_rows(pieces, whole, part=0):
    chip, core, _ = place()
    height = whole.shape[0] // len(pieces)
    return [
        (
            piece.at[part * height : (part + 1) * height, :],
            whole.at[aligned(2 * (chip ^ (n // 2)) + (core ^ (n % 2)), height), :],
        )
        for n, piece in enumerate(pieces)
    ]


def query_kernel(count, slot_row, lengths, states, *refs):
    pieces, (query, held, whole, semaphores) = refs[:count], refs[count:]
    slots, byte_count = query.shape[0], states.shape[0]
    copies = fetched([(states, held), *plane_rows(pieces, whole)], semaphores)
    index = lax.broadcasted_iota(jnp.int32, (slots, byte_count), 0)
    onehot = (index == slot_row[...]).astype(jnp.bfloat16)
    copies[0].wait()
    pooled = (dot(onehot, held[...]) / lengths[...]).astype(jnp.bfloat16)
    for copy in copies[1:]:
        copy.wait()
    query[...] = dot(pooled, whole[...]).astype(jnp.bfloat16)


def cross_kernel(count, tile, slot_row, query, states, *refs):
    pieces, (own, above, below, *scratch) = refs[:count], refs[count:]
    held, key_weight, value_weight, totals, summed, semaphores = scratch
    slots, width = query.shape
    spill = above.shape[0]
    head_count = width // HEAD_DIM
    pairs = [(states, held)]
    for part, weight in enumerate((key_weight, value_weight)):
        pairs += plane_rows(pieces, weight, part)
    copies = fetched(pairs, semaphores)
    totals[...] = jnp.zeros_like(totals)
    summed[...] = jnp.zeros_like(summed)
    for copy in copies:
        copy.wait()

    @pl.loop(0, states.shape[0] // tile)
    def _(step):
        span = aligned(step, tile)
        block = held[span, :]
        keys = dot(block, key_weight[...]).astype(jnp.bfloat16).astype(jnp.float32)
        index = lax.broadcasted_iota(jnp.int32, (slots, tile), 0)
        onehot = (index == slot_row[:, span]).astype(jnp.bfloat16)
        product = keys * lax.dot_general(
            onehot, query[...], (((0,), (0,)), ((), ())), preferred_element_type=jnp.float32
        )
        lane = lax.broadcasted_iota(jnp.int32, (tile, HEAD_DIM), 1)
        scores = jnp.zeros((tile, HEAD_DIM), jnp.float32)
        for head in range(head_count):
            total = jnp.sum(
                product[:, head * HEAD_DIM : (head + 1) * HEAD_DIM], axis=1, keepdims=True
            )
            scores = jnp.where(lane == head, total, scores)
        raw = capped_exp(scores / math.sqrt(HEAD_DIM))
        high = raw.astype(jnp.bfloat16)
        low = (raw - high.astype(jnp.float32)).astype(jnp.bfloat16)
        totals[...] += dot(onehot, high) + dot(onehot, low)
        values = dot(block, value_weight[...]).astype(jnp.bfloat16).astype(jnp.float32)
        weighted = jnp.concatenate(
            [
                (values[:, h * HEAD_DIM : (h + 1) * HEAD_DIM] * raw[:, h : h + 1]).astype(
                    jnp.bfloat16
                )
                for h in range(head_count)
            ],
            axis=1,
        )
        summed[...] += dot(onehot, weighted)

    total = totals[...]
    inverse = 1.0 / jnp.where(total > 0.0, total, 1.0)
    for h in range(head_count):
        part = slice(h * HEAD_DIM, (h + 1) * HEAD_DIM)
        heads = (summed[:, part] * inverse[:, h : h + 1]).astype(jnp.bfloat16)
        above[:, part] = heads[:spill]
        own[:, part] = heads[spill : slots - spill]
        below[:, part] = heads[slots - spill :]


def quarters(left, weight, outs):
    _, _, tensor = place()
    height = outs[0].shape[0]
    for r, out in enumerate(outs):
        block = left[aligned(tensor ^ r, height), :]
        out[...] = dot(block, weight[...]).astype(out.dtype)


def cross_out_kernel(count, weight, *refs):
    pieces, outs, whole = refs[:count], refs[count:-1], refs[-1]
    assemble(pieces, whole)
    quarters(whole, weight, outs)


def latent_out_kernel(count, weight, *refs):
    pieces, outs, whole = refs[:count], refs[count:-1], refs[-1]
    chip, core, _ = place()
    for n, piece in enumerate(pieces):
        index = (count // 2) * (core ^ (n % 2)) + (chip ^ (n // 2))
        whole[:, aligned(index, HEAD_DIM)] = piece[...]
    quarters(whole, weight, outs)


def arrange_kernel(*refs):
    weights, outs, semaphores = refs[:6], refs[6:-1], refs[-1]
    chip, core, _ = place()
    height = weights[0].shape[0]
    copies = fetched(
        [
            (
                weights[2 * m + n].at[:, aligned(len(outs) * core + (chip ^ d), HEAD_DIM)],
                out.at[n * height : (n + 1) * height, m * HEAD_DIM : (m + 1) * HEAD_DIM],
            )
            for d, out in enumerate(outs)
            for m in range(3)
            for n in range(2)
        ],
        semaphores,
    )
    for copy in copies:
        copy.wait()


def diagonal(size):
    return lax.broadcasted_iota(jnp.int32, (size, size), 0) == lax.broadcasted_iota(
        jnp.int32, (size, size), 1
    )


def project_kernel(count, gain, *refs):
    blocks, refs = refs[: 2 * count], refs[2 * count :]
    chips = (len(refs) - 1) // 2
    weights, outs, left = refs[:chips], refs[chips:-1], refs[-1]
    seq = lax.axis_index("seq")
    part, width = blocks[0].shape
    height = count * part
    totals = []
    for q in range(count):
        total = jnp.zeros((part, 1), jnp.float32)
        for n, block in enumerate(blocks[2 * q : 2 * q + 2]):
            hidden = block[...].astype(jnp.float32)
            total += jnp.sum(hidden * hidden, axis=1, keepdims=True)
            left[q * part : (q + 1) * part, n * width : (n + 1) * width] = (
                hidden * gain[:, aligned(seq ^ n, width)]
            ).astype(jnp.bfloat16)
        totals.append(jnp.sum(jnp.where(diagonal(part), total, 0.0), axis=0, keepdims=True))
    for weight, out in reversed(list(zip(weights, outs))):
        out[:height, :] = dot(left[...], weight[...]).astype(out.dtype)
    outs[0][height:, :] = jnp.zeros((outs[0].shape[0] - height, outs[0].shape[1]), jnp.float32)
    for out in outs[1:]:
        out[height:, :] = jnp.zeros((out.shape[0] - height, out.shape[1]), jnp.bfloat16)
    index = lax.broadcasted_iota(jnp.int32, (16, part), 0)
    own_sums, sent_sums = jnp.zeros((8, part), jnp.float32), jnp.zeros((16, part), jnp.float32)
    for q, row in enumerate(totals):
        high = row.astype(jnp.bfloat16).astype(jnp.float32)
        middle = (row - high).astype(jnp.bfloat16).astype(jnp.float32)
        own_sums = jnp.where(index[:8] == q, row, own_sums)
        for m, term in enumerate((high, middle, row - high - middle)):
            sent_sums = jnp.where(index == 3 * q + m, term, sent_sums)
    outs[0][height:, :part] = own_sums
    for out in outs[1:]:
        out[height:, :part] = sent_sums.astype(jnp.bfloat16)


def attention_kernel(groups, chips, depth, *refs):
    shares, attended, (query, key, value) = refs[: len(groups) * chips], refs[-4], refs[-3:]
    _, _, tensor = place()
    parts = sum(len(group) for group in groups)
    height = attended.shape[0] // parts
    own_place = diagonal(height)
    for g, group in enumerate(groups):
        end = len(group) * height
        own, *received = shares[g * chips : (g + 1) * chips]
        for q, r in enumerate(group):
            rows = slice(q * height, (q + 1) * height)
            total = own[rows, :]
            row = own[end:, :height][q : q + 1]
            for share in received:
                total += share[rows, :].astype(jnp.float32)
                terms = share[end:, :height].astype(jnp.float32)
                row += sum(terms[3 * q + m : 3 * q + m + 1] for m in range(3))
            column = jnp.sum(jnp.where(own_place, row, 0.0), axis=1, keepdims=True)
            total = (total * lax.rsqrt(column / depth + norm_eps)).astype(jnp.bfloat16)
            span = aligned(tensor ^ r, height)
            for m, kept in enumerate((query, key, value)):
                kept[span, :] = total[:, m * HEAD_DIM : (m + 1) * HEAD_DIM]
    causal = lax.broadcasted_iota(jnp.int32, (height, height), 0) >= lax.broadcasted_iota(
        jnp.int32, (height, height), 1
    )
    for i in range(parts):
        block = query[i * height : (i + 1) * height, :]
        numerator = jnp.zeros((height, HEAD_DIM), jnp.float32)
        denominator = jnp.zeros((height, 1), jnp.float32)
        for j in range(i + 1):
            span = slice(j * height, (j + 1) * height)
            scores = lax.dot_general(
                block, key[span, :], (((1,), (1,)), ((), ())), preferred_element_type=jnp.float32
            )
            raw = capped_exp(scores / math.sqrt(HEAD_DIM))
            if i == j:
                raw = jnp.where(causal, raw, 0.0)
            denominator += jnp.sum(raw, axis=1, keepdims=True)
            numerator += dot(raw.astype(jnp.bfloat16), value[span, :])
        attended[i * height : (i + 1) * height, :] = (numerator / denominator).astype(jnp.bfloat16)


def final_kernel(own, hidden, *refs):
    received, outs, whole = refs[:-3], refs[-3:-1], refs[-1]
    _, core, _ = place()
    total = own[...] + hidden[...].astype(jnp.float32)
    for block in received:
        total += block[...].astype(jnp.float32)
    whole[...] = total
    height = outs[0].shape[0]
    for flip, out in enumerate(outs):
        out[...] = whole[aligned(core ^ flip, height), :].astype(jnp.bfloat16)


def per_device(
    byte_states,
    byte_patch,
    patch_len,
    cross_query,
    cross_key,
    cross_value,
    cross_out,
    norm_gain,
    latent_query,
    latent_key,
    latent_value,
    latent_out,
):
    seq = lax.axis_index("seq")
    core = lax.rem(seq, 2)
    seq_count = lax.axis_size("seq")
    tensor_count = lax.axis_size("tensor")
    chip_count = seq_count // 2
    patch_count = patch_len.shape[0]
    patch_dev = patch_count // seq_count
    spill = patch_dev // 2
    slot_count = patch_dev + 2 * spill
    byte_count, byte_width = byte_states.shape
    local_width = cross_query.shape[1]
    out_width = cross_out.shape[1]
    quarter = patch_count // tensor_count
    bf16, f32 = jnp.bfloat16, jnp.float32
    tile = min(256, byte_count)

    def over_plane(block, earlier=()):
        pieces = []
        for d in range(chip_count):
            moved = exchanged(block, "seq", 2 * d) if d else block
            pieces += [moved, core_swapped(after(moved, *earlier) if d else moved)]
        return pieces

    slot_of = byte_patch - (seq * patch_dev - spill)
    slot_row = slot_of[None, :]
    edge = jnp.ones((spill,), jnp.int32)
    lengths = lax.dynamic_slice_in_dim(
        jnp.concatenate([edge, patch_len, edge]), seq * patch_dev, slot_count
    ).astype(f32)[:, None]
    query_pieces = over_plane(cross_query)
    (stacked,) = call(
        stack_kernel,
        [((2 * cross_key.shape[0], local_width), bf16)],
        cross_key,
        cross_value,
        far=2,
        scratch=[pltpu.SemaphoreType.DMA((2,))],
    )
    (query_slots,) = call(
        functools.partial(query_kernel, seq_count),
        [((slot_count, local_width), bf16)],
        slot_row,
        lengths,
        byte_states,
        *query_pieces,
        far=1 + seq_count,
        scratch=[
            pltpu.VMEM((byte_count, byte_width), bf16),
            pltpu.VMEM((byte_width, local_width), bf16),
            pltpu.SemaphoreType.DMA((1 + seq_count,)),
        ],
        flops=2 * slot_count * byte_width * (byte_count + local_width),
    )
    own, above, below = call(
        functools.partial(cross_kernel, seq_count, tile),
        [((height, local_width), bf16) for height in (patch_dev, spill, spill)],
        slot_row,
        query_slots,
        byte_states,
        *over_plane(stacked, (query_slots,)),
        far=1 + seq_count,
        scratch=[
            pltpu.VMEM((byte_count, byte_width), bf16),
            pltpu.VMEM((byte_width, local_width), bf16),
            pltpu.VMEM((byte_width, local_width), bf16),
            pltpu.VMEM((slot_count, HEAD_DIM), f32),
            pltpu.VMEM((slot_count, local_width), f32),
            pltpu.SemaphoreType.DMA((1 + 2 * seq_count,)),
        ],
        flops=4 * byte_count * local_width * (byte_width + slot_count),
    )

    spilled = [shifted(below, "seq", 1), shifted(above, "seq", -1)]
    weights = []
    for weight in (latent_query, latent_key, latent_value):
        weights += [weight, core_swapped(after(weight, own))]
    head_weights = call(
        arrange_kernel,
        [((2 * out_width, 3 * HEAD_DIM), bf16)] * chip_count,
        *weights,
        far=6,
        scratch=[pltpu.SemaphoreType.DMA((6 * chip_count,))],
    )
    own, *head_weights = lax.optimization_barrier((own, *head_weights))
    own = own + jnp.concatenate(spilled, axis=0)

    total, *sent = call(
        functools.partial(cross_out_kernel, seq_count),
        [((quarter, out_width), f32 if r == 0 else bf16) for r in range(tensor_count)],
        cross_out,
        *over_plane(own),
        scratch=[pltpu.VMEM((patch_count, local_width), bf16)],
        flops=2 * patch_count * local_width * out_width,
    )
    for r, block in enumerate(sent, 1):
        total = total + exchanged(block, "tensor", r).astype(f32)
    latent_in = total.astype(bf16)

    gain = norm_gain[None, :]
    groups = [[0], list(range(1, min(3, tensor_count))), list(range(3, tensor_count))]
    groups = [group for group in groups if group]
    shares, arrived = [], []
    for g, group in enumerate(groups):
        blocks = [latent_in]
        if g:
            start = after(latent_in, *arrived, *shares[:chip_count]) if g > 1 else latent_in
            arrived = [exchanged(start, "tensor", r) for r in group]
            blocks = [after(block, *shares[:chip_count]) for block in arrived]
        height = len(group) * quarter
        share, *sent = call(
            functools.partial(project_kernel, len(group)),
            [((height + 8, 3 * HEAD_DIM), f32)]
            + [((height + 16, 3 * HEAD_DIM), bf16)] * (chip_count - 1),
            gain,
            *[piece for block in blocks for piece in (block, core_swapped(block))],
            *head_weights,
            scratch=[pltpu.VMEM((height, 2 * out_width), bf16)],
            flops=2 * height * 2 * out_width * 3 * HEAD_DIM * chip_count,
        )
        if g > 1:
            sent = [after(part, *shares[(g - 1) * chip_count + 1 :]) for part in sent]
        shares += [share] + [exchanged(part, "seq", 2 * d) for d, part in enumerate(sent, 1)]
    (attended,) = call(
        functools.partial(attention_kernel, groups, chip_count, out_width * seq_count),
        [((patch_count, HEAD_DIM), bf16)],
        *shares,
        scratch=[pltpu.VMEM((patch_count, HEAD_DIM), bf16)] * 3,
        flops=2 * patch_count * patch_count * HEAD_DIM,
    )

    total, *sent = call(
        functools.partial(latent_out_kernel, seq_count),
        [((quarter, out_width), f32 if r == 0 else bf16) for r in range(tensor_count)],
        latent_out,
        *over_plane(attended),
        scratch=[pltpu.VMEM((patch_count, local_width), bf16)],
        flops=2 * patch_count * local_width * out_width,
    )
    pieces = call(
        final_kernel,
        [((patch_dev, out_width), bf16)] * 2,
        total,
        latent_in,
        *[exchanged(block, "tensor", r) for r, block in enumerate(sent, 1)],
        scratch=[pltpu.VMEM((quarter, out_width), f32)],
    )

    moved = []
    for flip in range(2):
        route = [
            (s * tensor_count + t, (2 * t + ((s % 2) ^ flip)) * tensor_count + s // 2)
            for s in range(seq_count)
            for t in range(tensor_count)
        ]
        moved.append(lax.ppermute(pieces[flip], ("seq", "tensor"), route))
    same, crossed = moved
    return jnp.concatenate(
        [jnp.where(core == 0, same, crossed), jnp.where(core == 0, crossed, same)], axis=1
    )


def head_per_device(mesh, heads):
    seq_count, tensor_count = mesh.shape["seq"], mesh.shape["tensor"]
    return (
        heads == seq_count * tensor_count
        and seq_count == 2 * tensor_count
        and tensor_count & (tensor_count - 1) == 0
    )


def solution(mesh):
    specs = (
        P("seq", None),
        P("seq"),
        P(),
        P("seq", "tensor"),
        P("seq", "tensor"),
        P("seq", "tensor"),
        P("tensor", "seq"),
        P(),
        P("seq", "tensor"),
        P("seq", "tensor"),
        P("seq", "tensor"),
        P("tensor", "seq"),
    )

    def whole(*arrays):
        chosen = (
            per_device
            if head_per_device(mesh, arrays[3].shape[1] // HEAD_DIM)
            else per_device_gathered
        )
        return jax.shard_map(
            chosen, mesh=mesh, in_specs=specs, out_specs=P("seq", "tensor"), check_vma=False
        )(*arrays)

    return whole
```

```python
import functools
import math

import jax
import jax.numpy as jnp
from jax import lax
from jax.experimental import pallas as pl
from jax.experimental.pallas import tpu as pltpu
from jax.sharding import PartitionSpec as P

HEAD_DIM = 128
PATCH_DEV = 128


score_cap = 30.0
norm_eps = 1e-05


def shifted(block, axis, distance):
    devices = range(lax.axis_size(axis))
    route = [(i - distance, i) for i in devices if i - distance in devices]
    return lax.ppermute(block, axis, route)


def capped_exp(scores):
    return jnp.exp(score_cap * jnp.tanh(scores / score_cap))


def contract_rows(left, right):
    return lax.dot_general(
        left,
        right,
        (((0,), (0,)), ((), ())),
        precision=lax.Precision.HIGHEST,
        preferred_element_type=jnp.float32,
    )


def per_device_gathered(
    byte_states,
    byte_patch,
    patch_len,
    cross_query,
    cross_key,
    cross_value,
    cross_out,
    norm_gain,
    latent_query,
    latent_key,
    latent_value,
    latent_out,
):
    seq_index = lax.axis_index("seq")
    tensor_count = lax.axis_size("tensor")
    (
        cross_query,
        cross_key,
        cross_value,
        latent_query,
        latent_key,
        latent_value,
        cross_out,
        latent_out,
    ) = (
        lax.all_gather(cross_query, "seq", axis=0, tiled=True),
        lax.all_gather(cross_key, "seq", axis=0, tiled=True),
        lax.all_gather(cross_value, "seq", axis=0, tiled=True),
        lax.all_gather(latent_query, "seq", axis=0, tiled=True),
        lax.all_gather(latent_key, "seq", axis=0, tiled=True),
        lax.all_gather(latent_value, "seq", axis=0, tiled=True),
        lax.all_gather(cross_out, "seq", axis=1, tiled=True),
        lax.all_gather(latent_out, "seq", axis=1, tiled=True),
    )
    latent_width = cross_out.shape[1]
    local_width = cross_out.shape[0]
    head_count = local_width // HEAD_DIM
    slot_count = 2 * PATCH_DEV
    byte_count = byte_states.shape[0]
    first_patch = byte_patch[0]
    slot_of = byte_patch - first_patch
    onehot_mask = slot_of[:, None] == jnp.arange(slot_count, dtype=jnp.int32)[None, :]
    onehot = onehot_mask.astype(jnp.bfloat16)
    onehot_float = onehot_mask.astype(jnp.float32)
    byte_sums = lax.dot_general(
        onehot, byte_states, (((0,), (0,)), ((), ())), preferred_element_type=jnp.float32
    )
    lengths_all = jnp.concatenate([patch_len, jnp.ones((slot_count,), jnp.int32)])
    lengths = lax.dynamic_slice_in_dim(lengths_all, first_patch, slot_count)
    pooled = (byte_sums / lengths.astype(jnp.float32)[:, None]).astype(jnp.bfloat16)
    query_slots = jnp.dot(pooled, cross_query, preferred_element_type=jnp.float32).astype(
        jnp.bfloat16
    )
    byte_keys = jnp.dot(byte_states, cross_key, preferred_element_type=jnp.float32).astype(
        jnp.bfloat16
    )
    byte_values = jnp.dot(byte_states, cross_value, preferred_element_type=jnp.float32).astype(
        jnp.bfloat16
    )
    query_bytes = jnp.dot(onehot, query_slots, preferred_element_type=jnp.float32)
    scores = (query_bytes * byte_keys.astype(jnp.float32)).reshape(
        byte_count, head_count, HEAD_DIM
    ).sum(axis=2) / math.sqrt(HEAD_DIM)
    byte_raw = capped_exp(scores)
    totals = contract_rows(onehot_float, byte_raw)
    totals = jnp.where(totals > 0.0, totals, 1.0)
    totals_bytes = jnp.dot(
        onehot_float, totals, precision=lax.Precision.HIGHEST, preferred_element_type=jnp.float32
    )
    byte_weight = (byte_raw / totals_bytes).astype(jnp.bfloat16)
    weighted = (
        byte_weight.astype(jnp.float32)[:, :, None]
        * byte_values.astype(jnp.float32).reshape(byte_count, head_count, HEAD_DIM)
    ).reshape(byte_count, local_width)
    cross_heads = contract_rows(onehot_float, weighted).astype(jnp.bfloat16)
    padding = jnp.zeros((2 * PATCH_DEV, cross_heads.shape[1]), cross_heads.dtype)
    padded = jnp.concatenate([padding, cross_heads, padding], axis=0)
    offset = seq_index * PATCH_DEV - first_patch + 2 * PATCH_DEV
    padded, offset = (padded, offset)
    owned_heads = lax.dynamic_slice_in_dim(padded, offset, PATCH_DEV, 0)
    for offset_step in (-1, 1):
        window = lax.dynamic_slice_in_dim(padded, offset + offset_step * PATCH_DEV, PATCH_DEV, 0)
        owned_heads = owned_heads + shifted(window, "seq", offset_step)
    partial_value = jnp.dot(owned_heads, cross_out, preferred_element_type=jnp.float32)
    latent_in = lax.psum(partial_value, "tensor").astype(jnp.bfloat16)
    hidden = latent_in.astype(jnp.float32)
    mean_square = jnp.mean(hidden * hidden, axis=1, keepdims=True)
    normed = (hidden * lax.rsqrt(mean_square + norm_eps) * norm_gain[None, :]).astype(jnp.bfloat16)
    query = (
        jnp.dot(normed, latent_query, preferred_element_type=jnp.float32)
        .astype(jnp.bfloat16)
        .reshape(PATCH_DEV, head_count, HEAD_DIM)
    )
    key_rows = jnp.dot(normed, latent_key, preferred_element_type=jnp.float32).astype(jnp.bfloat16)
    value_rows = jnp.dot(normed, latent_value, preferred_element_type=jnp.float32).astype(
        jnp.bfloat16
    )
    positions = seq_index * PATCH_DEV + jnp.arange(PATCH_DEV, dtype=jnp.int32)
    key_piece = lax.all_gather(key_rows, "seq", axis=0, tiled=True)
    value_piece = lax.all_gather(value_rows, "seq", axis=0, tiled=True)
    piece_rows = key_piece.shape[0]
    key_piece = key_piece.reshape(piece_rows, head_count, HEAD_DIM)
    value_piece = value_piece.reshape(piece_rows, head_count, HEAD_DIM)
    piece_scores = jnp.einsum(
        "qhd,khd->hqk", query, key_piece, preferred_element_type=jnp.float32
    ) / math.sqrt(HEAD_DIM)
    key_positions = jnp.arange(piece_rows, dtype=jnp.int32)
    allowed = key_positions[None, :] <= positions[:, None]
    exp_scores = jnp.where(allowed[None, :, :], capped_exp(piece_scores), 0.0)
    denominator = jnp.sum(exp_scores, axis=2)
    numerator = jnp.einsum(
        "hqk,khd->hqd",
        exp_scores.astype(jnp.bfloat16),
        value_piece,
        preferred_element_type=jnp.float32,
    )
    numerator, denominator = (numerator, denominator)
    attended = (numerator / denominator[:, :, None]).astype(jnp.bfloat16)
    attended = attended.transpose(1, 0, 2).reshape(PATCH_DEV, local_width)
    projected = jnp.dot(attended, latent_out, preferred_element_type=jnp.float32)
    mixed_sum = lax.psum_scatter(projected, "tensor", scatter_dimension=1, tiled=True)
    column_width = latent_width // tensor_count
    residual = lax.dynamic_slice_in_dim(
        hidden, lax.axis_index("tensor") * column_width, column_width, 1
    )
    return (residual + mixed_sum).astype(jnp.bfloat16)


def dot(left, right):
    return jnp.dot(left, right, preferred_element_type=jnp.float32)


def exchanged(block, axis, distance):
    route = [(i, i ^ distance) for i in range(lax.axis_size(axis))]
    return lax.ppermute(block, axis, route)


def core_swapped(block):
    return exchanged(block, "seq", 1)


def after(value, *earlier):
    return lax.optimization_barrier((value, *earlier))[0]


def place():
    seq = lax.axis_index("seq")
    return seq // 2, lax.rem(seq, 2), lax.axis_index("tensor")


def aligned(index, size):
    return pl.ds(pl.multiple_of(index * size, size), size)


def fetched(pairs, semaphores):
    copies = [
        pltpu.make_async_copy(source, target, semaphores.at[n])
        for n, (source, target) in enumerate(pairs)
    ]
    for copy in copies:
        copy.start()
    return copies


def call(kernel, outs, *operands, far=0, scratch=(), flops=0):
    shapes = [jax.ShapeDtypeStruct(shape, dtype) for shape, dtype in outs]
    moved = sum(o.size * o.dtype.itemsize for o in [*operands, *shapes])
    return pl.pallas_call(
        kernel,
        out_shape=shapes,
        in_specs=[pl.BlockSpec(memory_space=pltpu.VMEM)] * (len(operands) - far)
        + [pl.BlockSpec(memory_space=pl.ANY)] * far,
        out_specs=[pl.BlockSpec(memory_space=pltpu.VMEM)] * len(outs),
        scratch_shapes=list(scratch),
        compiler_params=pltpu.CompilerParams(vmem_limit_bytes=28 * 1024 * 1024),
        cost_estimate=pl.CostEstimate(flops=flops, bytes_accessed=moved, transcendentals=0),
    )(*operands)


def stack_kernel(*refs):
    sources, stacked, semaphores = refs[:-2], refs[-2], refs[-1]
    height = sources[0].shape[0]
    copies = fetched(
        [(s, stacked.at[n * height : (n + 1) * height, :]) for n, s in enumerate(sources)],
        semaphores,
    )
    for copy in copies:
        copy.wait()


def plane_rows(pieces, whole, part=0):
    chip, core, _ = place()
    height = whole.shape[0] // len(pieces)
    return [
        (
            piece.at[part * height : (part + 1) * height, :],
            whole.at[aligned(2 * (chip ^ (n // 2)) + (core ^ (n % 2)), height), :],
        )
        for n, piece in enumerate(pieces)
    ]


def query_kernel(count, slot_row, lengths, states, *refs):
    pieces, (query, held, whole, semaphores) = refs[:count], refs[count:]
    slots, byte_count = query.shape[0], states.shape[0]
    copies = fetched([(states, held), *plane_rows(pieces, whole)], semaphores)
    index = lax.broadcasted_iota(jnp.int32, (slots, byte_count), 0)
    onehot = (index == slot_row[...]).astype(jnp.bfloat16)
    copies[0].wait()
    pooled = (dot(onehot, held[...]) / lengths[...]).astype(jnp.bfloat16)
    for copy in copies[1:]:
        copy.wait()
    query[...] = dot(pooled, whole[...]).astype(jnp.bfloat16)


def cross_kernel(count, tile, slot_row, query, states, *refs):
    pieces, (own, above, below, *scratch) = refs[:count], refs[count:]
    held, key_weight, value_weight, totals, summed, semaphores = scratch
    slots, width = query.shape
    spill = above.shape[0]
    head_count = width // HEAD_DIM
    pairs = [(states, held)]
    for part, weight in enumerate((key_weight, value_weight)):
        pairs += plane_rows(pieces, weight, part)
    copies = fetched(pairs, semaphores)
    totals[...] = jnp.zeros_like(totals)
    summed[...] = jnp.zeros_like(summed)
    for copy in copies:
        copy.wait()

    @pl.loop(0, states.shape[0] // tile)
    def _(step):
        span = aligned(step, tile)
        block = held[span, :]
        keys = dot(block, key_weight[...]).astype(jnp.bfloat16).astype(jnp.float32)
        index = lax.broadcasted_iota(jnp.int32, (slots, tile), 0)
        onehot = (index == slot_row[:, span]).astype(jnp.bfloat16)
        product = keys * lax.dot_general(
            onehot, query[...], (((0,), (0,)), ((), ())), preferred_element_type=jnp.float32
        )
        lane = lax.broadcasted_iota(jnp.int32, (tile, HEAD_DIM), 1)
        scores = jnp.zeros((tile, HEAD_DIM), jnp.float32)
        for head in range(head_count):
            total = jnp.sum(
                product[:, head * HEAD_DIM : (head + 1) * HEAD_DIM], axis=1, keepdims=True
            )
            scores = jnp.where(lane == head, total, scores)
        raw = capped_exp(scores / math.sqrt(HEAD_DIM))
        high = raw.astype(jnp.bfloat16)
        low = (raw - high.astype(jnp.float32)).astype(jnp.bfloat16)
        totals[...] += dot(onehot, high) + dot(onehot, low)
        values = dot(block, value_weight[...]).astype(jnp.bfloat16).astype(jnp.float32)
        weighted = jnp.concatenate(
            [
                (values[:, h * HEAD_DIM : (h + 1) * HEAD_DIM] * raw[:, h : h + 1]).astype(
                    jnp.bfloat16
                )
                for h in range(head_count)
            ],
            axis=1,
        )
        summed[...] += dot(onehot, weighted)

    total = totals[...]
    inverse = 1.0 / jnp.where(total > 0.0, total, 1.0)
    for h in range(head_count):
        part = slice(h * HEAD_DIM, (h + 1) * HEAD_DIM)
        heads = (summed[:, part] * inverse[:, h : h + 1]).astype(jnp.bfloat16)
        above[:, part] = heads[:spill]
        own[:, part] = heads[spill : slots - spill]
        below[:, part] = heads[slots - spill :]


def spill_kernel(halves, own, first, last, *refs):
    outs, whole = refs[:-1], refs[-1]
    _, _, tensor = place()
    spill = first.shape[0]
    whole[:spill, :] = own[:spill, :] + first[...]
    whole[spill:, :] = own[spill:, :] + last[...]
    for half, out in zip(halves, outs):
        height = out.shape[0] // len(half)
        for n, r in enumerate(half):
            out[n * height : (n + 1) * height, :] = whole[aligned(tensor ^ r, height), :]


def products(whole, weight, outs):
    height = outs[0].shape[0]
    for n, out in enumerate(outs):
        block = whole[n * height : (n + 1) * height, :]
        out[...] = dot(block, weight[...]).astype(out.dtype)


def add_kernel(*refs):
    total = refs[0][...].astype(jnp.float32)
    for share in refs[1:-1]:
        total += share[...].astype(jnp.float32)
    refs[-1][...] = total


def cross_out_kernel(count, weight, *refs):
    pieces, outs, whole = refs[:count], refs[count:-1], refs[-1]
    chip, core, _ = place()
    height = pieces[0].shape[0] // len(outs)
    for n, piece in enumerate(pieces):
        index = 2 * (chip ^ (n // 2)) + (core ^ (n % 2))
        for m in range(len(outs)):
            whole[aligned(m * count + index, height), :] = piece[m * height : (m + 1) * height, :]
    products(whole, weight, outs)


def latent_out_kernel(count, weight, *refs):
    pieces, outs, whole = refs[:count], refs[count:-1], refs[-1]
    chip, core, _ = place()
    for n, piece in enumerate(pieces):
        index = (count // 2) * (core ^ (n % 2)) + (chip ^ (n // 2))
        whole[:, aligned(index, HEAD_DIM)] = piece[...]
    products(whole, weight, outs)


def arrange_kernel(*refs):
    weights, outs, semaphores = refs[:6], refs[6:-1], refs[-1]
    chip, core, _ = place()
    height = weights[0].shape[0]
    copies = fetched(
        [
            (
                weights[2 * m + n].at[:, aligned(len(outs) * core + (chip ^ d), HEAD_DIM)],
                out.at[n * height : (n + 1) * height, m * HEAD_DIM : (m + 1) * HEAD_DIM],
            )
            for d, out in enumerate(outs)
            for m in range(3)
            for n in range(2)
        ],
        semaphores,
    )
    for copy in copies:
        copy.wait()


def diagonal(size):
    return lax.broadcasted_iota(jnp.int32, (size, size), 0) == lax.broadcasted_iota(
        jnp.int32, (size, size), 1
    )


def project_kernel(count, gain, *refs):
    blocks, refs = refs[: 2 * count], refs[2 * count :]
    chips = (len(refs) - 1) // 2
    weights, outs, left = refs[:chips], refs[chips:-1], refs[-1]
    seq = lax.axis_index("seq")
    part, width = blocks[0].shape
    height = count * part
    totals = []
    for q in range(count):
        total = jnp.zeros((part, 1), jnp.float32)
        for n, block in enumerate(blocks[2 * q : 2 * q + 2]):
            hidden = block[...].astype(jnp.float32)
            total += jnp.sum(hidden * hidden, axis=1, keepdims=True)
            left[q * part : (q + 1) * part, n * width : (n + 1) * width] = (
                hidden * gain[:, aligned(seq ^ n, width)]
            ).astype(jnp.bfloat16)
        totals.append(jnp.sum(jnp.where(diagonal(part), total, 0.0), axis=0, keepdims=True))
    for weight, out in reversed(list(zip(weights, outs))):
        out[:height, :] = dot(left[...], weight[...]).astype(out.dtype)
    outs[0][height:, :] = jnp.zeros((outs[0].shape[0] - height, outs[0].shape[1]), jnp.float32)
    for out in outs[1:]:
        out[height:, :] = jnp.zeros((out.shape[0] - height, out.shape[1]), jnp.bfloat16)
    index = lax.broadcasted_iota(jnp.int32, (16, part), 0)
    own_sums, sent_sums = jnp.zeros((8, part), jnp.float32), jnp.zeros((16, part), jnp.float32)
    for q, row in enumerate(totals):
        high = row.astype(jnp.bfloat16).astype(jnp.float32)
        middle = (row - high).astype(jnp.bfloat16).astype(jnp.float32)
        own_sums = jnp.where(index[:8] == q, row, own_sums)
        for m, term in enumerate((high, middle, row - high - middle)):
            sent_sums = jnp.where(index == 3 * q + m, term, sent_sums)
    outs[0][height:, :part] = own_sums
    for out in outs[1:]:
        out[height:, :part] = sent_sums.astype(jnp.bfloat16)


def attention_kernel(groups, halves, chips, depth, *refs):
    shares, refs = refs[: len(groups) * chips], refs[len(groups) * chips :]
    outs, (query, key, value, attended) = refs[: len(halves)], refs[len(halves) :]
    _, _, tensor = place()
    parts = sum(len(group) for group in groups)
    height = attended.shape[0] // parts
    piece = height // (2 * chips)
    own_place = diagonal(height)
    for g, group in enumerate(groups):
        end = len(group) * height
        own, *received = shares[g * chips : (g + 1) * chips]
        for q, r in enumerate(group):
            rows = slice(q * height, (q + 1) * height)
            total = own[rows, :]
            row = own[end:, :height][q : q + 1]
            for share in received:
                total += share[rows, :].astype(jnp.float32)
                terms = share[end:, :height].astype(jnp.float32)
                row += sum(terms[3 * q + m : 3 * q + m + 1] for m in range(3))
            column = jnp.sum(jnp.where(own_place, row, 0.0), axis=1, keepdims=True)
            total = (total * lax.rsqrt(column / depth + norm_eps)).astype(jnp.bfloat16)
            for m, kept in enumerate((query, key, value)):
                for n in range(2 * chips):
                    kept[aligned(n * parts + (tensor ^ r), piece), :] = total[
                        n * piece : (n + 1) * piece, m * HEAD_DIM : (m + 1) * HEAD_DIM
                    ]
    causal = lax.broadcasted_iota(jnp.int32, (height, height), 0) >= lax.broadcasted_iota(
        jnp.int32, (height, height), 1
    )
    for i in range(parts):
        block = query[i * height : (i + 1) * height, :]
        numerator = jnp.zeros((height, HEAD_DIM), jnp.float32)
        denominator = jnp.zeros((height, 1), jnp.float32)
        for j in range(i + 1):
            span = slice(j * height, (j + 1) * height)
            scores = lax.dot_general(
                block, key[span, :], (((1,), (1,)), ((), ())), preferred_element_type=jnp.float32
            )
            raw = capped_exp(scores / math.sqrt(HEAD_DIM))
            if i == j:
                raw = jnp.where(causal, raw, 0.0)
            denominator += jnp.sum(raw, axis=1, keepdims=True)
            numerator += dot(raw.astype(jnp.bfloat16), value[span, :])
        attended[i * height : (i + 1) * height, :] = (numerator / denominator).astype(jnp.bfloat16)
    for half, out in zip(halves, outs):
        for n, r in enumerate(half):
            out[n * height : (n + 1) * height, :] = attended[aligned(tensor ^ r, height), :]


def final_kernel(parts, own, *refs):
    blocks, received, outs, whole = refs[:parts], refs[parts:-3], refs[-3:-1], refs[-1]
    _, core, tensor = place()
    total = own[...]
    for share in received:
        total += share[...].astype(jnp.float32)
    whole[...] = total
    height = outs[0].shape[0]
    piece = height // parts
    for n in range(2):
        for r, block in enumerate(blocks):
            span = aligned(n * parts + (tensor ^ r), piece)
            rows = aligned(2 * tensor + n, piece)
            whole[span, :] += block[rows, :].astype(jnp.float32)
    for flip, out in enumerate(outs):
        out[...] = whole[aligned(core ^ flip, height), :].astype(jnp.bfloat16)


def per_device(
    byte_states,
    byte_patch,
    patch_len,
    cross_query,
    cross_key,
    cross_value,
    cross_out,
    norm_gain,
    latent_query,
    latent_key,
    latent_value,
    latent_out,
):
    seq = lax.axis_index("seq")
    core = lax.rem(seq, 2)
    seq_count = lax.axis_size("seq")
    tensor_count = lax.axis_size("tensor")
    chip_count = seq_count // 2
    patch_count = patch_len.shape[0]
    patch_dev = patch_count // seq_count
    spill = patch_dev // 2
    slot_count = patch_dev + 2 * spill
    byte_count, byte_width = byte_states.shape
    local_width = cross_query.shape[1]
    out_width = cross_out.shape[1]
    quarter = patch_count // tensor_count
    bf16, f32 = jnp.bfloat16, jnp.float32
    tile = min(256, byte_count)

    def over_plane(block, earlier=()):
        pieces = []
        for d in range(chip_count):
            moved = exchanged(block, "seq", 2 * d) if d else block
            pieces += [moved, core_swapped(after(moved, *earlier) if d else moved)]
        return pieces

    slot_of = byte_patch - (seq * patch_dev - spill)
    slot_row = slot_of[None, :]
    edge = jnp.ones((spill,), jnp.int32)
    lengths = lax.dynamic_slice_in_dim(
        jnp.concatenate([edge, patch_len, edge]), seq * patch_dev, slot_count
    ).astype(f32)[:, None]
    query_pieces = over_plane(cross_query)
    (stacked,) = call(
        stack_kernel,
        [((2 * cross_key.shape[0], local_width), bf16)],
        cross_key,
        cross_value,
        far=2,
        scratch=[pltpu.SemaphoreType.DMA((2,))],
    )
    (query_slots,) = call(
        functools.partial(query_kernel, seq_count),
        [((slot_count, local_width), bf16)],
        slot_row,
        lengths,
        byte_states,
        *query_pieces,
        far=1 + seq_count,
        scratch=[
            pltpu.VMEM((byte_count, byte_width), bf16),
            pltpu.VMEM((byte_width, local_width), bf16),
            pltpu.SemaphoreType.DMA((1 + seq_count,)),
        ],
        flops=2 * slot_count * byte_width * (byte_count + local_width),
    )
    own, above, below = call(
        functools.partial(cross_kernel, seq_count, tile),
        [((height, local_width), bf16) for height in (patch_dev, spill, spill)],
        slot_row,
        query_slots,
        byte_states,
        *over_plane(stacked, (query_slots,)),
        far=1 + seq_count,
        scratch=[
            pltpu.VMEM((byte_count, byte_width), bf16),
            pltpu.VMEM((byte_width, local_width), bf16),
            pltpu.VMEM((byte_width, local_width), bf16),
            pltpu.VMEM((slot_count, HEAD_DIM), f32),
            pltpu.VMEM((slot_count, local_width), f32),
            pltpu.SemaphoreType.DMA((1 + 2 * seq_count,)),
        ],
        flops=4 * byte_count * local_width * (byte_width + slot_count),
    )

    half = max(1, tensor_count // 2)
    halves = [list(range(half, tensor_count)), list(range(half))]
    first, last = shifted(below, "seq", 1), shifted(above, "seq", -1)
    sorted_heads = call(
        functools.partial(spill_kernel, halves),
        [((patch_dev * len(group) // tensor_count, local_width), bf16) for group in halves],
        own,
        first,
        last,
        scratch=[pltpu.VMEM((patch_dev, local_width), bf16)],
    )

    def summed_shares(kernel, weight, operands, width):
        shares, earlier = [], ()
        for group, operand in zip(halves, operands):
            pieces = over_plane(after(operand, *earlier))
            height = len(group) * quarter
            outs = call(
                functools.partial(kernel, seq_count),
                [((quarter, out_width), bf16 if r else f32) for r in group],
                weight,
                *pieces,
                scratch=[pltpu.VMEM((height, width), bf16)],
                flops=2 * height * width * out_width,
            )
            earlier = outs[:1]
            shares += [exchanged(out, "tensor", r) if r else out for r, out in zip(group, outs)]
        far, (own_share, *near) = shares[: len(halves[0])], shares[len(halves[0]) :]
        (far_sum,) = call(
            add_kernel,
            [((quarter, out_width), f32)],
            *[after(share, own_share, *near) for share in far],
            flops=32 * patch_count * width * out_width,
        )
        return own_share, [far_sum, *near]

    total, received = summed_shares(cross_out_kernel, cross_out, sorted_heads, local_width)

    weights = []
    for weight in (latent_query, latent_key, latent_value):
        weights += [weight, core_swapped(after(weight, total))]
    head_weights = call(
        arrange_kernel,
        [((2 * out_width, 3 * HEAD_DIM), bf16)] * chip_count,
        *weights,
        far=6,
        scratch=[pltpu.SemaphoreType.DMA((6 * chip_count,))],
    )
    total, *head_weights = lax.optimization_barrier((total, *head_weights))
    for share in received:
        total = total + share.astype(f32)
    latent_in = total.astype(bf16)

    gain = norm_gain[None, :]
    groups = [[0], list(range(1, min(3, tensor_count))), list(range(3, tensor_count))]
    groups = [group for group in groups if group]
    shares, arrived, latent_blocks = [], [], [latent_in]
    for g, group in enumerate(groups):
        blocks = [latent_in]
        if g:
            start = after(latent_in, *arrived, *shares[:chip_count]) if g > 1 else latent_in
            arrived = [exchanged(start, "tensor", r) for r in group]
            latent_blocks += arrived
            blocks = [after(block, *shares[:chip_count]) for block in arrived]
        height = len(group) * quarter
        share, *sent = call(
            functools.partial(project_kernel, len(group)),
            [((height + 8, 3 * HEAD_DIM), f32)]
            + [((height + 16, 3 * HEAD_DIM), bf16)] * (chip_count - 1),
            gain,
            *[piece for block in blocks for piece in (block, core_swapped(block))],
            *head_weights,
            scratch=[pltpu.VMEM((height, 2 * out_width), bf16)],
            flops=2 * height * 2 * out_width * 3 * HEAD_DIM * chip_count,
        )
        if g > 1:
            sent[-1] = after(sent[-1], *shares[(g - 1) * chip_count + 1 :])
        shares += [share] + [exchanged(part, "seq", 2 * d) for d, part in enumerate(sent, 1)]
    attended = call(
        functools.partial(attention_kernel, groups, halves, chip_count, out_width * seq_count),
        [((len(group) * quarter, HEAD_DIM), bf16) for group in halves],
        *shares,
        scratch=[pltpu.VMEM((patch_count, HEAD_DIM), bf16)] * 4,
        flops=2 * patch_count * patch_count * HEAD_DIM,
    )

    total, received = summed_shares(latent_out_kernel, latent_out, attended, local_width)
    pieces = call(
        functools.partial(final_kernel, tensor_count),
        [((patch_dev, out_width), bf16)] * 2,
        total,
        *latent_blocks,
        *received,
        scratch=[pltpu.VMEM((quarter, out_width), f32)],
    )

    moved = []
    for flip in range(2):
        route = [
            (s * tensor_count + t, (2 * t + ((s % 2) ^ flip)) * tensor_count + s // 2)
            for s in range(seq_count)
            for t in range(tensor_count)
        ]
        moved.append(lax.ppermute(pieces[flip], ("seq", "tensor"), route))
    same, crossed = moved
    return jnp.concatenate(
        [jnp.where(core == 0, same, crossed), jnp.where(core == 0, crossed, same)], axis=1
    )


def head_per_device(mesh, heads):
    seq_count, tensor_count = mesh.shape["seq"], mesh.shape["tensor"]
    return (
        heads == seq_count * tensor_count
        and seq_count == 2 * tensor_count
        and tensor_count & (tensor_count - 1) == 0
    )


def solution(mesh):
    specs = (
        P("seq", None),
        P("seq"),
        P(),
        P("seq", "tensor"),
        P("seq", "tensor"),
        P("seq", "tensor"),
        P("tensor", "seq"),
        P(),
        P("seq", "tensor"),
        P("seq", "tensor"),
        P("seq", "tensor"),
        P("tensor", "seq"),
    )

    def whole(*arrays):
        chosen = (
            per_device
            if head_per_device(mesh, arrays[3].shape[1] // HEAD_DIM)
            else per_device_gathered
        )
        return jax.shard_map(
            chosen, mesh=mesh, in_specs=specs, out_specs=P("seq", "tensor"), check_vma=False
        )(*arrays)

    return whole
```

```python
import functools
import math

import jax
import jax.numpy as jnp
from jax import lax
from jax.experimental import pallas as pl
from jax.experimental.pallas import tpu as pltpu
from jax.sharding import PartitionSpec as P

HEAD_DIM = 128
PATCH_DEV = 128


score_cap = 30.0
norm_eps = 1e-05


def shifted(block, axis, distance):
    devices = range(lax.axis_size(axis))
    route = [(i - distance, i) for i in devices if i - distance in devices]
    return lax.ppermute(block, axis, route)


def capped_exp(scores):
    return jnp.exp(score_cap * jnp.tanh(scores / score_cap))


def contract_rows(left, right):
    return lax.dot_general(
        left,
        right,
        (((0,), (0,)), ((), ())),
        precision=lax.Precision.HIGHEST,
        preferred_element_type=jnp.float32,
    )


def per_device_gathered(
    byte_states,
    byte_patch,
    patch_len,
    cross_query,
    cross_key,
    cross_value,
    cross_out,
    norm_gain,
    latent_query,
    latent_key,
    latent_value,
    latent_out,
):
    seq_index = lax.axis_index("seq")
    tensor_count = lax.axis_size("tensor")
    (
        cross_query,
        cross_key,
        cross_value,
        latent_query,
        latent_key,
        latent_value,
        cross_out,
        latent_out,
    ) = (
        lax.all_gather(cross_query, "seq", axis=0, tiled=True),
        lax.all_gather(cross_key, "seq", axis=0, tiled=True),
        lax.all_gather(cross_value, "seq", axis=0, tiled=True),
        lax.all_gather(latent_query, "seq", axis=0, tiled=True),
        lax.all_gather(latent_key, "seq", axis=0, tiled=True),
        lax.all_gather(latent_value, "seq", axis=0, tiled=True),
        lax.all_gather(cross_out, "seq", axis=1, tiled=True),
        lax.all_gather(latent_out, "seq", axis=1, tiled=True),
    )
    latent_width = cross_out.shape[1]
    local_width = cross_out.shape[0]
    head_count = local_width // HEAD_DIM
    slot_count = 2 * PATCH_DEV
    byte_count = byte_states.shape[0]
    first_patch = byte_patch[0]
    slot_of = byte_patch - first_patch
    onehot_mask = slot_of[:, None] == jnp.arange(slot_count, dtype=jnp.int32)[None, :]
    onehot = onehot_mask.astype(jnp.bfloat16)
    onehot_float = onehot_mask.astype(jnp.float32)
    byte_sums = lax.dot_general(
        onehot, byte_states, (((0,), (0,)), ((), ())), preferred_element_type=jnp.float32
    )
    lengths_all = jnp.concatenate([patch_len, jnp.ones((slot_count,), jnp.int32)])
    lengths = lax.dynamic_slice_in_dim(lengths_all, first_patch, slot_count)
    pooled = (byte_sums / lengths.astype(jnp.float32)[:, None]).astype(jnp.bfloat16)
    query_slots = jnp.dot(pooled, cross_query, preferred_element_type=jnp.float32).astype(
        jnp.bfloat16
    )
    byte_keys = jnp.dot(byte_states, cross_key, preferred_element_type=jnp.float32).astype(
        jnp.bfloat16
    )
    byte_values = jnp.dot(byte_states, cross_value, preferred_element_type=jnp.float32).astype(
        jnp.bfloat16
    )
    query_bytes = jnp.dot(onehot, query_slots, preferred_element_type=jnp.float32)
    scores = (query_bytes * byte_keys.astype(jnp.float32)).reshape(
        byte_count, head_count, HEAD_DIM
    ).sum(axis=2) / math.sqrt(HEAD_DIM)
    byte_raw = capped_exp(scores)
    totals = contract_rows(onehot_float, byte_raw)
    totals = jnp.where(totals > 0.0, totals, 1.0)
    totals_bytes = jnp.dot(
        onehot_float, totals, precision=lax.Precision.HIGHEST, preferred_element_type=jnp.float32
    )
    byte_weight = (byte_raw / totals_bytes).astype(jnp.bfloat16)
    weighted = (
        byte_weight.astype(jnp.float32)[:, :, None]
        * byte_values.astype(jnp.float32).reshape(byte_count, head_count, HEAD_DIM)
    ).reshape(byte_count, local_width)
    cross_heads = contract_rows(onehot_float, weighted).astype(jnp.bfloat16)
    padding = jnp.zeros((2 * PATCH_DEV, cross_heads.shape[1]), cross_heads.dtype)
    padded = jnp.concatenate([padding, cross_heads, padding], axis=0)
    offset = seq_index * PATCH_DEV - first_patch + 2 * PATCH_DEV
    padded, offset = (padded, offset)
    owned_heads = lax.dynamic_slice_in_dim(padded, offset, PATCH_DEV, 0)
    for offset_step in (-1, 1):
        window = lax.dynamic_slice_in_dim(padded, offset + offset_step * PATCH_DEV, PATCH_DEV, 0)
        owned_heads = owned_heads + shifted(window, "seq", offset_step)
    partial_value = jnp.dot(owned_heads, cross_out, preferred_element_type=jnp.float32)
    latent_in = lax.psum(partial_value, "tensor").astype(jnp.bfloat16)
    hidden = latent_in.astype(jnp.float32)
    mean_square = jnp.mean(hidden * hidden, axis=1, keepdims=True)
    normed = (hidden * lax.rsqrt(mean_square + norm_eps) * norm_gain[None, :]).astype(jnp.bfloat16)
    query = (
        jnp.dot(normed, latent_query, preferred_element_type=jnp.float32)
        .astype(jnp.bfloat16)
        .reshape(PATCH_DEV, head_count, HEAD_DIM)
    )
    key_rows = jnp.dot(normed, latent_key, preferred_element_type=jnp.float32).astype(jnp.bfloat16)
    value_rows = jnp.dot(normed, latent_value, preferred_element_type=jnp.float32).astype(
        jnp.bfloat16
    )
    positions = seq_index * PATCH_DEV + jnp.arange(PATCH_DEV, dtype=jnp.int32)
    key_piece = lax.all_gather(key_rows, "seq", axis=0, tiled=True)
    value_piece = lax.all_gather(value_rows, "seq", axis=0, tiled=True)
    piece_rows = key_piece.shape[0]
    key_piece = key_piece.reshape(piece_rows, head_count, HEAD_DIM)
    value_piece = value_piece.reshape(piece_rows, head_count, HEAD_DIM)
    piece_scores = jnp.einsum(
        "qhd,khd->hqk", query, key_piece, preferred_element_type=jnp.float32
    ) / math.sqrt(HEAD_DIM)
    key_positions = jnp.arange(piece_rows, dtype=jnp.int32)
    allowed = key_positions[None, :] <= positions[:, None]
    exp_scores = jnp.where(allowed[None, :, :], capped_exp(piece_scores), 0.0)
    denominator = jnp.sum(exp_scores, axis=2)
    numerator = jnp.einsum(
        "hqk,khd->hqd",
        exp_scores.astype(jnp.bfloat16),
        value_piece,
        preferred_element_type=jnp.float32,
    )
    numerator, denominator = (numerator, denominator)
    attended = (numerator / denominator[:, :, None]).astype(jnp.bfloat16)
    attended = attended.transpose(1, 0, 2).reshape(PATCH_DEV, local_width)
    projected = jnp.dot(attended, latent_out, preferred_element_type=jnp.float32)
    mixed_sum = lax.psum_scatter(projected, "tensor", scatter_dimension=1, tiled=True)
    column_width = latent_width // tensor_count
    residual = lax.dynamic_slice_in_dim(
        hidden, lax.axis_index("tensor") * column_width, column_width, 1
    )
    return (residual + mixed_sum).astype(jnp.bfloat16)


def dot(left, right):
    return jnp.dot(left, right, preferred_element_type=jnp.float32)


def exchanged(block, axis, distance):
    route = [(i, i ^ distance) for i in range(lax.axis_size(axis))]
    return lax.ppermute(block, axis, route)


def core_swapped(block):
    return exchanged(block, "seq", 1)


def after(value, *earlier):
    return lax.optimization_barrier((value, *earlier))[0]


def place():
    seq = lax.axis_index("seq")
    return seq // 2, lax.rem(seq, 2), lax.axis_index("tensor")


def aligned(index, size):
    return pl.ds(pl.multiple_of(index * size, size), size)


def fetched(pairs, semaphores):
    copies = [
        pltpu.make_async_copy(source, target, semaphores.at[n])
        for n, (source, target) in enumerate(pairs)
    ]
    for copy in copies:
        copy.start()
    return copies


def call(kernel, outs, *operands, far=0, scratch=(), flops=0):
    shapes = [jax.ShapeDtypeStruct(shape, dtype) for shape, dtype in outs]
    moved = sum(o.size * o.dtype.itemsize for o in [*operands, *shapes])
    return pl.pallas_call(
        kernel,
        out_shape=shapes,
        in_specs=[pl.BlockSpec(memory_space=pltpu.VMEM)] * (len(operands) - far)
        + [pl.BlockSpec(memory_space=pl.ANY)] * far,
        out_specs=[pl.BlockSpec(memory_space=pltpu.VMEM)] * len(outs),
        scratch_shapes=list(scratch),
        compiler_params=pltpu.CompilerParams(vmem_limit_bytes=28 * 1024 * 1024),
        cost_estimate=pl.CostEstimate(flops=flops, bytes_accessed=moved, transcendentals=0),
    )(*operands)


def assemble(pieces, whole):
    chip, core, _ = place()
    for n, piece in enumerate(pieces):
        index = 2 * (chip ^ (n // 2)) + (core ^ (n % 2))
        whole[aligned(index, piece.shape[0]), :] = piece[...]


def stack_kernel(*refs):
    sources, stacked, semaphores = refs[:-2], refs[-2], refs[-1]
    height = sources[0].shape[0]
    copies = fetched(
        [(s, stacked.at[n * height : (n + 1) * height, :]) for n, s in enumerate(sources)],
        semaphores,
    )
    for copy in copies:
        copy.wait()


def plane_rows(pieces, whole, part=0):
    chip, core, _ = place()
    height = whole.shape[0] // len(pieces)
    return [
        (
            piece.at[part * height : (part + 1) * height, :],
            whole.at[aligned(2 * (chip ^ (n // 2)) + (core ^ (n % 2)), height), :],
        )
        for n, piece in enumerate(pieces)
    ]


def query_kernel(count, slot_row, lengths, states, *refs):
    pieces, (query, held, whole, semaphores) = refs[:count], refs[count:]
    slots, byte_count = query.shape[0], states.shape[0]
    copies = fetched([(states, held), *plane_rows(pieces, whole)], semaphores)
    index = lax.broadcasted_iota(jnp.int32, (slots, byte_count), 0)
    onehot = (index == slot_row[...]).astype(jnp.bfloat16)
    copies[0].wait()
    pooled = (dot(onehot, held[...]) / lengths[...]).astype(jnp.bfloat16)
    for copy in copies[1:]:
        copy.wait()
    query[...] = dot(pooled, whole[...]).astype(jnp.bfloat16)


def cross_kernel(count, tile, slot_row, query, states, *refs):
    pieces, (own, above, below, *scratch) = refs[:count], refs[count:]
    held, key_weight, value_weight, totals, summed, semaphores = scratch
    slots, width = query.shape
    spill = above.shape[0]
    head_count = width // HEAD_DIM
    pairs = [(states, held)]
    for part, weight in enumerate((key_weight, value_weight)):
        pairs += plane_rows(pieces, weight, part)
    copies = fetched(pairs, semaphores)
    totals[...] = jnp.zeros_like(totals)
    summed[...] = jnp.zeros_like(summed)
    for copy in copies:
        copy.wait()

    @pl.loop(0, states.shape[0] // tile)
    def _(step):
        span = aligned(step, tile)
        block = held[span, :]
        keys = dot(block, key_weight[...]).astype(jnp.bfloat16).astype(jnp.float32)
        index = lax.broadcasted_iota(jnp.int32, (slots, tile), 0)
        onehot = (index == slot_row[:, span]).astype(jnp.bfloat16)
        product = keys * lax.dot_general(
            onehot, query[...], (((0,), (0,)), ((), ())), preferred_element_type=jnp.float32
        )
        lane = lax.broadcasted_iota(jnp.int32, (tile, HEAD_DIM), 1)
        scores = jnp.zeros((tile, HEAD_DIM), jnp.float32)
        for head in range(head_count):
            total = jnp.sum(
                product[:, head * HEAD_DIM : (head + 1) * HEAD_DIM], axis=1, keepdims=True
            )
            scores = jnp.where(lane == head, total, scores)
        raw = capped_exp(scores / math.sqrt(HEAD_DIM))
        high = raw.astype(jnp.bfloat16)
        low = (raw - high.astype(jnp.float32)).astype(jnp.bfloat16)
        totals[...] += dot(onehot, high) + dot(onehot, low)
        values = dot(block, value_weight[...]).astype(jnp.bfloat16).astype(jnp.float32)
        weighted = jnp.concatenate(
            [
                (values[:, h * HEAD_DIM : (h + 1) * HEAD_DIM] * raw[:, h : h + 1]).astype(
                    jnp.bfloat16
                )
                for h in range(head_count)
            ],
            axis=1,
        )
        summed[...] += dot(onehot, weighted)

    total = totals[...]
    inverse = 1.0 / jnp.where(total > 0.0, total, 1.0)
    for h in range(head_count):
        part = slice(h * HEAD_DIM, (h + 1) * HEAD_DIM)
        heads = (summed[:, part] * inverse[:, h : h + 1]).astype(jnp.bfloat16)
        above[:, part] = heads[:spill]
        own[:, part] = heads[spill : slots - spill]
        below[:, part] = heads[slots - spill :]


def quarters(left, weight, outs):
    _, _, tensor = place()
    height = outs[0].shape[0]
    for r, out in enumerate(outs):
        block = left[aligned(tensor ^ r, height), :]
        out[...] = dot(block, weight[...]).astype(out.dtype)


def cross_out_kernel(count, weight, *refs):
    pieces, outs, whole = refs[:count], refs[count:-1], refs[-1]
    assemble(pieces, whole)
    quarters(whole, weight, outs)


def latent_out_kernel(count, parts, weight, *refs):
    pieces, blocks, refs = refs[:count], refs[count : count + parts], refs[count + parts :]
    outs, (whole, hidden) = refs[:-2], refs[-2:]
    chip, core, tensor = place()
    for n, piece in enumerate(pieces):
        index = (count // 2) * (core ^ (n % 2)) + (chip ^ (n // 2))
        whole[:, aligned(index, HEAD_DIM)] = piece[...]
    height = outs[0].shape[0]
    for r, block in enumerate(blocks):
        hidden[aligned(tensor ^ r, height), :] = block[...]
    share = (tensor == chip).astype(jnp.float32)
    for d, out in reversed(list(enumerate(outs))):
        span = aligned(chip ^ d, height)
        product = dot(whole[span, :], weight[...])
        out[...] = (product + hidden[span, :].astype(jnp.float32) * share).astype(out.dtype)


def column_kernel(*refs):
    blocks, outs, whole = refs[: (len(refs) - 1) // 2], refs[(len(refs) - 1) // 2 : -1], refs[-1]
    chip, _, tensor = place()
    height = blocks[0].shape[0]
    for d, block in enumerate(blocks):
        whole[aligned(chip ^ d, height), :] = block[...].astype(jnp.float32)
    for r, out in enumerate(outs):
        out[...] = whole[aligned(tensor ^ r, height), :].astype(out.dtype)


def arrange_kernel(*refs):
    weights, outs, semaphores = refs[:6], refs[6:-1], refs[-1]
    chip, core, _ = place()
    height = weights[0].shape[0]
    copies = fetched(
        [
            (
                weights[2 * m + n].at[:, aligned(len(outs) * core + (chip ^ d), HEAD_DIM)],
                out.at[n * height : (n + 1) * height, m * HEAD_DIM : (m + 1) * HEAD_DIM],
            )
            for d, out in enumerate(outs)
            for m in range(3)
            for n in range(2)
        ],
        semaphores,
    )
    for copy in copies:
        copy.wait()


def diagonal(size):
    return lax.broadcasted_iota(jnp.int32, (size, size), 0) == lax.broadcasted_iota(
        jnp.int32, (size, size), 1
    )


def project_kernel(count, gain, *refs):
    blocks, refs = refs[: 2 * count], refs[2 * count :]
    chips = (len(refs) - 1) // 2
    weights, outs, left = refs[:chips], refs[chips:-1], refs[-1]
    seq = lax.axis_index("seq")
    part, width = blocks[0].shape
    height = count * part
    totals = []
    for q in range(count):
        total = jnp.zeros((part, 1), jnp.float32)
        for n, block in enumerate(blocks[2 * q : 2 * q + 2]):
            hidden = block[...].astype(jnp.float32)
            total += jnp.sum(hidden * hidden, axis=1, keepdims=True)
            left[q * part : (q + 1) * part, n * width : (n + 1) * width] = (
                hidden * gain[:, aligned(seq ^ n, width)]
            ).astype(jnp.bfloat16)
        totals.append(jnp.sum(jnp.where(diagonal(part), total, 0.0), axis=0, keepdims=True))
    for weight, out in reversed(list(zip(weights, outs))):
        out[:height, :] = dot(left[...], weight[...]).astype(out.dtype)
    outs[0][height:, :] = jnp.zeros((outs[0].shape[0] - height, outs[0].shape[1]), jnp.float32)
    for out in outs[1:]:
        out[height:, :] = jnp.zeros((out.shape[0] - height, out.shape[1]), jnp.bfloat16)
    index = lax.broadcasted_iota(jnp.int32, (16, part), 0)
    own_sums, sent_sums = jnp.zeros((8, part), jnp.float32), jnp.zeros((16, part), jnp.float32)
    for q, row in enumerate(totals):
        high = row.astype(jnp.bfloat16).astype(jnp.float32)
        middle = (row - high).astype(jnp.bfloat16).astype(jnp.float32)
        own_sums = jnp.where(index[:8] == q, row, own_sums)
        for m, term in enumerate((high, middle, row - high - middle)):
            sent_sums = jnp.where(index == 3 * q + m, term, sent_sums)
    outs[0][height:, :part] = own_sums
    for out in outs[1:]:
        out[height:, :part] = sent_sums.astype(jnp.bfloat16)


def attention_kernel(groups, chips, depth, *refs):
    shares, attended, (query, key, value) = refs[: len(groups) * chips], refs[-4], refs[-3:]
    _, _, tensor = place()
    parts = sum(len(group) for group in groups)
    height = attended.shape[0] // parts
    own_place = diagonal(height)
    for g, group in enumerate(groups):
        end = len(group) * height
        own, *received = shares[g * chips : (g + 1) * chips]
        for q, r in enumerate(group):
            rows = slice(q * height, (q + 1) * height)
            total = own[rows, :]
            row = own[end:, :height][q : q + 1]
            for share in received:
                total += share[rows, :].astype(jnp.float32)
                terms = share[end:, :height].astype(jnp.float32)
                row += sum(terms[3 * q + m : 3 * q + m + 1] for m in range(3))
            column = jnp.sum(jnp.where(own_place, row, 0.0), axis=1, keepdims=True)
            total = (total * lax.rsqrt(column / depth + norm_eps)).astype(jnp.bfloat16)
            span = aligned(tensor ^ r, height)
            for m, kept in enumerate((query, key, value)):
                kept[span, :] = total[:, m * HEAD_DIM : (m + 1) * HEAD_DIM]
    causal = lax.broadcasted_iota(jnp.int32, (height, height), 0) >= lax.broadcasted_iota(
        jnp.int32, (height, height), 1
    )
    for i in range(parts):
        block = query[i * height : (i + 1) * height, :]
        numerator = jnp.zeros((height, HEAD_DIM), jnp.float32)
        denominator = jnp.zeros((height, 1), jnp.float32)
        for j in range(i + 1):
            span = slice(j * height, (j + 1) * height)
            scores = lax.dot_general(
                block, key[span, :], (((1,), (1,)), ((), ())), preferred_element_type=jnp.float32
            )
            raw = capped_exp(scores / math.sqrt(HEAD_DIM))
            if i == j:
                raw = jnp.where(causal, raw, 0.0)
            denominator += jnp.sum(raw, axis=1, keepdims=True)
            numerator += dot(raw.astype(jnp.bfloat16), value[span, :])
        attended[i * height : (i + 1) * height, :] = (numerator / denominator).astype(jnp.bfloat16)


def final_kernel(own, *refs):
    received, outs, whole = refs[:-3], refs[-3:-1], refs[-1]
    _, core, _ = place()
    total = own[...]
    for block in received:
        total += block[...].astype(jnp.float32)
    whole[...] = total
    height = outs[0].shape[0]
    for flip, out in enumerate(outs):
        out[...] = whole[aligned(core ^ flip, height), :].astype(jnp.bfloat16)


def per_device(
    byte_states,
    byte_patch,
    patch_len,
    cross_query,
    cross_key,
    cross_value,
    cross_out,
    norm_gain,
    latent_query,
    latent_key,
    latent_value,
    latent_out,
):
    seq = lax.axis_index("seq")
    core = lax.rem(seq, 2)
    seq_count = lax.axis_size("seq")
    tensor_count = lax.axis_size("tensor")
    chip_count = seq_count // 2
    patch_count = patch_len.shape[0]
    patch_dev = patch_count // seq_count
    spill = patch_dev // 2
    slot_count = patch_dev + 2 * spill
    byte_count, byte_width = byte_states.shape
    local_width = cross_query.shape[1]
    out_width = cross_out.shape[1]
    quarter = patch_count // tensor_count
    bf16, f32 = jnp.bfloat16, jnp.float32
    tile = min(256, byte_count)

    def over_plane(block, earlier=()):
        pieces = []
        for d in range(chip_count):
            moved = exchanged(block, "seq", 2 * d) if d else block
            pieces += [moved, core_swapped(after(moved, *earlier) if d else moved)]
        return pieces

    slot_of = byte_patch - (seq * patch_dev - spill)
    slot_row = slot_of[None, :]
    edge = jnp.ones((spill,), jnp.int32)
    lengths = lax.dynamic_slice_in_dim(
        jnp.concatenate([edge, patch_len, edge]), seq * patch_dev, slot_count
    ).astype(f32)[:, None]
    query_pieces = over_plane(cross_query)
    (stacked,) = call(
        stack_kernel,
        [((2 * cross_key.shape[0], local_width), bf16)],
        cross_key,
        cross_value,
        far=2,
        scratch=[pltpu.SemaphoreType.DMA((2,))],
    )
    (query_slots,) = call(
        functools.partial(query_kernel, seq_count),
        [((slot_count, local_width), bf16)],
        slot_row,
        lengths,
        byte_states,
        *query_pieces,
        far=1 + seq_count,
        scratch=[
            pltpu.VMEM((byte_count, byte_width), bf16),
            pltpu.VMEM((byte_width, local_width), bf16),
            pltpu.SemaphoreType.DMA((1 + seq_count,)),
        ],
        flops=2 * slot_count * byte_width * (byte_count + local_width),
    )
    own, above, below = call(
        functools.partial(cross_kernel, seq_count, tile),
        [((height, local_width), bf16) for height in (patch_dev, spill, spill)],
        slot_row,
        query_slots,
        byte_states,
        *over_plane(stacked, (query_slots,)),
        far=1 + seq_count,
        scratch=[
            pltpu.VMEM((byte_count, byte_width), bf16),
            pltpu.VMEM((byte_width, local_width), bf16),
            pltpu.VMEM((byte_width, local_width), bf16),
            pltpu.VMEM((slot_count, HEAD_DIM), f32),
            pltpu.VMEM((slot_count, local_width), f32),
            pltpu.SemaphoreType.DMA((1 + 2 * seq_count,)),
        ],
        flops=4 * byte_count * local_width * (byte_width + slot_count),
    )

    spilled = [shifted(below, "seq", 1), shifted(above, "seq", -1)]
    own = own + jnp.concatenate(spilled, axis=0)

    total, *sent = call(
        functools.partial(cross_out_kernel, seq_count),
        [((quarter, out_width), f32 if r == 0 else bf16) for r in range(tensor_count)],
        cross_out,
        *over_plane(own),
        scratch=[pltpu.VMEM((patch_count, local_width), bf16)],
        flops=2 * patch_count * local_width * out_width,
    )
    received = [exchanged(block, "tensor", r) for r, block in enumerate(sent, 1)]

    weights = []
    for weight in (latent_query, latent_key, latent_value):
        weights += [weight, core_swapped(after(weight, total))]
    head_weights = call(
        arrange_kernel,
        [((2 * out_width, 3 * HEAD_DIM), bf16)] * chip_count,
        *weights,
        far=6,
        scratch=[pltpu.SemaphoreType.DMA((6 * chip_count,))],
    )
    total, *head_weights = lax.optimization_barrier((total, *head_weights))
    for share in received:
        total = total + share.astype(f32)
    latent_in = total.astype(bf16)

    gain = norm_gain[None, :]
    groups = [[0], list(range(1, min(3, tensor_count))), list(range(3, tensor_count))]
    groups = [group for group in groups if group]
    shares, arrived, latent_blocks = [], [], [latent_in]
    for g, group in enumerate(groups):
        blocks = [latent_in]
        if g:
            start = after(latent_in, *arrived, *shares[:chip_count]) if g > 1 else latent_in
            arrived = [exchanged(start, "tensor", r) for r in group]
            latent_blocks += arrived
            blocks = [after(block, *shares[:chip_count]) for block in arrived]
        height = len(group) * quarter
        share, *sent = call(
            functools.partial(project_kernel, len(group)),
            [((height + 8, 3 * HEAD_DIM), f32)]
            + [((height + 16, 3 * HEAD_DIM), bf16)] * (chip_count - 1),
            gain,
            *[piece for block in blocks for piece in (block, core_swapped(block))],
            *head_weights,
            scratch=[pltpu.VMEM((height, 2 * out_width), bf16)],
            flops=2 * height * 2 * out_width * 3 * HEAD_DIM * chip_count,
        )
        if g > 1:
            sent = [after(part, *shares[(g - 1) * chip_count + 1 :]) for part in sent]
        shares += [share] + [exchanged(part, "seq", 2 * d) for d, part in enumerate(sent, 1)]
    (attended,) = call(
        functools.partial(attention_kernel, groups, chip_count, out_width * seq_count),
        [((patch_count, HEAD_DIM), bf16)],
        *shares,
        scratch=[pltpu.VMEM((patch_count, HEAD_DIM), bf16)] * 3,
        flops=2 * patch_count * patch_count * HEAD_DIM,
    )

    own, *sent = call(
        functools.partial(latent_out_kernel, seq_count, tensor_count),
        [((quarter, out_width), bf16 if d else f32) for d in range(chip_count)],
        latent_out,
        *over_plane(attended),
        *latent_blocks,
        scratch=[
            pltpu.VMEM((patch_count, local_width), bf16),
            pltpu.VMEM((patch_count, out_width), bf16),
        ],
        flops=2 * patch_count * local_width * out_width,
    )

    total, *sent = call(
        column_kernel,
        [((quarter, out_width), bf16 if r else f32) for r in range(tensor_count)],
        own,
        *[exchanged(block, "seq", 2 * d) for d, block in enumerate(sent, 1)],
        scratch=[pltpu.VMEM((patch_count, out_width), f32)],
    )
    same, crossed = call(
        final_kernel,
        [((patch_dev, out_width), bf16)] * 2,
        total,
        *[exchanged(block, "tensor", r) for r, block in enumerate(sent, 1)],
        scratch=[pltpu.VMEM((quarter, out_width), f32)],
    )
    crossed = core_swapped(crossed)
    return jnp.concatenate(
        [jnp.where(core == 0, same, crossed), jnp.where(core == 0, crossed, same)], axis=1
    )


def head_per_device(mesh, heads):
    seq_count, tensor_count = mesh.shape["seq"], mesh.shape["tensor"]
    return (
        heads == seq_count * tensor_count
        and seq_count == 2 * tensor_count
        and tensor_count & (tensor_count - 1) == 0
    )


def solution(mesh):
    specs = (
        P("seq", None),
        P("seq"),
        P(),
        P("seq", "tensor"),
        P("seq", "tensor"),
        P("seq", "tensor"),
        P("tensor", "seq"),
        P(),
        P("seq", "tensor"),
        P("seq", "tensor"),
        P("seq", "tensor"),
        P("tensor", "seq"),
    )

    def whole(*arrays):
        chosen = (
            per_device
            if head_per_device(mesh, arrays[3].shape[1] // HEAD_DIM)
            else per_device_gathered
        )
        return jax.shard_map(
            chosen, mesh=mesh, in_specs=specs, out_specs=P("seq", "tensor"), check_vma=False
        )(*arrays)

    return whole
```

```python
import functools
import math

import jax
import jax.numpy as jnp
from jax import lax
from jax.experimental import pallas as pl
from jax.experimental.pallas import tpu as pltpu
from jax.sharding import PartitionSpec as P

HEAD_DIM = 128
PATCH_DEV = 128


score_cap = 30.0
norm_eps = 1e-05


def shifted(block, axis, distance):
    devices = range(lax.axis_size(axis))
    route = [(i - distance, i) for i in devices if i - distance in devices]
    return lax.ppermute(block, axis, route)


def capped_exp(scores):
    return jnp.exp(score_cap * jnp.tanh(scores / score_cap))


def contract_rows(left, right):
    return lax.dot_general(
        left,
        right,
        (((0,), (0,)), ((), ())),
        precision=lax.Precision.HIGHEST,
        preferred_element_type=jnp.float32,
    )


def per_device_gathered(
    byte_states,
    byte_patch,
    patch_len,
    cross_query,
    cross_key,
    cross_value,
    cross_out,
    norm_gain,
    latent_query,
    latent_key,
    latent_value,
    latent_out,
):
    seq_index = lax.axis_index("seq")
    tensor_count = lax.axis_size("tensor")
    (
        cross_query,
        cross_key,
        cross_value,
        latent_query,
        latent_key,
        latent_value,
        cross_out,
        latent_out,
    ) = (
        lax.all_gather(cross_query, "seq", axis=0, tiled=True),
        lax.all_gather(cross_key, "seq", axis=0, tiled=True),
        lax.all_gather(cross_value, "seq", axis=0, tiled=True),
        lax.all_gather(latent_query, "seq", axis=0, tiled=True),
        lax.all_gather(latent_key, "seq", axis=0, tiled=True),
        lax.all_gather(latent_value, "seq", axis=0, tiled=True),
        lax.all_gather(cross_out, "seq", axis=1, tiled=True),
        lax.all_gather(latent_out, "seq", axis=1, tiled=True),
    )
    latent_width = cross_out.shape[1]
    local_width = cross_out.shape[0]
    head_count = local_width // HEAD_DIM
    slot_count = 2 * PATCH_DEV
    byte_count = byte_states.shape[0]
    first_patch = byte_patch[0]
    slot_of = byte_patch - first_patch
    onehot_mask = slot_of[:, None] == jnp.arange(slot_count, dtype=jnp.int32)[None, :]
    onehot = onehot_mask.astype(jnp.bfloat16)
    onehot_float = onehot_mask.astype(jnp.float32)
    byte_sums = lax.dot_general(
        onehot, byte_states, (((0,), (0,)), ((), ())), preferred_element_type=jnp.float32
    )
    lengths_all = jnp.concatenate([patch_len, jnp.ones((slot_count,), jnp.int32)])
    lengths = lax.dynamic_slice_in_dim(lengths_all, first_patch, slot_count)
    pooled = (byte_sums / lengths.astype(jnp.float32)[:, None]).astype(jnp.bfloat16)
    query_slots = jnp.dot(pooled, cross_query, preferred_element_type=jnp.float32).astype(
        jnp.bfloat16
    )
    byte_keys = jnp.dot(byte_states, cross_key, preferred_element_type=jnp.float32).astype(
        jnp.bfloat16
    )
    byte_values = jnp.dot(byte_states, cross_value, preferred_element_type=jnp.float32).astype(
        jnp.bfloat16
    )
    query_bytes = jnp.dot(onehot, query_slots, preferred_element_type=jnp.float32)
    scores = (query_bytes * byte_keys.astype(jnp.float32)).reshape(
        byte_count, head_count, HEAD_DIM
    ).sum(axis=2) / math.sqrt(HEAD_DIM)
    byte_raw = capped_exp(scores)
    totals = contract_rows(onehot_float, byte_raw)
    totals = jnp.where(totals > 0.0, totals, 1.0)
    totals_bytes = jnp.dot(
        onehot_float, totals, precision=lax.Precision.HIGHEST, preferred_element_type=jnp.float32
    )
    byte_weight = (byte_raw / totals_bytes).astype(jnp.bfloat16)
    weighted = (
        byte_weight.astype(jnp.float32)[:, :, None]
        * byte_values.astype(jnp.float32).reshape(byte_count, head_count, HEAD_DIM)
    ).reshape(byte_count, local_width)
    cross_heads = contract_rows(onehot_float, weighted).astype(jnp.bfloat16)
    padding = jnp.zeros((2 * PATCH_DEV, cross_heads.shape[1]), cross_heads.dtype)
    padded = jnp.concatenate([padding, cross_heads, padding], axis=0)
    offset = seq_index * PATCH_DEV - first_patch + 2 * PATCH_DEV
    padded, offset = (padded, offset)
    owned_heads = lax.dynamic_slice_in_dim(padded, offset, PATCH_DEV, 0)
    for offset_step in (-1, 1):
        window = lax.dynamic_slice_in_dim(padded, offset + offset_step * PATCH_DEV, PATCH_DEV, 0)
        owned_heads = owned_heads + shifted(window, "seq", offset_step)
    partial_value = jnp.dot(owned_heads, cross_out, preferred_element_type=jnp.float32)
    latent_in = lax.psum(partial_value, "tensor").astype(jnp.bfloat16)
    hidden = latent_in.astype(jnp.float32)
    mean_square = jnp.mean(hidden * hidden, axis=1, keepdims=True)
    normed = (hidden * lax.rsqrt(mean_square + norm_eps) * norm_gain[None, :]).astype(jnp.bfloat16)
    query = (
        jnp.dot(normed, latent_query, preferred_element_type=jnp.float32)
        .astype(jnp.bfloat16)
        .reshape(PATCH_DEV, head_count, HEAD_DIM)
    )
    key_rows = jnp.dot(normed, latent_key, preferred_element_type=jnp.float32).astype(jnp.bfloat16)
    value_rows = jnp.dot(normed, latent_value, preferred_element_type=jnp.float32).astype(
        jnp.bfloat16
    )
    positions = seq_index * PATCH_DEV + jnp.arange(PATCH_DEV, dtype=jnp.int32)
    key_piece = lax.all_gather(key_rows, "seq", axis=0, tiled=True)
    value_piece = lax.all_gather(value_rows, "seq", axis=0, tiled=True)
    piece_rows = key_piece.shape[0]
    key_piece = key_piece.reshape(piece_rows, head_count, HEAD_DIM)
    value_piece = value_piece.reshape(piece_rows, head_count, HEAD_DIM)
    piece_scores = jnp.einsum(
        "qhd,khd->hqk", query, key_piece, preferred_element_type=jnp.float32
    ) / math.sqrt(HEAD_DIM)
    key_positions = jnp.arange(piece_rows, dtype=jnp.int32)
    allowed = key_positions[None, :] <= positions[:, None]
    exp_scores = jnp.where(allowed[None, :, :], capped_exp(piece_scores), 0.0)
    denominator = jnp.sum(exp_scores, axis=2)
    numerator = jnp.einsum(
        "hqk,khd->hqd",
        exp_scores.astype(jnp.bfloat16),
        value_piece,
        preferred_element_type=jnp.float32,
    )
    numerator, denominator = (numerator, denominator)
    attended = (numerator / denominator[:, :, None]).astype(jnp.bfloat16)
    attended = attended.transpose(1, 0, 2).reshape(PATCH_DEV, local_width)
    projected = jnp.dot(attended, latent_out, preferred_element_type=jnp.float32)
    mixed_sum = lax.psum_scatter(projected, "tensor", scatter_dimension=1, tiled=True)
    column_width = latent_width // tensor_count
    residual = lax.dynamic_slice_in_dim(
        hidden, lax.axis_index("tensor") * column_width, column_width, 1
    )
    return (residual + mixed_sum).astype(jnp.bfloat16)


def dot(left, right):
    return jnp.dot(left, right, preferred_element_type=jnp.float32)


def exchanged(block, axis, distance):
    route = [(i, i ^ distance) for i in range(lax.axis_size(axis))]
    return lax.ppermute(block, axis, route)


def core_swapped(block):
    return exchanged(block, "seq", 1)


def after(value, *earlier):
    return lax.optimization_barrier((value, *earlier))[0]


def place():
    seq = lax.axis_index("seq")
    return seq // 2, lax.rem(seq, 2), lax.axis_index("tensor")


def aligned(index, size):
    return pl.ds(pl.multiple_of(index * size, size), size)


def fetched(pairs, semaphores):
    copies = [
        pltpu.make_async_copy(source, target, semaphores.at[n])
        for n, (source, target) in enumerate(pairs)
    ]
    for copy in copies:
        copy.start()
    return copies


def call(kernel, outs, *operands, far=0, scratch=(), flops=0):
    shapes = [jax.ShapeDtypeStruct(shape, dtype) for shape, dtype in outs]
    moved = sum(o.size * o.dtype.itemsize for o in [*operands, *shapes])
    return pl.pallas_call(
        kernel,
        out_shape=shapes,
        in_specs=[pl.BlockSpec(memory_space=pltpu.VMEM)] * (len(operands) - far)
        + [pl.BlockSpec(memory_space=pl.ANY)] * far,
        out_specs=[pl.BlockSpec(memory_space=pltpu.VMEM)] * len(outs),
        scratch_shapes=list(scratch),
        compiler_params=pltpu.CompilerParams(vmem_limit_bytes=28 * 1024 * 1024),
        cost_estimate=pl.CostEstimate(flops=flops, bytes_accessed=moved, transcendentals=0),
    )(*operands)


def assemble(pieces, whole):
    chip, core, _ = place()
    for n, piece in enumerate(pieces):
        index = 2 * (chip ^ (n // 2)) + (core ^ (n % 2))
        whole[aligned(index, piece.shape[0]), :] = piece[...]


def plane_rows(pieces, whole):
    chip, core, _ = place()
    return [
        (piece, whole.at[aligned(2 * (chip ^ (n // 2)) + (core ^ (n % 2)), piece.shape[0]), :])
        for n, piece in enumerate(pieces)
    ]


def query_kernel(count, slot_row, lengths, states, *refs):
    pieces, (query, held, whole, semaphores) = refs[:count], refs[count:]
    slots, byte_count = query.shape[0], states.shape[0]
    copies = fetched([(states, held), *plane_rows(pieces, whole)], semaphores)
    index = lax.broadcasted_iota(jnp.int32, (slots, byte_count), 0)
    onehot = (index == slot_row[...]).astype(jnp.bfloat16)
    copies[0].wait()
    pooled = (dot(onehot, held[...]) / lengths[...]).astype(jnp.bfloat16)
    for copy in copies[1:]:
        copy.wait()
    query[...] = dot(pooled, whole[...]).astype(jnp.bfloat16)


def cross_kernel(count, tile, slot_row, query, states, *refs):
    pieces, (own, above, below, *scratch) = refs[: 2 * count], refs[2 * count :]
    held, key_weight, value_weight, totals, summed, semaphores = scratch
    slots, width = query.shape
    spill = above.shape[0]
    head_count = width // HEAD_DIM
    pairs = [(states, held)]
    pairs += plane_rows(pieces[:count], key_weight) + plane_rows(pieces[count:], value_weight)
    copies = fetched(pairs, semaphores)
    totals[...] = jnp.zeros_like(totals)
    summed[...] = jnp.zeros_like(summed)
    for copy in copies:
        copy.wait()

    @pl.loop(0, states.shape[0] // tile)
    def _(step):
        span = aligned(step, tile)
        block = held[span, :]
        keys = dot(block, key_weight[...]).astype(jnp.bfloat16).astype(jnp.float32)
        index = lax.broadcasted_iota(jnp.int32, (slots, tile), 0)
        onehot = (index == slot_row[:, span]).astype(jnp.bfloat16)
        product = keys * lax.dot_general(
            onehot, query[...], (((0,), (0,)), ((), ())), preferred_element_type=jnp.float32
        )
        lane = lax.broadcasted_iota(jnp.int32, (tile, HEAD_DIM), 1)
        scores = jnp.zeros((tile, HEAD_DIM), jnp.float32)
        for head in range(head_count):
            total = jnp.sum(
                product[:, head * HEAD_DIM : (head + 1) * HEAD_DIM], axis=1, keepdims=True
            )
            scores = jnp.where(lane == head, total, scores)
        raw = capped_exp(scores / math.sqrt(HEAD_DIM))
        high = raw.astype(jnp.bfloat16)
        low = (raw - high.astype(jnp.float32)).astype(jnp.bfloat16)
        totals[...] += dot(onehot, high) + dot(onehot, low)
        values = dot(block, value_weight[...]).astype(jnp.bfloat16).astype(jnp.float32)
        weighted = jnp.concatenate(
            [
                (values[:, h * HEAD_DIM : (h + 1) * HEAD_DIM] * raw[:, h : h + 1]).astype(
                    jnp.bfloat16
                )
                for h in range(head_count)
            ],
            axis=1,
        )
        summed[...] += dot(onehot, weighted)

    total = totals[...]
    inverse = 1.0 / jnp.where(total > 0.0, total, 1.0)
    for h in range(head_count):
        part = slice(h * HEAD_DIM, (h + 1) * HEAD_DIM)
        heads = (summed[:, part] * inverse[:, h : h + 1]).astype(jnp.bfloat16)
        above[:, part] = heads[:spill]
        own[:, part] = heads[spill : slots - spill]
        below[:, part] = heads[slots - spill :]


def quarters(left, weight, outs):
    _, _, tensor = place()
    height = outs[0].shape[0]
    for r, out in enumerate(outs):
        block = left[aligned(tensor ^ r, height), :]
        out[...] = dot(block, weight[...]).astype(out.dtype)


def cross_out_kernel(count, weight, *refs):
    pieces, outs, whole = refs[:count], refs[count:-1], refs[-1]
    assemble(pieces, whole)
    quarters(whole, weight, outs)


def latent_out_kernel(count, *refs):
    chips = count // 2
    pieces, weights, refs = refs[:count], refs[count : count + chips], refs[count + chips :]
    outs, (whole, held, products_of, semaphores) = refs[:chips], refs[chips:]
    chip, core, tensor = place()
    copies = fetched([(weight, held.at[d]) for d, weight in enumerate(weights)], semaphores)
    for n, piece in enumerate(pieces):
        index = chips * (core ^ (n % 2)) + (chip ^ (n // 2))
        whole[:, aligned(index, HEAD_DIM)] = piece[...]
    height = whole.shape[0]
    for d, copy in enumerate(copies):
        copy.wait()
        products_of[aligned(chip ^ d, height), :] = dot(whole[...], held[d])
    for r, out in enumerate(outs):
        out[...] = products_of[aligned(tensor ^ r, height), :].astype(out.dtype)


def arrange_kernel(*refs):
    weights, outs, semaphores = refs[:6], refs[6:-1], refs[-1]
    chip, core, _ = place()
    height = weights[0].shape[0]
    copies = fetched(
        [
            (
                weights[2 * m + n].at[:, aligned(len(outs) * core + (chip ^ d), HEAD_DIM)],
                out.at[n * height : (n + 1) * height, m * HEAD_DIM : (m + 1) * HEAD_DIM],
            )
            for d, out in enumerate(outs)
            for m in range(3)
            for n in range(2)
        ],
        semaphores,
    )
    for copy in copies:
        copy.wait()


def diagonal(size):
    return lax.broadcasted_iota(jnp.int32, (size, size), 0) == lax.broadcasted_iota(
        jnp.int32, (size, size), 1
    )


def project_kernel(count, gain, *refs):
    blocks, refs = refs[: 2 * count], refs[2 * count :]
    chips = (len(refs) - 1) // 2
    weights, outs, left = refs[:chips], refs[chips:-1], refs[-1]
    seq = lax.axis_index("seq")
    part, width = blocks[0].shape
    height = count * part
    totals = []
    for q in range(count):
        total = jnp.zeros((part, 1), jnp.float32)
        for n, block in enumerate(blocks[2 * q : 2 * q + 2]):
            hidden = block[...].astype(jnp.float32)
            total += jnp.sum(hidden * hidden, axis=1, keepdims=True)
            left[q * part : (q + 1) * part, n * width : (n + 1) * width] = (
                hidden * gain[:, aligned(seq ^ n, width)]
            ).astype(jnp.bfloat16)
        totals.append(jnp.sum(jnp.where(diagonal(part), total, 0.0), axis=0, keepdims=True))
    for weight, out in reversed(list(zip(weights, outs))):
        out[:height, :] = dot(left[...], weight[...]).astype(out.dtype)
    outs[0][height:, :] = jnp.zeros((outs[0].shape[0] - height, outs[0].shape[1]), jnp.float32)
    for out in outs[1:]:
        out[height:, :] = jnp.zeros((out.shape[0] - height, out.shape[1]), jnp.bfloat16)
    index = lax.broadcasted_iota(jnp.int32, (16, part), 0)
    own_sums, sent_sums = jnp.zeros((8, part), jnp.float32), jnp.zeros((16, part), jnp.float32)
    for q, row in enumerate(totals):
        high = row.astype(jnp.bfloat16).astype(jnp.float32)
        middle = (row - high).astype(jnp.bfloat16).astype(jnp.float32)
        own_sums = jnp.where(index[:8] == q, row, own_sums)
        for m, term in enumerate((high, middle, row - high - middle)):
            sent_sums = jnp.where(index == 3 * q + m, term, sent_sums)
    outs[0][height:, :part] = own_sums
    for out in outs[1:]:
        out[height:, :part] = sent_sums.astype(jnp.bfloat16)


def attention_kernel(groups, chips, depth, *refs):
    shares, refs = refs[: len(groups) * chips], refs[len(groups) * chips :]
    outs, (query, key, value, attended) = refs[:chips], refs[chips:]
    chip, _, tensor = place()
    parts = sum(len(group) for group in groups)
    height = attended.shape[0] // parts
    own_place = diagonal(height)
    for g, group in enumerate(groups):
        end = len(group) * height
        own, *received = shares[g * chips : (g + 1) * chips]
        for q, r in enumerate(group):
            rows = slice(q * height, (q + 1) * height)
            total = own[rows, :]
            row = own[end:, :height][q : q + 1]
            for share in received:
                total += share[rows, :].astype(jnp.float32)
                terms = share[end:, :height].astype(jnp.float32)
                row += sum(terms[3 * q + m : 3 * q + m + 1] for m in range(3))
            column = jnp.sum(jnp.where(own_place, row, 0.0), axis=1, keepdims=True)
            total = (total * lax.rsqrt(column / depth + norm_eps)).astype(jnp.bfloat16)
            span = aligned(tensor ^ r, height)
            for m, kept in enumerate((query, key, value)):
                kept[span, :] = total[:, m * HEAD_DIM : (m + 1) * HEAD_DIM]
    causal = lax.broadcasted_iota(jnp.int32, (height, height), 0) >= lax.broadcasted_iota(
        jnp.int32, (height, height), 1
    )
    for i in range(parts):
        block = query[i * height : (i + 1) * height, :]
        numerator = jnp.zeros((height, HEAD_DIM), jnp.float32)
        denominator = jnp.zeros((height, 1), jnp.float32)
        for j in range(i + 1):
            span = slice(j * height, (j + 1) * height)
            scores = lax.dot_general(
                block, key[span, :], (((1,), (1,)), ((), ())), preferred_element_type=jnp.float32
            )
            raw = capped_exp(scores / math.sqrt(HEAD_DIM))
            if i == j:
                raw = jnp.where(causal, raw, 0.0)
            denominator += jnp.sum(raw, axis=1, keepdims=True)
            numerator += dot(raw.astype(jnp.bfloat16), value[span, :])
        attended[i * height : (i + 1) * height, :] = (numerator / denominator).astype(jnp.bfloat16)
    for d, out in enumerate(outs):
        out[...] = attended[aligned(chip ^ d, out.shape[0]), :]


def final_kernel(own, *refs):
    received, outs, whole = refs[:-3], refs[-3:-1], refs[-1]
    _, core, _ = place()
    total = own[...]
    for block in received:
        total += block[...].astype(jnp.float32)
    whole[...] = total
    height = outs[0].shape[0]
    for flip, out in enumerate(outs):
        out[...] = whole[aligned(core ^ flip, height), :].astype(jnp.bfloat16)


def per_device(
    byte_states,
    byte_patch,
    patch_len,
    cross_query,
    cross_key,
    cross_value,
    cross_out,
    norm_gain,
    latent_query,
    latent_key,
    latent_value,
    latent_out,
):
    seq = lax.axis_index("seq")
    core = lax.rem(seq, 2)
    seq_count = lax.axis_size("seq")
    tensor_count = lax.axis_size("tensor")
    chip_count = seq_count // 2
    patch_count = patch_len.shape[0]
    patch_dev = patch_count // seq_count
    spill = patch_dev // 2
    slot_count = patch_dev + 2 * spill
    byte_count, byte_width = byte_states.shape
    local_width = cross_query.shape[1]
    out_width = cross_out.shape[1]
    quarter = patch_count // tensor_count
    bf16, f32 = jnp.bfloat16, jnp.float32
    tile = min(1024, byte_count)

    def over_plane(block, earlier=(), last_hop=None):
        moved = [block]
        for d in range(1, chip_count):
            hop = last_hop(d) if last_hop else d
            moved.append(exchanged(moved[d ^ hop], "seq", 2 * hop))
        pieces = []
        for d, part in enumerate(moved):
            pieces += [part, core_swapped(after(part, *earlier) if d else part)]
        return pieces

    slot_of = byte_patch - (seq * patch_dev - spill)
    slot_row = slot_of[None, :]
    edge = jnp.ones((spill,), jnp.int32)
    lengths = lax.dynamic_slice_in_dim(
        jnp.concatenate([edge, patch_len, edge]), seq * patch_dev, slot_count
    ).astype(f32)[:, None]
    query_pieces = over_plane(cross_query)
    (query_slots,) = call(
        functools.partial(query_kernel, seq_count),
        [((slot_count, local_width), bf16)],
        slot_row,
        lengths,
        byte_states,
        *query_pieces,
        far=1 + seq_count,
        scratch=[
            pltpu.VMEM((byte_count, byte_width), bf16),
            pltpu.VMEM((byte_width, local_width), bf16),
            pltpu.SemaphoreType.DMA((1 + seq_count,)),
        ],
        flops=2 * slot_count * byte_width * (byte_count + local_width),
    )
    key_pieces = over_plane(cross_key, (query_slots,), lambda d: 1 << (d.bit_length() - 1))
    value_pieces = over_plane(cross_value, (query_slots,), lambda d: d & -d)

    near = (key_pieces[-2], value_pieces[-2])
    weights = []
    for weight in (latent_query, latent_key, latent_value):
        weights += [weight, core_swapped(after(weight, *near))]
    out_weights = [latent_out, exchanged(after(latent_out, *near), "seq", 2 * (chip_count - 1))]
    own, above, below = call(
        functools.partial(cross_kernel, seq_count, tile),
        [((height, local_width), bf16) for height in (patch_dev, spill, spill)],
        slot_row,
        query_slots,
        byte_states,
        *key_pieces,
        *value_pieces,
        far=1 + 2 * seq_count,
        scratch=[
            pltpu.VMEM((byte_count, byte_width), bf16),
            pltpu.VMEM((byte_width, local_width), bf16),
            pltpu.VMEM((byte_width, local_width), bf16),
            pltpu.VMEM((slot_count, HEAD_DIM), f32),
            pltpu.VMEM((slot_count, local_width), f32),
            pltpu.SemaphoreType.DMA((1 + 2 * seq_count,)),
        ],
        flops=4 * byte_count * local_width * (byte_width + slot_count),
    )

    spilled = [shifted(below, "seq", 1), shifted(above, "seq", -1)]
    own, out_weights[-1] = lax.optimization_barrier((own, out_weights[-1]))
    own = own + jnp.concatenate(spilled, axis=0)

    total, *sent = call(
        functools.partial(cross_out_kernel, seq_count),
        [((quarter, out_width), f32 if r == 0 else bf16) for r in range(tensor_count)],
        cross_out,
        *over_plane(own),
        scratch=[pltpu.VMEM((patch_count, local_width), bf16)],
        flops=2 * patch_count * local_width * out_width,
    )
    received = [exchanged(block, "tensor", r) for r, block in enumerate(sent, 1)]

    head_weights = call(
        arrange_kernel,
        [((2 * out_width, 3 * HEAD_DIM), bf16)] * chip_count,
        *[after(weight, total) for weight in weights],
        far=6,
        scratch=[pltpu.SemaphoreType.DMA((6 * chip_count,))],
    )
    for d in range(1, chip_count - 1):
        out_weights.insert(d, exchanged(after(latent_out, total), "seq", 2 * d))
    total, *rest = lax.optimization_barrier((total, *head_weights, *out_weights))
    head_weights, out_weights = rest[:chip_count], rest[chip_count:]
    for share in received:
        total = total + share.astype(f32)
    latent_in = total.astype(bf16)

    gain = norm_gain[None, :]
    groups = [[0], list(range(1, min(3, tensor_count))), list(range(3, tensor_count))]
    groups = [group for group in groups if group]
    shares, arrived = [], []
    for g, group in enumerate(groups):
        blocks = [latent_in]
        if g:
            start = after(latent_in, *arrived, *shares[:chip_count]) if g > 1 else latent_in
            arrived = [exchanged(start, "tensor", r) for r in group]
            blocks = [after(block, *shares[:chip_count]) for block in arrived]
        height = len(group) * quarter
        share, *sent = call(
            functools.partial(project_kernel, len(group)),
            [((height + 8, 3 * HEAD_DIM), f32)]
            + [((height + 16, 3 * HEAD_DIM), bf16)] * (chip_count - 1),
            gain,
            *[piece for block in blocks for piece in (block, core_swapped(block))],
            *head_weights,
            scratch=[pltpu.VMEM((height, 2 * out_width), bf16)],
            flops=2 * height * 2 * out_width * 3 * HEAD_DIM * chip_count,
        )
        if g > 1:
            sent = [after(part, *shares[(g - 1) * chip_count + 1 :]) for part in sent]
        shares += [share] + [exchanged(part, "seq", 2 * d) for d, part in enumerate(sent, 1)]
    attended = call(
        functools.partial(attention_kernel, groups, chip_count, out_width * seq_count),
        [((quarter, HEAD_DIM), bf16)] * chip_count,
        *shares,
        scratch=[pltpu.VMEM((patch_count, HEAD_DIM), bf16)] * 4,
        flops=2 * patch_count * patch_count * HEAD_DIM,
    )

    route = [
        (s * tensor_count + t, (2 * t + s % 2) * tensor_count + s // 2)
        for s in range(seq_count)
        for t in range(tensor_count)
    ]
    residual = lax.ppermute(after(latent_in, *arrived), ("seq", "tensor"), route)

    pieces = []
    for d, block in enumerate(attended):
        moved = exchanged(block, "seq", 2 * d) if d else block
        pieces += [moved, core_swapped(moved)]
    pieces[0], residual = lax.optimization_barrier((pieces[0], residual))
    total, *sent = call(
        functools.partial(latent_out_kernel, seq_count),
        [((quarter, out_width), bf16 if r else f32) for r in range(tensor_count)],
        *pieces,
        *out_weights,
        far=chip_count,
        scratch=[
            pltpu.VMEM((quarter, local_width), bf16),
            pltpu.VMEM((chip_count, local_width, out_width), bf16),
            pltpu.VMEM((patch_count, out_width), f32),
            pltpu.SemaphoreType.DMA((chip_count,)),
        ],
        flops=2 * quarter * local_width * out_width * chip_count,
    )
    same, crossed = call(
        final_kernel,
        [((patch_dev, out_width), bf16)] * 2,
        total,
        residual,
        *[exchanged(block, "tensor", r) for r, block in enumerate(sent, 1)],
        scratch=[pltpu.VMEM((quarter, out_width), f32)],
    )
    crossed = core_swapped(crossed)
    return jnp.concatenate(
        [jnp.where(core == 0, same, crossed), jnp.where(core == 0, crossed, same)], axis=1
    )


def head_per_device(mesh, heads):
    seq_count, tensor_count = mesh.shape["seq"], mesh.shape["tensor"]
    return (
        heads == seq_count * tensor_count
        and seq_count == 2 * tensor_count
        and tensor_count & (tensor_count - 1) == 0
    )


def solution(mesh):
    specs = (
        P("seq", None),
        P("seq"),
        P(),
        P("seq", "tensor"),
        P("seq", "tensor"),
        P("seq", "tensor"),
        P("tensor", "seq"),
        P(),
        P("seq", "tensor"),
        P("seq", "tensor"),
        P("seq", "tensor"),
        P("tensor", "seq"),
    )

    def whole(*arrays):
        chosen = (
            per_device
            if head_per_device(mesh, arrays[3].shape[1] // HEAD_DIM)
            else per_device_gathered
        )
        return jax.shard_map(
            chosen, mesh=mesh, in_specs=specs, out_specs=P("seq", "tensor"), check_vma=False
        )(*arrays)

    return whole
```

```python
import functools
import math

import jax
import jax.numpy as jnp
from jax import lax
from jax.experimental import pallas as pl
from jax.experimental.pallas import tpu as pltpu
from jax.sharding import PartitionSpec as P

HEAD_DIM = 128
PATCH_DEV = 128


score_cap = 30.0
norm_eps = 1e-05


def shifted(block, axis, distance):
    devices = range(lax.axis_size(axis))
    route = [(i - distance, i) for i in devices if i - distance in devices]
    return lax.ppermute(block, axis, route)


def capped_exp(scores):
    return jnp.exp(score_cap * jnp.tanh(scores / score_cap))


def contract_rows(left, right):
    return lax.dot_general(
        left,
        right,
        (((0,), (0,)), ((), ())),
        precision=lax.Precision.HIGHEST,
        preferred_element_type=jnp.float32,
    )


def per_device_gathered(
    byte_states,
    byte_patch,
    patch_len,
    cross_query,
    cross_key,
    cross_value,
    cross_out,
    norm_gain,
    latent_query,
    latent_key,
    latent_value,
    latent_out,
):
    seq_index = lax.axis_index("seq")
    tensor_count = lax.axis_size("tensor")
    (
        cross_query,
        cross_key,
        cross_value,
        latent_query,
        latent_key,
        latent_value,
        cross_out,
        latent_out,
    ) = (
        lax.all_gather(cross_query, "seq", axis=0, tiled=True),
        lax.all_gather(cross_key, "seq", axis=0, tiled=True),
        lax.all_gather(cross_value, "seq", axis=0, tiled=True),
        lax.all_gather(latent_query, "seq", axis=0, tiled=True),
        lax.all_gather(latent_key, "seq", axis=0, tiled=True),
        lax.all_gather(latent_value, "seq", axis=0, tiled=True),
        lax.all_gather(cross_out, "seq", axis=1, tiled=True),
        lax.all_gather(latent_out, "seq", axis=1, tiled=True),
    )
    latent_width = cross_out.shape[1]
    local_width = cross_out.shape[0]
    head_count = local_width // HEAD_DIM
    slot_count = 2 * PATCH_DEV
    byte_count = byte_states.shape[0]
    first_patch = byte_patch[0]
    slot_of = byte_patch - first_patch
    onehot_mask = slot_of[:, None] == jnp.arange(slot_count, dtype=jnp.int32)[None, :]
    onehot = onehot_mask.astype(jnp.bfloat16)
    onehot_float = onehot_mask.astype(jnp.float32)
    byte_sums = lax.dot_general(
        onehot, byte_states, (((0,), (0,)), ((), ())), preferred_element_type=jnp.float32
    )
    lengths_all = jnp.concatenate([patch_len, jnp.ones((slot_count,), jnp.int32)])
    lengths = lax.dynamic_slice_in_dim(lengths_all, first_patch, slot_count)
    pooled = (byte_sums / lengths.astype(jnp.float32)[:, None]).astype(jnp.bfloat16)
    query_slots = jnp.dot(pooled, cross_query, preferred_element_type=jnp.float32).astype(
        jnp.bfloat16
    )
    byte_keys = jnp.dot(byte_states, cross_key, preferred_element_type=jnp.float32).astype(
        jnp.bfloat16
    )
    byte_values = jnp.dot(byte_states, cross_value, preferred_element_type=jnp.float32).astype(
        jnp.bfloat16
    )
    query_bytes = jnp.dot(onehot, query_slots, preferred_element_type=jnp.float32)
    scores = (query_bytes * byte_keys.astype(jnp.float32)).reshape(
        byte_count, head_count, HEAD_DIM
    ).sum(axis=2) / math.sqrt(HEAD_DIM)
    byte_raw = capped_exp(scores)
    totals = contract_rows(onehot_float, byte_raw)
    totals = jnp.where(totals > 0.0, totals, 1.0)
    totals_bytes = jnp.dot(
        onehot_float, totals, precision=lax.Precision.HIGHEST, preferred_element_type=jnp.float32
    )
    byte_weight = (byte_raw / totals_bytes).astype(jnp.bfloat16)
    weighted = (
        byte_weight.astype(jnp.float32)[:, :, None]
        * byte_values.astype(jnp.float32).reshape(byte_count, head_count, HEAD_DIM)
    ).reshape(byte_count, local_width)
    cross_heads = contract_rows(onehot_float, weighted).astype(jnp.bfloat16)
    padding = jnp.zeros((2 * PATCH_DEV, cross_heads.shape[1]), cross_heads.dtype)
    padded = jnp.concatenate([padding, cross_heads, padding], axis=0)
    offset = seq_index * PATCH_DEV - first_patch + 2 * PATCH_DEV
    padded, offset = (padded, offset)
    owned_heads = lax.dynamic_slice_in_dim(padded, offset, PATCH_DEV, 0)
    for offset_step in (-1, 1):
        window = lax.dynamic_slice_in_dim(padded, offset + offset_step * PATCH_DEV, PATCH_DEV, 0)
        owned_heads = owned_heads + shifted(window, "seq", offset_step)
    partial_value = jnp.dot(owned_heads, cross_out, preferred_element_type=jnp.float32)
    latent_in = lax.psum(partial_value, "tensor").astype(jnp.bfloat16)
    hidden = latent_in.astype(jnp.float32)
    mean_square = jnp.mean(hidden * hidden, axis=1, keepdims=True)
    normed = (hidden * lax.rsqrt(mean_square + norm_eps) * norm_gain[None, :]).astype(jnp.bfloat16)
    query = (
        jnp.dot(normed, latent_query, preferred_element_type=jnp.float32)
        .astype(jnp.bfloat16)
        .reshape(PATCH_DEV, head_count, HEAD_DIM)
    )
    key_rows = jnp.dot(normed, latent_key, preferred_element_type=jnp.float32).astype(jnp.bfloat16)
    value_rows = jnp.dot(normed, latent_value, preferred_element_type=jnp.float32).astype(
        jnp.bfloat16
    )
    positions = seq_index * PATCH_DEV + jnp.arange(PATCH_DEV, dtype=jnp.int32)
    key_piece = lax.all_gather(key_rows, "seq", axis=0, tiled=True)
    value_piece = lax.all_gather(value_rows, "seq", axis=0, tiled=True)
    piece_rows = key_piece.shape[0]
    key_piece = key_piece.reshape(piece_rows, head_count, HEAD_DIM)
    value_piece = value_piece.reshape(piece_rows, head_count, HEAD_DIM)
    piece_scores = jnp.einsum(
        "qhd,khd->hqk", query, key_piece, preferred_element_type=jnp.float32
    ) / math.sqrt(HEAD_DIM)
    key_positions = jnp.arange(piece_rows, dtype=jnp.int32)
    allowed = key_positions[None, :] <= positions[:, None]
    exp_scores = jnp.where(allowed[None, :, :], capped_exp(piece_scores), 0.0)
    denominator = jnp.sum(exp_scores, axis=2)
    numerator = jnp.einsum(
        "hqk,khd->hqd",
        exp_scores.astype(jnp.bfloat16),
        value_piece,
        preferred_element_type=jnp.float32,
    )
    numerator, denominator = (numerator, denominator)
    attended = (numerator / denominator[:, :, None]).astype(jnp.bfloat16)
    attended = attended.transpose(1, 0, 2).reshape(PATCH_DEV, local_width)
    projected = jnp.dot(attended, latent_out, preferred_element_type=jnp.float32)
    mixed_sum = lax.psum_scatter(projected, "tensor", scatter_dimension=1, tiled=True)
    column_width = latent_width // tensor_count
    residual = lax.dynamic_slice_in_dim(
        hidden, lax.axis_index("tensor") * column_width, column_width, 1
    )
    return (residual + mixed_sum).astype(jnp.bfloat16)


def dot(left, right):
    return jnp.dot(left, right, preferred_element_type=jnp.float32)


def exchanged(block, axis, distance):
    route = [(i, i ^ distance) for i in range(lax.axis_size(axis))]
    return lax.ppermute(block, axis, route)


def core_swapped(block):
    return exchanged(block, "seq", 1)


def after(value, *earlier):
    return lax.optimization_barrier((value, *earlier))[0]


def place():
    seq = lax.axis_index("seq")
    return seq // 2, lax.rem(seq, 2), lax.axis_index("tensor")


def aligned(index, size):
    return pl.ds(pl.multiple_of(index * size, size), size)


def fetched(pairs, semaphores):
    copies = [
        pltpu.make_async_copy(source, target, semaphores.at[n])
        for n, (source, target) in enumerate(pairs)
    ]
    for copy in copies:
        copy.start()
    return copies


def call(kernel, outs, *operands, far=0, scratch=(), flops=0):
    shapes = [jax.ShapeDtypeStruct(shape, dtype) for shape, dtype in outs]
    moved = sum(o.size * o.dtype.itemsize for o in [*operands, *shapes])
    return pl.pallas_call(
        kernel,
        out_shape=shapes,
        in_specs=[pl.BlockSpec(memory_space=pltpu.VMEM)] * (len(operands) - far)
        + [pl.BlockSpec(memory_space=pl.ANY)] * far,
        out_specs=[pl.BlockSpec(memory_space=pltpu.VMEM)] * len(outs),
        scratch_shapes=list(scratch),
        compiler_params=pltpu.CompilerParams(vmem_limit_bytes=28 * 1024 * 1024),
        cost_estimate=pl.CostEstimate(flops=flops, bytes_accessed=moved, transcendentals=0),
    )(*operands)


def assemble(pieces, whole):
    chip, core, _ = place()
    for n, piece in enumerate(pieces):
        index = 2 * (chip ^ (n // 2)) + (core ^ (n % 2))
        whole[aligned(index, piece.shape[0]), :] = piece[...]


def plane_rows(pieces, whole):
    chip, core, _ = place()
    return [
        (piece, whole.at[aligned(2 * (chip ^ (n // 2)) + (core ^ (n % 2)), piece.shape[0]), :])
        for n, piece in enumerate(pieces)
    ]


def query_kernel(count, slot_row, lengths, states, *refs):
    pieces, (query, held, whole, semaphores) = refs[:count], refs[count:]
    slots, byte_count = query.shape[0], states.shape[0]
    copies = fetched([(states, held), *plane_rows(pieces, whole)], semaphores)
    index = lax.broadcasted_iota(jnp.int32, (slots, byte_count), 0)
    onehot = (index == slot_row[...]).astype(jnp.bfloat16)
    copies[0].wait()
    pooled = (dot(onehot, held[...]) / lengths[...]).astype(jnp.bfloat16)
    for copy in copies[1:]:
        copy.wait()
    query[...] = dot(pooled, whole[...]).astype(jnp.bfloat16)


def cross_kernel(count, tile, slot_row, query, states, *refs):
    pieces, (own, above, below, *scratch) = refs[: 2 * count], refs[2 * count :]
    held, key_weight, value_weight, totals, summed, semaphores = scratch
    slots, width = query.shape
    spill = above.shape[0]
    head_count = width // HEAD_DIM
    pairs = [(states, held)]
    pairs += plane_rows(pieces[:count], key_weight) + plane_rows(pieces[count:], value_weight)
    copies = fetched(pairs, semaphores)
    totals[...] = jnp.zeros_like(totals)
    summed[...] = jnp.zeros_like(summed)
    for copy in copies:
        copy.wait()

    @pl.loop(0, states.shape[0] // tile)
    def _(step):
        span = aligned(step, tile)
        block = held[span, :]
        keys = dot(block, key_weight[...]).astype(jnp.bfloat16).astype(jnp.float32)
        index = lax.broadcasted_iota(jnp.int32, (slots, tile), 0)
        onehot = (index == slot_row[:, span]).astype(jnp.bfloat16)
        product = keys * lax.dot_general(
            onehot, query[...], (((0,), (0,)), ((), ())), preferred_element_type=jnp.float32
        )
        lane = lax.broadcasted_iota(jnp.int32, (tile, HEAD_DIM), 1)
        scores = jnp.zeros((tile, HEAD_DIM), jnp.float32)
        for head in range(head_count):
            total = jnp.sum(
                product[:, head * HEAD_DIM : (head + 1) * HEAD_DIM], axis=1, keepdims=True
            )
            scores = jnp.where(lane == head, total, scores)
        raw = capped_exp(scores / math.sqrt(HEAD_DIM))
        high = raw.astype(jnp.bfloat16)
        low = (raw - high.astype(jnp.float32)).astype(jnp.bfloat16)
        totals[...] += dot(onehot, high) + dot(onehot, low)
        values = dot(block, value_weight[...]).astype(jnp.bfloat16).astype(jnp.float32)
        weighted = jnp.concatenate(
            [
                (values[:, h * HEAD_DIM : (h + 1) * HEAD_DIM] * raw[:, h : h + 1]).astype(
                    jnp.bfloat16
                )
                for h in range(head_count)
            ],
            axis=1,
        )
        summed[...] += dot(onehot, weighted)

    total = totals[...]
    inverse = 1.0 / jnp.where(total > 0.0, total, 1.0)
    for h in range(head_count):
        part = slice(h * HEAD_DIM, (h + 1) * HEAD_DIM)
        heads = (summed[:, part] * inverse[:, h : h + 1]).astype(jnp.bfloat16)
        above[:, part] = heads[:spill]
        own[:, part] = heads[spill : slots - spill]
        below[:, part] = heads[slots - spill :]


def quarters(left, weight, outs):
    _, _, tensor = place()
    height = outs[0].shape[0]
    for r, out in enumerate(outs):
        block = left[aligned(tensor ^ r, height), :]
        out[...] = dot(block, weight[...]).astype(out.dtype)


def cross_out_kernel(count, weight, *refs):
    pieces, outs, whole = refs[:count], refs[count:-1], refs[-1]
    assemble(pieces, whole)
    quarters(whole, weight, outs)


def latent_out_kernel(count, *refs):
    chips = count // 2
    pieces, weights, refs = refs[:count], refs[count : count + chips], refs[count + chips :]
    outs, (whole, held, products_of, semaphores) = refs[:chips], refs[chips:]
    chip, core, tensor = place()
    copies = fetched([(weight, held.at[d]) for d, weight in enumerate(weights)], semaphores)
    for n, piece in enumerate(pieces):
        index = chips * (core ^ (n % 2)) + (chip ^ (n // 2))
        whole[:, aligned(index, HEAD_DIM)] = piece[...]
    height = whole.shape[0]
    for d, copy in enumerate(copies):
        copy.wait()
        products_of[aligned(chip ^ d, height), :] = dot(whole[...], held[d])
    for r, out in enumerate(outs):
        out[...] = products_of[aligned(tensor ^ r, height), :].astype(out.dtype)


def arrange_kernel(*refs):
    weights, outs, semaphores = refs[:6], refs[6:-1], refs[-1]
    chip, core, _ = place()
    height = weights[0].shape[0]
    copies = fetched(
        [
            (
                weights[2 * m + n].at[:, aligned(len(outs) * core + (chip ^ d), HEAD_DIM)],
                out.at[n * height : (n + 1) * height, m * HEAD_DIM : (m + 1) * HEAD_DIM],
            )
            for d, out in enumerate(outs)
            for m in range(3)
            for n in range(2)
        ],
        semaphores,
    )
    for copy in copies:
        copy.wait()


def diagonal(size):
    return lax.broadcasted_iota(jnp.int32, (size, size), 0) == lax.broadcasted_iota(
        jnp.int32, (size, size), 1
    )


def project_kernel(count, gain, *refs):
    blocks, refs = refs[: 2 * count], refs[2 * count :]
    chips = (len(refs) - 1) // 2
    weights, outs, left = refs[:chips], refs[chips:-1], refs[-1]
    seq = lax.axis_index("seq")
    part, width = blocks[0].shape
    height = count * part
    totals = []
    for q in range(count):
        total = jnp.zeros((part, 1), jnp.float32)
        for n, block in enumerate(blocks[2 * q : 2 * q + 2]):
            hidden = block[...].astype(jnp.float32)
            total += jnp.sum(hidden * hidden, axis=1, keepdims=True)
            left[q * part : (q + 1) * part, n * width : (n + 1) * width] = (
                hidden * gain[:, aligned(seq ^ n, width)]
            ).astype(jnp.bfloat16)
        totals.append(jnp.sum(jnp.where(diagonal(part), total, 0.0), axis=0, keepdims=True))
    for weight, out in reversed(list(zip(weights, outs))):
        out[:height, :] = dot(left[...], weight[...]).astype(out.dtype)
    outs[0][height:, :] = jnp.zeros((outs[0].shape[0] - height, outs[0].shape[1]), jnp.float32)
    for out in outs[1:]:
        out[height:, :] = jnp.zeros((out.shape[0] - height, out.shape[1]), jnp.bfloat16)
    index = lax.broadcasted_iota(jnp.int32, (16, part), 0)
    own_sums, sent_sums = jnp.zeros((8, part), jnp.float32), jnp.zeros((16, part), jnp.float32)
    for q, row in enumerate(totals):
        high = row.astype(jnp.bfloat16).astype(jnp.float32)
        middle = (row - high).astype(jnp.bfloat16).astype(jnp.float32)
        own_sums = jnp.where(index[:8] == q, row, own_sums)
        for m, term in enumerate((high, middle, row - high - middle)):
            sent_sums = jnp.where(index == 3 * q + m, term, sent_sums)
    outs[0][height:, :part] = own_sums
    for out in outs[1:]:
        out[height:, :part] = sent_sums.astype(jnp.bfloat16)


def attention_kernel(groups, chips, depth, *refs):
    shares, refs = refs[: len(groups) * chips], refs[len(groups) * chips :]
    outs, (query, key, value, attended) = refs[:chips], refs[chips:]
    chip, _, tensor = place()
    parts = sum(len(group) for group in groups)
    height = attended.shape[0] // parts
    own_place = diagonal(height)
    for g, group in enumerate(groups):
        end = len(group) * height
        own, *received = shares[g * chips : (g + 1) * chips]
        for q, r in enumerate(group):
            rows = slice(q * height, (q + 1) * height)
            total = own[rows, :]
            row = own[end:, :height][q : q + 1]
            for share in received:
                total += share[rows, :].astype(jnp.float32)
                terms = share[end:, :height].astype(jnp.float32)
                row += sum(terms[3 * q + m : 3 * q + m + 1] for m in range(3))
            column = jnp.sum(jnp.where(own_place, row, 0.0), axis=1, keepdims=True)
            total = (total * lax.rsqrt(column / depth + norm_eps)).astype(jnp.bfloat16)
            span = aligned(tensor ^ r, height)
            for m, kept in enumerate((query, key, value)):
                kept[span, :] = total[:, m * HEAD_DIM : (m + 1) * HEAD_DIM]
    causal = lax.broadcasted_iota(jnp.int32, (height, height), 0) >= lax.broadcasted_iota(
        jnp.int32, (height, height), 1
    )
    for i in range(parts):
        block = query[i * height : (i + 1) * height, :]
        numerator = jnp.zeros((height, HEAD_DIM), jnp.float32)
        denominator = jnp.zeros((height, 1), jnp.float32)
        for j in range(i + 1):
            span = slice(j * height, (j + 1) * height)
            scores = lax.dot_general(
                block, key[span, :], (((1,), (1,)), ((), ())), preferred_element_type=jnp.float32
            )
            raw = capped_exp(scores / math.sqrt(HEAD_DIM))
            if i == j:
                raw = jnp.where(causal, raw, 0.0)
            denominator += jnp.sum(raw, axis=1, keepdims=True)
            numerator += dot(raw.astype(jnp.bfloat16), value[span, :])
        attended[i * height : (i + 1) * height, :] = (numerator / denominator).astype(jnp.bfloat16)
    for d, out in enumerate(outs):
        out[...] = attended[aligned(chip ^ d, out.shape[0]), :]


def final_kernel(own, *refs):
    received, outs, whole = refs[:-3], refs[-3:-1], refs[-1]
    _, core, _ = place()
    total = own[...]
    for block in received:
        total += block[...].astype(jnp.float32)
    whole[...] = total
    height = outs[0].shape[0]
    for flip, out in enumerate(outs):
        out[...] = whole[aligned(core ^ flip, height), :].astype(jnp.bfloat16)


def per_device(
    byte_states,
    byte_patch,
    patch_len,
    cross_query,
    cross_key,
    cross_value,
    cross_out,
    norm_gain,
    latent_query,
    latent_key,
    latent_value,
    latent_out,
):
    seq = lax.axis_index("seq")
    core = lax.rem(seq, 2)
    seq_count = lax.axis_size("seq")
    tensor_count = lax.axis_size("tensor")
    chip_count = seq_count // 2
    patch_count = patch_len.shape[0]
    patch_dev = patch_count // seq_count
    spill = patch_dev // 2
    slot_count = patch_dev + 2 * spill
    byte_count, byte_width = byte_states.shape
    local_width = cross_query.shape[1]
    out_width = cross_out.shape[1]
    quarter = patch_count // tensor_count
    bf16, f32 = jnp.bfloat16, jnp.float32
    tile = min(1024, byte_count)

    def over_plane(block, earlier=(), last_hop=None):
        moved = [block]
        for d in range(1, chip_count):
            hop = last_hop(d) if last_hop else d
            moved.append(exchanged(moved[d ^ hop], "seq", 2 * hop))
        pieces = []
        for d, part in enumerate(moved):
            pieces += [part, core_swapped(after(part, *earlier) if d else part)]
        return pieces

    slot_of = byte_patch - (seq * patch_dev - spill)
    slot_row = slot_of[None, :]
    edge = jnp.ones((spill,), jnp.int32)
    lengths = lax.dynamic_slice_in_dim(
        jnp.concatenate([edge, patch_len, edge]), seq * patch_dev, slot_count
    ).astype(f32)[:, None]
    query_pieces = over_plane(cross_query)
    (query_slots,) = call(
        functools.partial(query_kernel, seq_count),
        [((slot_count, local_width), bf16)],
        slot_row,
        lengths,
        byte_states,
        *query_pieces,
        far=1 + seq_count,
        scratch=[
            pltpu.VMEM((byte_count, byte_width), bf16),
            pltpu.VMEM((byte_width, local_width), bf16),
            pltpu.SemaphoreType.DMA((1 + seq_count,)),
        ],
        flops=2 * slot_count * byte_width * (byte_count + local_width),
    )
    key_pieces = over_plane(cross_key, (query_slots,), lambda d: 1 << (d.bit_length() - 1))
    value_pieces = over_plane(cross_value, (query_slots,), lambda d: d & -d)

    near = (key_pieces[-2], value_pieces[-2])
    weights = []
    for weight in (latent_query, latent_key, latent_value):
        weights += [weight, core_swapped(after(weight, *near))]
    out_weights = [latent_out, exchanged(after(latent_out, *near), "seq", 2 * (chip_count - 1))]
    own, above, below = call(
        functools.partial(cross_kernel, seq_count, tile),
        [((height, local_width), bf16) for height in (patch_dev, spill, spill)],
        slot_row,
        query_slots,
        byte_states,
        *key_pieces,
        *value_pieces,
        far=1 + 2 * seq_count,
        scratch=[
            pltpu.VMEM((byte_count, byte_width), bf16),
            pltpu.VMEM((byte_width, local_width), bf16),
            pltpu.VMEM((byte_width, local_width), bf16),
            pltpu.VMEM((slot_count, HEAD_DIM), f32),
            pltpu.VMEM((slot_count, local_width), f32),
            pltpu.SemaphoreType.DMA((1 + 2 * seq_count,)),
        ],
        flops=4 * byte_count * local_width * (byte_width + slot_count),
    )

    spilled = [shifted(below, "seq", 1), shifted(above, "seq", -1)]
    own, out_weights[-1] = lax.optimization_barrier((own, out_weights[-1]))
    own = own + jnp.concatenate(spilled, axis=0)

    total, *sent = call(
        functools.partial(cross_out_kernel, seq_count),
        [((quarter, out_width), f32 if r == 0 else bf16) for r in range(tensor_count)],
        cross_out,
        *over_plane(own),
        scratch=[pltpu.VMEM((patch_count, local_width), bf16)],
        flops=2 * patch_count * local_width * out_width,
    )
    received = [exchanged(block, "tensor", r) for r, block in enumerate(sent, 1)]

    head_weights = call(
        arrange_kernel,
        [((2 * out_width, 3 * HEAD_DIM), bf16)] * chip_count,
        *[after(weight, total) for weight in weights],
        far=6,
        scratch=[pltpu.SemaphoreType.DMA((6 * chip_count,))],
    )
    for d in range(1, chip_count - 1):
        out_weights.insert(d, exchanged(after(latent_out, total), "seq", 2 * d))
    total, *rest = lax.optimization_barrier((total, *head_weights, *out_weights))
    head_weights, out_weights = rest[:chip_count], rest[chip_count:]
    for share in received:
        total = total + share.astype(f32)
    latent_in = total.astype(bf16)

    gain = norm_gain[None, :]
    groups = [[0], list(range(1, min(3, tensor_count))), list(range(3, tensor_count))]
    groups = [group for group in groups if group]
    shares, arrived = [], []
    for g, group in enumerate(groups):
        blocks = [latent_in]
        if g:
            start = after(latent_in, *arrived, *shares[:chip_count]) if g > 1 else latent_in
            arrived = [exchanged(start, "tensor", r) for r in group]
            blocks = [after(block, *shares[:chip_count]) for block in arrived]
        height = len(group) * quarter
        share, *sent = call(
            functools.partial(project_kernel, len(group)),
            [((height + 8, 3 * HEAD_DIM), f32)]
            + [((height + 16, 3 * HEAD_DIM), bf16)] * (chip_count - 1),
            gain,
            *[piece for block in blocks for piece in (block, core_swapped(block))],
            *head_weights,
            scratch=[pltpu.VMEM((height, 2 * out_width), bf16)],
            flops=2 * height * 2 * out_width * 3 * HEAD_DIM * chip_count,
        )
        if g > 1:
            sent[2:] = [after(part, *shares[(g - 1) * chip_count + 1 :]) for part in sent[2:]]
        shares += [share] + [exchanged(part, "seq", 2 * d) for d, part in enumerate(sent, 1)]
    attended = call(
        functools.partial(attention_kernel, groups, chip_count, out_width * seq_count),
        [((quarter, HEAD_DIM), bf16)] * chip_count,
        *shares,
        scratch=[pltpu.VMEM((patch_count, HEAD_DIM), bf16)] * 4,
        flops=2 * patch_count * patch_count * HEAD_DIM,
    )

    route = [
        (s * tensor_count + t, (2 * t + s % 2) * tensor_count + s // 2)
        for s in range(seq_count)
        for t in range(tensor_count)
    ]
    residual = lax.ppermute(after(latent_in, *arrived), ("seq", "tensor"), route)

    pieces = []
    for d, block in enumerate(attended):
        moved = exchanged(block, "seq", 2 * d) if d else block
        pieces += [moved, core_swapped(moved)]
    pieces[0], residual = lax.optimization_barrier((pieces[0], residual))
    total, *sent = call(
        functools.partial(latent_out_kernel, seq_count),
        [((quarter, out_width), bf16 if r else f32) for r in range(tensor_count)],
        *pieces,
        *out_weights,
        far=chip_count,
        scratch=[
            pltpu.VMEM((quarter, local_width), bf16),
            pltpu.VMEM((chip_count, local_width, out_width), bf16),
            pltpu.VMEM((patch_count, out_width), f32),
            pltpu.SemaphoreType.DMA((chip_count,)),
        ],
        flops=2 * quarter * local_width * out_width * chip_count,
    )
    same, crossed = call(
        final_kernel,
        [((patch_dev, out_width), bf16)] * 2,
        total,
        residual,
        *[exchanged(block, "tensor", r) for r, block in enumerate(sent, 1)],
        scratch=[pltpu.VMEM((quarter, out_width), f32)],
    )
    crossed = core_swapped(crossed)
    return jnp.concatenate(
        [jnp.where(core == 0, same, crossed), jnp.where(core == 0, crossed, same)], axis=1
    )


def head_per_device(mesh, heads):
    seq_count, tensor_count = mesh.shape["seq"], mesh.shape["tensor"]
    return (
        heads == seq_count * tensor_count
        and seq_count == 2 * tensor_count
        and tensor_count & (tensor_count - 1) == 0
    )


def solution(mesh):
    specs = (
        P("seq", None),
        P("seq"),
        P(),
        P("seq", "tensor"),
        P("seq", "tensor"),
        P("seq", "tensor"),
        P("tensor", "seq"),
        P(),
        P("seq", "tensor"),
        P("seq", "tensor"),
        P("seq", "tensor"),
        P("tensor", "seq"),
    )

    def whole(*arrays):
        chosen = (
            per_device
            if head_per_device(mesh, arrays[3].shape[1] // HEAD_DIM)
            else per_device_gathered
        )
        return jax.shard_map(
            chosen, mesh=mesh, in_specs=specs, out_specs=P("seq", "tensor"), check_vma=False
        )(*arrays)

    return whole
```

```python
import functools
import math

import jax
import jax.numpy as jnp
from jax import lax
from jax.experimental import pallas as pl
from jax.experimental.pallas import tpu as pltpu
from jax.sharding import PartitionSpec as P

HEAD_DIM = 128
PATCH_DEV = 128


score_cap = 30.0
norm_eps = 1e-05


def shifted(block, axis, distance):
    devices = range(lax.axis_size(axis))
    route = [(i - distance, i) for i in devices if i - distance in devices]
    return lax.ppermute(block, axis, route)


def capped_exp(scores):
    return jnp.exp(score_cap * jnp.tanh(scores / score_cap))


def contract_rows(left, right):
    return lax.dot_general(
        left,
        right,
        (((0,), (0,)), ((), ())),
        precision=lax.Precision.HIGHEST,
        preferred_element_type=jnp.float32,
    )


def per_device_gathered(
    byte_states,
    byte_patch,
    patch_len,
    cross_query,
    cross_key,
    cross_value,
    cross_out,
    norm_gain,
    latent_query,
    latent_key,
    latent_value,
    latent_out,
):
    seq_index = lax.axis_index("seq")
    tensor_count = lax.axis_size("tensor")
    (
        cross_query,
        cross_key,
        cross_value,
        latent_query,
        latent_key,
        latent_value,
        cross_out,
        latent_out,
    ) = (
        lax.all_gather(cross_query, "seq", axis=0, tiled=True),
        lax.all_gather(cross_key, "seq", axis=0, tiled=True),
        lax.all_gather(cross_value, "seq", axis=0, tiled=True),
        lax.all_gather(latent_query, "seq", axis=0, tiled=True),
        lax.all_gather(latent_key, "seq", axis=0, tiled=True),
        lax.all_gather(latent_value, "seq", axis=0, tiled=True),
        lax.all_gather(cross_out, "seq", axis=1, tiled=True),
        lax.all_gather(latent_out, "seq", axis=1, tiled=True),
    )
    latent_width = cross_out.shape[1]
    local_width = cross_out.shape[0]
    head_count = local_width // HEAD_DIM
    slot_count = 2 * PATCH_DEV
    byte_count = byte_states.shape[0]
    first_patch = byte_patch[0]
    slot_of = byte_patch - first_patch
    onehot_mask = slot_of[:, None] == jnp.arange(slot_count, dtype=jnp.int32)[None, :]
    onehot = onehot_mask.astype(jnp.bfloat16)
    onehot_float = onehot_mask.astype(jnp.float32)
    byte_sums = lax.dot_general(
        onehot, byte_states, (((0,), (0,)), ((), ())), preferred_element_type=jnp.float32
    )
    lengths_all = jnp.concatenate([patch_len, jnp.ones((slot_count,), jnp.int32)])
    lengths = lax.dynamic_slice_in_dim(lengths_all, first_patch, slot_count)
    pooled = (byte_sums / lengths.astype(jnp.float32)[:, None]).astype(jnp.bfloat16)
    query_slots = jnp.dot(pooled, cross_query, preferred_element_type=jnp.float32).astype(
        jnp.bfloat16
    )
    byte_keys = jnp.dot(byte_states, cross_key, preferred_element_type=jnp.float32).astype(
        jnp.bfloat16
    )
    byte_values = jnp.dot(byte_states, cross_value, preferred_element_type=jnp.float32).astype(
        jnp.bfloat16
    )
    query_bytes = jnp.dot(onehot, query_slots, preferred_element_type=jnp.float32)
    scores = (query_bytes * byte_keys.astype(jnp.float32)).reshape(
        byte_count, head_count, HEAD_DIM
    ).sum(axis=2) / math.sqrt(HEAD_DIM)
    byte_raw = capped_exp(scores)
    totals = contract_rows(onehot_float, byte_raw)
    totals = jnp.where(totals > 0.0, totals, 1.0)
    totals_bytes = jnp.dot(
        onehot_float, totals, precision=lax.Precision.HIGHEST, preferred_element_type=jnp.float32
    )
    byte_weight = (byte_raw / totals_bytes).astype(jnp.bfloat16)
    weighted = (
        byte_weight.astype(jnp.float32)[:, :, None]
        * byte_values.astype(jnp.float32).reshape(byte_count, head_count, HEAD_DIM)
    ).reshape(byte_count, local_width)
    cross_heads = contract_rows(onehot_float, weighted).astype(jnp.bfloat16)
    padding = jnp.zeros((2 * PATCH_DEV, cross_heads.shape[1]), cross_heads.dtype)
    padded = jnp.concatenate([padding, cross_heads, padding], axis=0)
    offset = seq_index * PATCH_DEV - first_patch + 2 * PATCH_DEV
    padded, offset = (padded, offset)
    owned_heads = lax.dynamic_slice_in_dim(padded, offset, PATCH_DEV, 0)
    for offset_step in (-1, 1):
        window = lax.dynamic_slice_in_dim(padded, offset + offset_step * PATCH_DEV, PATCH_DEV, 0)
        owned_heads = owned_heads + shifted(window, "seq", offset_step)
    partial_value = jnp.dot(owned_heads, cross_out, preferred_element_type=jnp.float32)
    latent_in = lax.psum(partial_value, "tensor").astype(jnp.bfloat16)
    hidden = latent_in.astype(jnp.float32)
    mean_square = jnp.mean(hidden * hidden, axis=1, keepdims=True)
    normed = (hidden * lax.rsqrt(mean_square + norm_eps) * norm_gain[None, :]).astype(jnp.bfloat16)
    query = (
        jnp.dot(normed, latent_query, preferred_element_type=jnp.float32)
        .astype(jnp.bfloat16)
        .reshape(PATCH_DEV, head_count, HEAD_DIM)
    )
    key_rows = jnp.dot(normed, latent_key, preferred_element_type=jnp.float32).astype(jnp.bfloat16)
    value_rows = jnp.dot(normed, latent_value, preferred_element_type=jnp.float32).astype(
        jnp.bfloat16
    )
    positions = seq_index * PATCH_DEV + jnp.arange(PATCH_DEV, dtype=jnp.int32)
    key_piece = lax.all_gather(key_rows, "seq", axis=0, tiled=True)
    value_piece = lax.all_gather(value_rows, "seq", axis=0, tiled=True)
    piece_rows = key_piece.shape[0]
    key_piece = key_piece.reshape(piece_rows, head_count, HEAD_DIM)
    value_piece = value_piece.reshape(piece_rows, head_count, HEAD_DIM)
    piece_scores = jnp.einsum(
        "qhd,khd->hqk", query, key_piece, preferred_element_type=jnp.float32
    ) / math.sqrt(HEAD_DIM)
    key_positions = jnp.arange(piece_rows, dtype=jnp.int32)
    allowed = key_positions[None, :] <= positions[:, None]
    exp_scores = jnp.where(allowed[None, :, :], capped_exp(piece_scores), 0.0)
    denominator = jnp.sum(exp_scores, axis=2)
    numerator = jnp.einsum(
        "hqk,khd->hqd",
        exp_scores.astype(jnp.bfloat16),
        value_piece,
        preferred_element_type=jnp.float32,
    )
    numerator, denominator = (numerator, denominator)
    attended = (numerator / denominator[:, :, None]).astype(jnp.bfloat16)
    attended = attended.transpose(1, 0, 2).reshape(PATCH_DEV, local_width)
    projected = jnp.dot(attended, latent_out, preferred_element_type=jnp.float32)
    mixed_sum = lax.psum_scatter(projected, "tensor", scatter_dimension=1, tiled=True)
    column_width = latent_width // tensor_count
    residual = lax.dynamic_slice_in_dim(
        hidden, lax.axis_index("tensor") * column_width, column_width, 1
    )
    return (residual + mixed_sum).astype(jnp.bfloat16)


def dot(left, right):
    return jnp.dot(left, right, preferred_element_type=jnp.float32)


def exchanged(block, axis, distance):
    route = [(i, i ^ distance) for i in range(lax.axis_size(axis))]
    return lax.ppermute(block, axis, route)


def core_swapped(block):
    return exchanged(block, "seq", 1)


def after(value, *earlier):
    return lax.optimization_barrier((value, *earlier))[0]


def place():
    seq = lax.axis_index("seq")
    return seq // 2, lax.rem(seq, 2), lax.axis_index("tensor")


def aligned(index, size):
    return pl.ds(pl.multiple_of(index * size, size), size)


def fetched(pairs, semaphores):
    copies = [
        pltpu.make_async_copy(source, target, semaphores.at[n])
        for n, (source, target) in enumerate(pairs)
    ]
    for copy in copies:
        copy.start()
    return copies


def call(kernel, outs, *operands, far=0, scratch=(), flops=0):
    shapes = [jax.ShapeDtypeStruct(shape, dtype) for shape, dtype in outs]
    moved = sum(o.size * o.dtype.itemsize for o in [*operands, *shapes])
    return pl.pallas_call(
        kernel,
        out_shape=shapes,
        in_specs=[pl.BlockSpec(memory_space=pltpu.VMEM)] * (len(operands) - far)
        + [pl.BlockSpec(memory_space=pl.ANY)] * far,
        out_specs=[pl.BlockSpec(memory_space=pltpu.VMEM)] * len(outs),
        scratch_shapes=list(scratch),
        compiler_params=pltpu.CompilerParams(vmem_limit_bytes=28 * 1024 * 1024),
        cost_estimate=pl.CostEstimate(flops=flops, bytes_accessed=moved, transcendentals=0),
    )(*operands)


def assemble(pieces, whole):
    chip, core, _ = place()
    for n, piece in enumerate(pieces):
        index = 2 * (chip ^ (n // 2)) + (core ^ (n % 2))
        whole[aligned(index, piece.shape[0]), :] = piece[...]


def plane_rows(pieces, whole):
    chip, core, _ = place()
    return [
        (piece, whole.at[aligned(2 * (chip ^ (n // 2)) + (core ^ (n % 2)), piece.shape[0]), :])
        for n, piece in enumerate(pieces)
    ]


def query_kernel(count, slot_row, lengths, states, *refs):
    pieces, (query, held, whole, semaphores) = refs[:count], refs[count:]
    slots, byte_count = query.shape[0], states.shape[0]
    copies = fetched([(states, held), *plane_rows(pieces, whole)], semaphores)
    index = lax.broadcasted_iota(jnp.int32, (slots, byte_count), 0)
    onehot = (index == slot_row[...]).astype(jnp.bfloat16)
    copies[0].wait()
    pooled = (dot(onehot, held[...]) / lengths[...]).astype(jnp.bfloat16)
    for copy in copies[1:]:
        copy.wait()
    query[...] = dot(pooled, whole[...]).astype(jnp.bfloat16)


def cross_kernel(count, tile, slot_row, query, states, *refs):
    pieces, (own, above, below, *scratch) = refs[: 2 * count], refs[2 * count :]
    held, key_weight, value_weight, totals, summed, semaphores = scratch
    slots, width = query.shape
    spill = above.shape[0]
    head_count = width // HEAD_DIM
    pairs = [(states, held)]
    pairs += plane_rows(pieces[:count], key_weight) + plane_rows(pieces[count:], value_weight)
    copies = fetched(pairs, semaphores)
    totals[...] = jnp.zeros_like(totals)
    summed[...] = jnp.zeros_like(summed)
    for copy in copies:
        copy.wait()

    @pl.loop(0, states.shape[0] // tile)
    def _(step):
        span = aligned(step, tile)
        block = held[span, :]
        keys = dot(block, key_weight[...]).astype(jnp.bfloat16).astype(jnp.float32)
        index = lax.broadcasted_iota(jnp.int32, (slots, tile), 0)
        onehot = (index == slot_row[:, span]).astype(jnp.bfloat16)
        product = keys * lax.dot_general(
            onehot, query[...], (((0,), (0,)), ((), ())), preferred_element_type=jnp.float32
        )
        lane = lax.broadcasted_iota(jnp.int32, (tile, HEAD_DIM), 1)
        scores = jnp.zeros((tile, HEAD_DIM), jnp.float32)
        for head in range(head_count):
            total = jnp.sum(
                product[:, head * HEAD_DIM : (head + 1) * HEAD_DIM], axis=1, keepdims=True
            )
            scores = jnp.where(lane == head, total, scores)
        raw = capped_exp(scores / math.sqrt(HEAD_DIM))
        high = raw.astype(jnp.bfloat16)
        low = (raw - high.astype(jnp.float32)).astype(jnp.bfloat16)
        totals[...] += dot(onehot, high) + dot(onehot, low)
        values = dot(block, value_weight[...]).astype(jnp.bfloat16).astype(jnp.float32)
        weighted = jnp.concatenate(
            [
                (values[:, h * HEAD_DIM : (h + 1) * HEAD_DIM] * raw[:, h : h + 1]).astype(
                    jnp.bfloat16
                )
                for h in range(head_count)
            ],
            axis=1,
        )
        summed[...] += dot(onehot, weighted)

    total = totals[...]
    inverse = 1.0 / jnp.where(total > 0.0, total, 1.0)
    for h in range(head_count):
        part = slice(h * HEAD_DIM, (h + 1) * HEAD_DIM)
        heads = (summed[:, part] * inverse[:, h : h + 1]).astype(jnp.bfloat16)
        above[:, part] = heads[:spill]
        own[:, part] = heads[spill : slots - spill]
        below[:, part] = heads[slots - spill :]


def quarters(left, weight, outs):
    _, _, tensor = place()
    height = outs[0].shape[0]
    for r, out in enumerate(outs):
        block = left[aligned(tensor ^ r, height), :]
        out[...] = dot(block, weight[...]).astype(out.dtype)


def cross_out_kernel(count, weight, *refs):
    pieces, outs, whole = refs[:count], refs[count:-1], refs[-1]
    assemble(pieces, whole)
    quarters(whole, weight, outs)


def latent_out_kernel(count, *refs):
    chips = count // 2
    pieces, weights, refs = refs[:count], refs[count : count + chips], refs[count + chips :]
    outs, (whole, held, products_of, semaphores) = refs[:chips], refs[chips:]
    chip, core, tensor = place()
    copies = fetched([(weight, held.at[d]) for d, weight in enumerate(weights)], semaphores)
    for n, piece in enumerate(pieces):
        index = chips * (core ^ (n % 2)) + (chip ^ (n // 2))
        whole[:, aligned(index, HEAD_DIM)] = piece[...]
    height = whole.shape[0]
    for d, copy in enumerate(copies):
        copy.wait()
        products_of[aligned(chip ^ d, height), :] = dot(whole[...], held[d])
    for r, out in enumerate(outs):
        out[...] = products_of[aligned(tensor ^ r, height), :].astype(out.dtype)


def arrange_kernel(*refs):
    weights, outs, semaphores = refs[:6], refs[6:-1], refs[-1]
    chip, core, _ = place()
    height = weights[0].shape[0]
    copies = fetched(
        [
            (
                weights[2 * m + n].at[:, aligned(len(outs) * core + (chip ^ d), HEAD_DIM)],
                out.at[n * height : (n + 1) * height, m * HEAD_DIM : (m + 1) * HEAD_DIM],
            )
            for d, out in enumerate(outs)
            for m in range(3)
            for n in range(2)
        ],
        semaphores,
    )
    for copy in copies:
        copy.wait()


def diagonal(size):
    return lax.broadcasted_iota(jnp.int32, (size, size), 0) == lax.broadcasted_iota(
        jnp.int32, (size, size), 1
    )


def project_kernel(count, gain, *refs):
    blocks, refs = refs[: 2 * count], refs[2 * count :]
    chips = (len(refs) - 1) // 2
    weights, outs, left = refs[:chips], refs[chips:-1], refs[-1]
    seq = lax.axis_index("seq")
    part, width = blocks[0].shape
    height = count * part
    totals = []
    for q in range(count):
        total = jnp.zeros((part, 1), jnp.float32)
        for n, block in enumerate(blocks[2 * q : 2 * q + 2]):
            hidden = block[...].astype(jnp.float32)
            total += jnp.sum(hidden * hidden, axis=1, keepdims=True)
            left[q * part : (q + 1) * part, n * width : (n + 1) * width] = (
                hidden * gain[:, aligned(seq ^ n, width)]
            ).astype(jnp.bfloat16)
        totals.append(jnp.sum(jnp.where(diagonal(part), total, 0.0), axis=0, keepdims=True))
    for weight, out in reversed(list(zip(weights, outs))):
        out[:height, :] = dot(left[...], weight[...]).astype(out.dtype)
    outs[0][height:, :] = jnp.zeros((outs[0].shape[0] - height, outs[0].shape[1]), jnp.float32)
    for out in outs[1:]:
        out[height:, :] = jnp.zeros((out.shape[0] - height, out.shape[1]), jnp.bfloat16)
    index = lax.broadcasted_iota(jnp.int32, (16, part), 0)
    own_sums, sent_sums = jnp.zeros((8, part), jnp.float32), jnp.zeros((16, part), jnp.float32)
    for q, row in enumerate(totals):
        high = row.astype(jnp.bfloat16).astype(jnp.float32)
        middle = (row - high).astype(jnp.bfloat16).astype(jnp.float32)
        own_sums = jnp.where(index[:8] == q, row, own_sums)
        for m, term in enumerate((high, middle, row - high - middle)):
            sent_sums = jnp.where(index == 3 * q + m, term, sent_sums)
    outs[0][height:, :part] = own_sums
    for out in outs[1:]:
        out[height:, :part] = sent_sums.astype(jnp.bfloat16)


def attention_kernel(groups, chips, depth, *refs):
    shares, refs = refs[: len(groups) * chips], refs[len(groups) * chips :]
    outs, (query, key, value, attended) = refs[:chips], refs[chips:]
    chip, _, tensor = place()
    parts = sum(len(group) for group in groups)
    height = attended.shape[0] // parts
    own_place = diagonal(height)
    for g, group in enumerate(groups):
        end = len(group) * height
        own, *received = shares[g * chips : (g + 1) * chips]
        for q, r in enumerate(group):
            rows = slice(q * height, (q + 1) * height)
            total = own[rows, :]
            row = own[end:, :height][q : q + 1]
            for share in received:
                total += share[rows, :].astype(jnp.float32)
                terms = share[end:, :height].astype(jnp.float32)
                row += sum(terms[3 * q + m : 3 * q + m + 1] for m in range(3))
            column = jnp.sum(jnp.where(own_place, row, 0.0), axis=1, keepdims=True)
            total = (total * lax.rsqrt(column / depth + norm_eps)).astype(jnp.bfloat16)
            span = aligned(tensor ^ r, height)
            for m, kept in enumerate((query, key, value)):
                kept[span, :] = total[:, m * HEAD_DIM : (m + 1) * HEAD_DIM]
    causal = lax.broadcasted_iota(jnp.int32, (height, height), 0) >= lax.broadcasted_iota(
        jnp.int32, (height, height), 1
    )
    for i in range(parts):
        block = query[i * height : (i + 1) * height, :]
        numerator = jnp.zeros((height, HEAD_DIM), jnp.float32)
        denominator = jnp.zeros((height, 1), jnp.float32)
        for j in range(i + 1):
            span = slice(j * height, (j + 1) * height)
            scores = lax.dot_general(
                block, key[span, :], (((1,), (1,)), ((), ())), preferred_element_type=jnp.float32
            )
            raw = capped_exp(scores / math.sqrt(HEAD_DIM))
            if i == j:
                raw = jnp.where(causal, raw, 0.0)
            denominator += jnp.sum(raw, axis=1, keepdims=True)
            numerator += dot(raw.astype(jnp.bfloat16), value[span, :])
        attended[i * height : (i + 1) * height, :] = (numerator / denominator).astype(jnp.bfloat16)
    for d, out in enumerate(outs):
        out[...] = attended[aligned(chip ^ d, out.shape[0]), :]


def final_kernel(own, latent, *refs):
    received, outs, whole = refs[:-3], refs[-3:-1], refs[-1]
    chip, core, tensor = place()
    total = own[...] + jnp.where(chip == tensor, latent[...].astype(jnp.float32), 0.0)
    for block in received:
        total += block[...].astype(jnp.float32)
    whole[...] = total
    height = outs[0].shape[0]
    for flip, out in enumerate(outs):
        out[...] = whole[aligned(core ^ flip, height), :].astype(jnp.bfloat16)


def per_device(
    byte_states,
    byte_patch,
    patch_len,
    cross_query,
    cross_key,
    cross_value,
    cross_out,
    norm_gain,
    latent_query,
    latent_key,
    latent_value,
    latent_out,
):
    seq = lax.axis_index("seq")
    core = lax.rem(seq, 2)
    seq_count = lax.axis_size("seq")
    tensor_count = lax.axis_size("tensor")
    chip_count = seq_count // 2
    patch_count = patch_len.shape[0]
    patch_dev = patch_count // seq_count
    spill = patch_dev // 2
    slot_count = patch_dev + 2 * spill
    byte_count, byte_width = byte_states.shape
    local_width = cross_query.shape[1]
    out_width = cross_out.shape[1]
    quarter = patch_count // tensor_count
    bf16, f32 = jnp.bfloat16, jnp.float32
    tile = min(1024, byte_count)

    def over_plane(block, earlier=(), last_hop=None):
        moved = [block]
        for d in range(1, chip_count):
            hop = last_hop(d) if last_hop else d
            moved.append(exchanged(moved[d ^ hop], "seq", 2 * hop))
        pieces = []
        for d, part in enumerate(moved):
            pieces += [part, core_swapped(after(part, *earlier) if d else part)]
        return pieces

    slot_of = byte_patch - (seq * patch_dev - spill)
    slot_row = slot_of[None, :]
    edge = jnp.ones((spill,), jnp.int32)
    lengths = lax.dynamic_slice_in_dim(
        jnp.concatenate([edge, patch_len, edge]), seq * patch_dev, slot_count
    ).astype(f32)[:, None]
    query_pieces = over_plane(cross_query)
    (query_slots,) = call(
        functools.partial(query_kernel, seq_count),
        [((slot_count, local_width), bf16)],
        slot_row,
        lengths,
        byte_states,
        *query_pieces,
        far=1 + seq_count,
        scratch=[
            pltpu.VMEM((byte_count, byte_width), bf16),
            pltpu.VMEM((byte_width, local_width), bf16),
            pltpu.SemaphoreType.DMA((1 + seq_count,)),
        ],
        flops=2 * slot_count * byte_width * (byte_count + local_width),
    )
    key_pieces = over_plane(cross_key, (query_slots,), lambda d: 1 << (d.bit_length() - 1))
    value_pieces = over_plane(cross_value, (query_slots,), lambda d: d & -d)

    near = (key_pieces[-2], value_pieces[-2])
    weights = []
    for weight in (latent_query, latent_key, latent_value):
        weights += [weight, core_swapped(after(weight, *near))]
    out_weights = [latent_out, exchanged(after(latent_out, *near), "seq", 2 * (chip_count - 1))]
    own, above, below = call(
        functools.partial(cross_kernel, seq_count, tile),
        [((height, local_width), bf16) for height in (patch_dev, spill, spill)],
        slot_row,
        query_slots,
        byte_states,
        *key_pieces,
        *value_pieces,
        far=1 + 2 * seq_count,
        scratch=[
            pltpu.VMEM((byte_count, byte_width), bf16),
            pltpu.VMEM((byte_width, local_width), bf16),
            pltpu.VMEM((byte_width, local_width), bf16),
            pltpu.VMEM((slot_count, HEAD_DIM), f32),
            pltpu.VMEM((slot_count, local_width), f32),
            pltpu.SemaphoreType.DMA((1 + 2 * seq_count,)),
        ],
        flops=4 * byte_count * local_width * (byte_width + slot_count),
    )

    spilled = [shifted(below, "seq", 1), shifted(above, "seq", -1)]
    own, out_weights[-1] = lax.optimization_barrier((own, out_weights[-1]))
    own = own + jnp.concatenate(spilled, axis=0)

    total, *sent = call(
        functools.partial(cross_out_kernel, seq_count),
        [((quarter, out_width), f32 if r == 0 else bf16) for r in range(tensor_count)],
        cross_out,
        *over_plane(own),
        scratch=[pltpu.VMEM((patch_count, local_width), bf16)],
        flops=2 * patch_count * local_width * out_width,
    )
    received = [exchanged(block, "tensor", r) for r, block in enumerate(sent, 1)]

    head_weights = call(
        arrange_kernel,
        [((2 * out_width, 3 * HEAD_DIM), bf16)] * chip_count,
        *[after(weight, total) for weight in weights],
        far=6,
        scratch=[pltpu.SemaphoreType.DMA((6 * chip_count,))],
    )
    for d in range(1, chip_count - 1):
        out_weights.insert(d, exchanged(after(latent_out, total), "seq", 2 * d))
    total, *rest = lax.optimization_barrier((total, *head_weights, *out_weights))
    head_weights, out_weights = rest[:chip_count], rest[chip_count:]
    for share in received:
        total = total + share.astype(f32)
    latent_in = total.astype(bf16)

    gain = norm_gain[None, :]
    groups = [[0], list(range(1, min(3, tensor_count))), list(range(3, tensor_count))]
    groups = [group for group in groups if group]
    shares, arrived, latent_blocks = [], [], [latent_in]
    for g, group in enumerate(groups):
        blocks = [latent_in]
        if g:
            start = after(latent_in, *arrived, *shares[:chip_count]) if g > 1 else latent_in
            arrived = [exchanged(start, "tensor", r) for r in group]
            latent_blocks += arrived
            blocks = [after(block, *shares[:chip_count]) for block in arrived]
        height = len(group) * quarter
        share, *sent = call(
            functools.partial(project_kernel, len(group)),
            [((height + 8, 3 * HEAD_DIM), f32)]
            + [((height + 16, 3 * HEAD_DIM), bf16)] * (chip_count - 1),
            gain,
            *[piece for block in blocks for piece in (block, core_swapped(block))],
            *head_weights,
            scratch=[pltpu.VMEM((height, 2 * out_width), bf16)],
            flops=2 * height * 2 * out_width * 3 * HEAD_DIM * chip_count,
        )
        if g > 1:
            sent[2:] = [after(part, *shares[(g - 1) * chip_count + 1 :]) for part in sent[2:]]
        shares += [share] + [exchanged(part, "seq", 2 * d) for d, part in enumerate(sent, 1)]
    attended = call(
        functools.partial(attention_kernel, groups, chip_count, out_width * seq_count),
        [((quarter, HEAD_DIM), bf16)] * chip_count,
        *shares,
        scratch=[pltpu.VMEM((patch_count, HEAD_DIM), bf16)] * 4,
        flops=2 * patch_count * patch_count * HEAD_DIM,
    )

    pieces = []
    for d, block in enumerate(attended):
        moved = exchanged(block, "seq", 2 * d) if d else block
        pieces += [moved, core_swapped(moved)]
    total, *sent = call(
        functools.partial(latent_out_kernel, seq_count),
        [((quarter, out_width), bf16 if r else f32) for r in range(tensor_count)],
        *pieces,
        *out_weights,
        far=chip_count,
        scratch=[
            pltpu.VMEM((quarter, local_width), bf16),
            pltpu.VMEM((chip_count, local_width, out_width), bf16),
            pltpu.VMEM((patch_count, out_width), f32),
            pltpu.SemaphoreType.DMA((chip_count,)),
        ],
        flops=2 * quarter * local_width * out_width * chip_count,
    )
    received = [exchanged(block, "tensor", r) for r, block in enumerate(sent, 1)]

    residual = [latent_in]
    for d in range(1, chip_count):
        route = [
            ((2 * t + k) * tensor_count + t, (2 * (t ^ d) + k) * tensor_count + t)
            for t in range(tensor_count)
            for k in range(2)
        ]
        block = after(latent_blocks[d], *(received[:1] if d == chip_count - 1 else [total]))
        residual.append(lax.ppermute(block, ("seq", "tensor"), route))
    same, crossed = call(
        final_kernel,
        [((patch_dev, out_width), bf16)] * 2,
        total,
        *residual,
        *received,
        scratch=[pltpu.VMEM((quarter, out_width), f32)],
    )
    crossed = core_swapped(crossed)
    return jnp.concatenate(
        [jnp.where(core == 0, same, crossed), jnp.where(core == 0, crossed, same)], axis=1
    )


def head_per_device(mesh, heads):
    seq_count, tensor_count = mesh.shape["seq"], mesh.shape["tensor"]
    return (
        heads == seq_count * tensor_count
        and seq_count == 2 * tensor_count
        and tensor_count & (tensor_count - 1) == 0
    )


def solution(mesh):
    specs = (
        P("seq", None),
        P("seq"),
        P(),
        P("seq", "tensor"),
        P("seq", "tensor"),
        P("seq", "tensor"),
        P("tensor", "seq"),
        P(),
        P("seq", "tensor"),
        P("seq", "tensor"),
        P("seq", "tensor"),
        P("tensor", "seq"),
    )

    def whole(*arrays):
        chosen = (
            per_device
            if head_per_device(mesh, arrays[3].shape[1] // HEAD_DIM)
            else per_device_gathered
        )
        return jax.shard_map(
            chosen, mesh=mesh, in_specs=specs, out_specs=P("seq", "tensor"), check_vma=False
        )(*arrays)

    return whole
```

```python
import functools
import math

import jax
import jax.numpy as jnp
from jax import lax
from jax.experimental import pallas as pl
from jax.experimental.pallas import tpu as pltpu
from jax.sharding import PartitionSpec as P

HEAD_DIM = 128
PATCH_DEV = 128


score_cap = 30.0
norm_eps = 1e-05


def shifted(block, axis, distance):
    devices = range(lax.axis_size(axis))
    route = [(i - distance, i) for i in devices if i - distance in devices]
    return lax.ppermute(block, axis, route)


def capped_exp(scores):
    return jnp.exp(score_cap * jnp.tanh(scores / score_cap))


def contract_rows(left, right):
    return lax.dot_general(
        left,
        right,
        (((0,), (0,)), ((), ())),
        precision=lax.Precision.HIGHEST,
        preferred_element_type=jnp.float32,
    )


def per_device_gathered(
    byte_states,
    byte_patch,
    patch_len,
    cross_query,
    cross_key,
    cross_value,
    cross_out,
    norm_gain,
    latent_query,
    latent_key,
    latent_value,
    latent_out,
):
    seq_index = lax.axis_index("seq")
    tensor_count = lax.axis_size("tensor")
    (
        cross_query,
        cross_key,
        cross_value,
        latent_query,
        latent_key,
        latent_value,
        cross_out,
        latent_out,
    ) = (
        lax.all_gather(cross_query, "seq", axis=0, tiled=True),
        lax.all_gather(cross_key, "seq", axis=0, tiled=True),
        lax.all_gather(cross_value, "seq", axis=0, tiled=True),
        lax.all_gather(latent_query, "seq", axis=0, tiled=True),
        lax.all_gather(latent_key, "seq", axis=0, tiled=True),
        lax.all_gather(latent_value, "seq", axis=0, tiled=True),
        lax.all_gather(cross_out, "seq", axis=1, tiled=True),
        lax.all_gather(latent_out, "seq", axis=1, tiled=True),
    )
    latent_width = cross_out.shape[1]
    local_width = cross_out.shape[0]
    head_count = local_width // HEAD_DIM
    slot_count = 2 * PATCH_DEV
    byte_count = byte_states.shape[0]
    first_patch = byte_patch[0]
    slot_of = byte_patch - first_patch
    onehot_mask = slot_of[:, None] == jnp.arange(slot_count, dtype=jnp.int32)[None, :]
    onehot = onehot_mask.astype(jnp.bfloat16)
    onehot_float = onehot_mask.astype(jnp.float32)
    byte_sums = lax.dot_general(
        onehot, byte_states, (((0,), (0,)), ((), ())), preferred_element_type=jnp.float32
    )
    lengths_all = jnp.concatenate([patch_len, jnp.ones((slot_count,), jnp.int32)])
    lengths = lax.dynamic_slice_in_dim(lengths_all, first_patch, slot_count)
    pooled = (byte_sums / lengths.astype(jnp.float32)[:, None]).astype(jnp.bfloat16)
    query_slots = jnp.dot(pooled, cross_query, preferred_element_type=jnp.float32).astype(
        jnp.bfloat16
    )
    byte_keys = jnp.dot(byte_states, cross_key, preferred_element_type=jnp.float32).astype(
        jnp.bfloat16
    )
    byte_values = jnp.dot(byte_states, cross_value, preferred_element_type=jnp.float32).astype(
        jnp.bfloat16
    )
    query_bytes = jnp.dot(onehot, query_slots, preferred_element_type=jnp.float32)
    scores = (query_bytes * byte_keys.astype(jnp.float32)).reshape(
        byte_count, head_count, HEAD_DIM
    ).sum(axis=2) / math.sqrt(HEAD_DIM)
    byte_raw = capped_exp(scores)
    totals = contract_rows(onehot_float, byte_raw)
    totals = jnp.where(totals > 0.0, totals, 1.0)
    totals_bytes = jnp.dot(
        onehot_float, totals, precision=lax.Precision.HIGHEST, preferred_element_type=jnp.float32
    )
    byte_weight = (byte_raw / totals_bytes).astype(jnp.bfloat16)
    weighted = (
        byte_weight.astype(jnp.float32)[:, :, None]
        * byte_values.astype(jnp.float32).reshape(byte_count, head_count, HEAD_DIM)
    ).reshape(byte_count, local_width)
    cross_heads = contract_rows(onehot_float, weighted).astype(jnp.bfloat16)
    padding = jnp.zeros((2 * PATCH_DEV, cross_heads.shape[1]), cross_heads.dtype)
    padded = jnp.concatenate([padding, cross_heads, padding], axis=0)
    offset = seq_index * PATCH_DEV - first_patch + 2 * PATCH_DEV
    padded, offset = (padded, offset)
    owned_heads = lax.dynamic_slice_in_dim(padded, offset, PATCH_DEV, 0)
    for offset_step in (-1, 1):
        window = lax.dynamic_slice_in_dim(padded, offset + offset_step * PATCH_DEV, PATCH_DEV, 0)
        owned_heads = owned_heads + shifted(window, "seq", offset_step)
    partial_value = jnp.dot(owned_heads, cross_out, preferred_element_type=jnp.float32)
    latent_in = lax.psum(partial_value, "tensor").astype(jnp.bfloat16)
    hidden = latent_in.astype(jnp.float32)
    mean_square = jnp.mean(hidden * hidden, axis=1, keepdims=True)
    normed = (hidden * lax.rsqrt(mean_square + norm_eps) * norm_gain[None, :]).astype(jnp.bfloat16)
    query = (
        jnp.dot(normed, latent_query, preferred_element_type=jnp.float32)
        .astype(jnp.bfloat16)
        .reshape(PATCH_DEV, head_count, HEAD_DIM)
    )
    key_rows = jnp.dot(normed, latent_key, preferred_element_type=jnp.float32).astype(jnp.bfloat16)
    value_rows = jnp.dot(normed, latent_value, preferred_element_type=jnp.float32).astype(
        jnp.bfloat16
    )
    positions = seq_index * PATCH_DEV + jnp.arange(PATCH_DEV, dtype=jnp.int32)
    key_piece = lax.all_gather(key_rows, "seq", axis=0, tiled=True)
    value_piece = lax.all_gather(value_rows, "seq", axis=0, tiled=True)
    piece_rows = key_piece.shape[0]
    key_piece = key_piece.reshape(piece_rows, head_count, HEAD_DIM)
    value_piece = value_piece.reshape(piece_rows, head_count, HEAD_DIM)
    piece_scores = jnp.einsum(
        "qhd,khd->hqk", query, key_piece, preferred_element_type=jnp.float32
    ) / math.sqrt(HEAD_DIM)
    key_positions = jnp.arange(piece_rows, dtype=jnp.int32)
    allowed = key_positions[None, :] <= positions[:, None]
    exp_scores = jnp.where(allowed[None, :, :], capped_exp(piece_scores), 0.0)
    denominator = jnp.sum(exp_scores, axis=2)
    numerator = jnp.einsum(
        "hqk,khd->hqd",
        exp_scores.astype(jnp.bfloat16),
        value_piece,
        preferred_element_type=jnp.float32,
    )
    numerator, denominator = (numerator, denominator)
    attended = (numerator / denominator[:, :, None]).astype(jnp.bfloat16)
    attended = attended.transpose(1, 0, 2).reshape(PATCH_DEV, local_width)
    projected = jnp.dot(attended, latent_out, preferred_element_type=jnp.float32)
    mixed_sum = lax.psum_scatter(projected, "tensor", scatter_dimension=1, tiled=True)
    column_width = latent_width // tensor_count
    residual = lax.dynamic_slice_in_dim(
        hidden, lax.axis_index("tensor") * column_width, column_width, 1
    )
    return (residual + mixed_sum).astype(jnp.bfloat16)


def dot(left, right):
    return jnp.dot(left, right, preferred_element_type=jnp.float32)


def exchanged(block, axis, distance):
    route = [(i, i ^ distance) for i in range(lax.axis_size(axis))]
    return lax.ppermute(block, axis, route)


def core_swapped(block):
    return exchanged(block, "seq", 1)


def after(value, *earlier):
    return lax.optimization_barrier((value, *earlier))[0]


def place():
    seq = lax.axis_index("seq")
    return seq // 2, lax.rem(seq, 2), lax.axis_index("tensor")


def aligned(index, size):
    return pl.ds(pl.multiple_of(index * size, size), size)


def fetched(pairs, semaphores):
    copies = [
        pltpu.make_async_copy(source, target, semaphores.at[n])
        for n, (source, target) in enumerate(pairs)
    ]
    for copy in copies:
        copy.start()
    return copies


def call(kernel, outs, *operands, far=0, scratch=(), flops=0):
    shapes = [jax.ShapeDtypeStruct(shape, dtype) for shape, dtype in outs]
    moved = sum(o.size * o.dtype.itemsize for o in [*operands, *shapes])
    return pl.pallas_call(
        kernel,
        out_shape=shapes,
        in_specs=[pl.BlockSpec(memory_space=pltpu.VMEM)] * (len(operands) - far)
        + [pl.BlockSpec(memory_space=pl.ANY)] * far,
        out_specs=[pl.BlockSpec(memory_space=pltpu.VMEM)] * len(outs),
        scratch_shapes=list(scratch),
        compiler_params=pltpu.CompilerParams(vmem_limit_bytes=28 * 1024 * 1024),
        cost_estimate=pl.CostEstimate(flops=flops, bytes_accessed=moved, transcendentals=0),
    )(*operands)


def assemble(pieces, whole):
    chip, core, _ = place()
    for n, piece in enumerate(pieces):
        index = 2 * (chip ^ (n // 2)) + (core ^ (n % 2))
        whole[aligned(index, piece.shape[0]), :] = piece[...]


def plane_rows(pieces, whole):
    chip, core, _ = place()
    return [
        (piece, whole.at[aligned(2 * (chip ^ (n // 2)) + (core ^ (n % 2)), piece.shape[0]), :])
        for n, piece in enumerate(pieces)
    ]


def query_kernel(count, slot_row, lengths, states, *refs):
    pieces, (query, held, whole, semaphores) = refs[:count], refs[count:]
    slots, byte_count = query.shape[0], states.shape[0]
    copies = fetched([(states, held), *plane_rows(pieces, whole)], semaphores)
    index = lax.broadcasted_iota(jnp.int32, (slots, byte_count), 0)
    onehot = (index == slot_row[...]).astype(jnp.bfloat16)
    copies[0].wait()
    pooled = (dot(onehot, held[...]) / lengths[...]).astype(jnp.bfloat16)
    for copy in copies[1:]:
        copy.wait()
    query[...] = dot(pooled, whole[...]).astype(jnp.bfloat16)


def cross_kernel(count, tile, slot_row, query, states, *refs):
    pieces, (own, above, below, *scratch) = refs[: 2 * count], refs[2 * count :]
    held, key_weight, value_weight, totals, summed, semaphores = scratch
    slots, width = query.shape
    spill = above.shape[0]
    head_count = width // HEAD_DIM
    pairs = [(states, held)]
    pairs += plane_rows(pieces[:count], key_weight) + plane_rows(pieces[count:], value_weight)
    copies = fetched(pairs, semaphores)
    totals[...] = jnp.zeros_like(totals)
    summed[...] = jnp.zeros_like(summed)
    for copy in copies:
        copy.wait()

    @pl.loop(0, states.shape[0] // tile)
    def _(step):
        span = aligned(step, tile)
        block = held[span, :]
        keys = dot(block, key_weight[...]).astype(jnp.bfloat16).astype(jnp.float32)
        index = lax.broadcasted_iota(jnp.int32, (slots, tile), 0)
        onehot = (index == slot_row[:, span]).astype(jnp.bfloat16)
        product = keys * lax.dot_general(
            onehot, query[...], (((0,), (0,)), ((), ())), preferred_element_type=jnp.float32
        )
        lane = lax.broadcasted_iota(jnp.int32, (tile, HEAD_DIM), 1)
        scores = jnp.zeros((tile, HEAD_DIM), jnp.float32)
        for head in range(head_count):
            total = jnp.sum(
                product[:, head * HEAD_DIM : (head + 1) * HEAD_DIM], axis=1, keepdims=True
            )
            scores = jnp.where(lane == head, total, scores)
        raw = capped_exp(scores / math.sqrt(HEAD_DIM))
        high = raw.astype(jnp.bfloat16)
        low = (raw - high.astype(jnp.float32)).astype(jnp.bfloat16)
        totals[...] += dot(onehot, high) + dot(onehot, low)
        values = dot(block, value_weight[...]).astype(jnp.bfloat16).astype(jnp.float32)
        weighted = jnp.concatenate(
            [
                (values[:, h * HEAD_DIM : (h + 1) * HEAD_DIM] * raw[:, h : h + 1]).astype(
                    jnp.bfloat16
                )
                for h in range(head_count)
            ],
            axis=1,
        )
        summed[...] += dot(onehot, weighted)

    total = totals[...]
    inverse = 1.0 / jnp.where(total > 0.0, total, 1.0)
    for h in range(head_count):
        part = slice(h * HEAD_DIM, (h + 1) * HEAD_DIM)
        heads = (summed[:, part] * inverse[:, h : h + 1]).astype(jnp.bfloat16)
        above[:, part] = heads[:spill]
        own[:, part] = heads[spill : slots - spill]
        below[:, part] = heads[slots - spill :]


def quarters(left, weight, outs):
    _, _, tensor = place()
    height = outs[0].shape[0]
    for r, out in enumerate(outs):
        block = left[aligned(tensor ^ r, height), :]
        out[...] = dot(block, weight[...]).astype(out.dtype)


def cross_out_kernel(count, weight, *refs):
    pieces, outs, whole = refs[:count], refs[count:-1], refs[-1]
    assemble(pieces, whole)
    quarters(whole, weight, outs)


def latent_out_kernel(count, *refs):
    chips = count // 2
    pieces, weights, refs = refs[:count], refs[count : count + chips], refs[count + chips :]
    outs, (whole, held, products_of, semaphores) = refs[:chips], refs[chips:]
    chip, core, tensor = place()
    copies = fetched([(weight, held.at[d]) for d, weight in enumerate(weights)], semaphores)
    for n, piece in enumerate(pieces):
        index = chips * (core ^ (n % 2)) + (chip ^ (n // 2))
        whole[:, aligned(index, HEAD_DIM)] = piece[...]
    height = whole.shape[0]
    for d, copy in enumerate(copies):
        copy.wait()
        products_of[aligned(chip ^ d, height), :] = dot(whole[...], held[d])
    for r, out in enumerate(outs):
        out[...] = products_of[aligned(tensor ^ r, height), :].astype(out.dtype)


def arrange_kernel(*refs):
    weights, outs, semaphores = refs[:6], refs[6:-1], refs[-1]
    chip, core, _ = place()
    height = weights[0].shape[0]
    copies = fetched(
        [
            (
                weights[2 * m + n].at[:, aligned(len(outs) * core + (chip ^ d), HEAD_DIM)],
                out.at[n * height : (n + 1) * height, m * HEAD_DIM : (m + 1) * HEAD_DIM],
            )
            for d, out in enumerate(outs)
            for m in range(3)
            for n in range(2)
        ],
        semaphores,
    )
    for copy in copies:
        copy.wait()


def diagonal(size):
    return lax.broadcasted_iota(jnp.int32, (size, size), 0) == lax.broadcasted_iota(
        jnp.int32, (size, size), 1
    )


def project_kernel(count, gain, *refs):
    blocks, refs = refs[: 2 * count], refs[2 * count :]
    chips = (len(refs) - 1) // 2
    weights, outs, left = refs[:chips], refs[chips:-1], refs[-1]
    seq = lax.axis_index("seq")
    part, width = blocks[0].shape
    height = count * part
    totals = []
    for q in range(count):
        total = jnp.zeros((part, 1), jnp.float32)
        for n, block in enumerate(blocks[2 * q : 2 * q + 2]):
            hidden = block[...].astype(jnp.float32)
            total += jnp.sum(hidden * hidden, axis=1, keepdims=True)
            left[q * part : (q + 1) * part, n * width : (n + 1) * width] = (
                hidden * gain[:, aligned(seq ^ n, width)]
            ).astype(jnp.bfloat16)
        totals.append(jnp.sum(jnp.where(diagonal(part), total, 0.0), axis=0, keepdims=True))
    for weight, out in reversed(list(zip(weights, outs))):
        out[:height, :] = dot(left[...], weight[...]).astype(out.dtype)
    outs[0][height:, :] = jnp.zeros((outs[0].shape[0] - height, outs[0].shape[1]), jnp.float32)
    for out in outs[1:]:
        out[height:, :] = jnp.zeros((out.shape[0] - height, out.shape[1]), jnp.bfloat16)
    index = lax.broadcasted_iota(jnp.int32, (16, part), 0)
    own_sums, sent_sums = jnp.zeros((8, part), jnp.float32), jnp.zeros((16, part), jnp.float32)
    for q, row in enumerate(totals):
        high = row.astype(jnp.bfloat16).astype(jnp.float32)
        middle = (row - high).astype(jnp.bfloat16).astype(jnp.float32)
        own_sums = jnp.where(index[:8] == q, row, own_sums)
        for m, term in enumerate((high, middle, row - high - middle)):
            sent_sums = jnp.where(index == 3 * q + m, term, sent_sums)
    outs[0][height:, :part] = own_sums
    for out in outs[1:]:
        out[height:, :part] = sent_sums.astype(jnp.bfloat16)


def attention_kernel(groups, chips, depth, *refs):
    shares, refs = refs[: len(groups) * chips], refs[len(groups) * chips :]
    outs, (query, key, value, attended) = refs[:chips], refs[chips:]
    chip, _, tensor = place()
    parts = sum(len(group) for group in groups)
    height = attended.shape[0] // parts
    own_place = diagonal(height)
    for g, group in enumerate(groups):
        end = len(group) * height
        own, *received = shares[g * chips : (g + 1) * chips]
        for q, r in enumerate(group):
            rows = slice(q * height, (q + 1) * height)
            total = own[rows, :]
            row = own[end:, :height][q : q + 1]
            for share in received:
                total += share[rows, :].astype(jnp.float32)
                terms = share[end:, :height].astype(jnp.float32)
                row += sum(terms[3 * q + m : 3 * q + m + 1] for m in range(3))
            column = jnp.sum(jnp.where(own_place, row, 0.0), axis=1, keepdims=True)
            total = (total * lax.rsqrt(column / depth + norm_eps)).astype(jnp.bfloat16)
            span = aligned(tensor ^ r, height)
            for m, kept in enumerate((query, key, value)):
                kept[span, :] = total[:, m * HEAD_DIM : (m + 1) * HEAD_DIM]
    causal = lax.broadcasted_iota(jnp.int32, (height, height), 0) >= lax.broadcasted_iota(
        jnp.int32, (height, height), 1
    )
    for i in range(parts):
        block = query[i * height : (i + 1) * height, :]
        numerator = jnp.zeros((height, HEAD_DIM), jnp.float32)
        denominator = jnp.zeros((height, 1), jnp.float32)
        for j in range(i + 1):
            span = slice(j * height, (j + 1) * height)
            scores = lax.dot_general(
                block, key[span, :], (((1,), (1,)), ((), ())), preferred_element_type=jnp.float32
            )
            raw = capped_exp(scores / math.sqrt(HEAD_DIM))
            if i == j:
                raw = jnp.where(causal, raw, 0.0)
            denominator += jnp.sum(raw, axis=1, keepdims=True)
            numerator += dot(raw.astype(jnp.bfloat16), value[span, :])
        attended[i * height : (i + 1) * height, :] = (numerator / denominator).astype(jnp.bfloat16)
    for d, out in enumerate(outs):
        out[...] = attended[aligned(chip ^ d, out.shape[0]), :]


def final_kernel(own, latent, *refs):
    received, outs, whole = refs[:-3], refs[-3:-1], refs[-1]
    chip, core, tensor = place()
    total = own[...] + jnp.where(chip == tensor, latent[...].astype(jnp.float32), 0.0)
    for block in received:
        total += block[...].astype(jnp.float32)
    whole[...] = total
    height = outs[0].shape[0]
    for flip, out in enumerate(outs):
        out[...] = whole[aligned(core ^ flip, height), :].astype(jnp.bfloat16)


def per_device(
    byte_states,
    byte_patch,
    patch_len,
    cross_query,
    cross_key,
    cross_value,
    cross_out,
    norm_gain,
    latent_query,
    latent_key,
    latent_value,
    latent_out,
):
    seq = lax.axis_index("seq")
    core = lax.rem(seq, 2)
    seq_count = lax.axis_size("seq")
    tensor_count = lax.axis_size("tensor")
    chip_count = seq_count // 2
    patch_count = patch_len.shape[0]
    patch_dev = patch_count // seq_count
    spill = patch_dev // 2
    slot_count = patch_dev + 2 * spill
    byte_count, byte_width = byte_states.shape
    local_width = cross_query.shape[1]
    out_width = cross_out.shape[1]
    quarter = patch_count // tensor_count
    bf16, f32 = jnp.bfloat16, jnp.float32
    tile = min(1024, byte_count)

    def over_plane(block, earlier=(), last_hop=None):
        moved = [block]
        for d in range(1, chip_count):
            hop = last_hop(d) if last_hop else d
            moved.append(exchanged(moved[d ^ hop], "seq", 2 * hop))
        pieces = []
        for d, part in enumerate(moved):
            pieces += [part, core_swapped(after(part, *earlier) if d else part)]
        return pieces

    slot_of = byte_patch - (seq * patch_dev - spill)
    slot_row = slot_of[None, :]
    edge = jnp.ones((spill,), jnp.int32)
    lengths = lax.dynamic_slice_in_dim(
        jnp.concatenate([edge, patch_len, edge]), seq * patch_dev, slot_count
    ).astype(f32)[:, None]
    query_pieces = over_plane(cross_query)
    (query_slots,) = call(
        functools.partial(query_kernel, seq_count),
        [((slot_count, local_width), bf16)],
        slot_row,
        lengths,
        byte_states,
        *query_pieces,
        far=1 + seq_count,
        scratch=[
            pltpu.VMEM((byte_count, byte_width), bf16),
            pltpu.VMEM((byte_width, local_width), bf16),
            pltpu.SemaphoreType.DMA((1 + seq_count,)),
        ],
        flops=2 * slot_count * byte_width * (byte_count + local_width),
    )
    key_pieces = over_plane(cross_key, (query_slots,), lambda d: 1 << (d.bit_length() - 1))
    value_pieces = over_plane(cross_value, (query_slots,), lambda d: d & -d)

    near = (key_pieces[-2], value_pieces[-2])
    weights = []
    for weight in (latent_query, latent_key, latent_value):
        weights += [weight, core_swapped(after(weight, *near))]
    out_weights = [latent_out, exchanged(after(latent_out, *near), "seq", 2 * (chip_count - 1))]
    own, above, below = call(
        functools.partial(cross_kernel, seq_count, tile),
        [((height, local_width), bf16) for height in (patch_dev, spill, spill)],
        slot_row,
        query_slots,
        byte_states,
        *key_pieces,
        *value_pieces,
        far=1 + 2 * seq_count,
        scratch=[
            pltpu.VMEM((byte_count, byte_width), bf16),
            pltpu.VMEM((byte_width, local_width), bf16),
            pltpu.VMEM((byte_width, local_width), bf16),
            pltpu.VMEM((slot_count, HEAD_DIM), f32),
            pltpu.VMEM((slot_count, local_width), f32),
            pltpu.SemaphoreType.DMA((1 + 2 * seq_count,)),
        ],
        flops=4 * byte_count * local_width * (byte_width + slot_count),
    )

    spilled = [shifted(below, "seq", 1), shifted(above, "seq", -1)]
    own, out_weights[-1] = lax.optimization_barrier((own, out_weights[-1]))
    own = own + jnp.concatenate(spilled, axis=0)

    total, *sent = call(
        functools.partial(cross_out_kernel, seq_count),
        [((quarter, out_width), f32 if r == 0 else bf16) for r in range(tensor_count)],
        cross_out,
        *over_plane(own),
        scratch=[pltpu.VMEM((patch_count, local_width), bf16)],
        flops=2 * patch_count * local_width * out_width,
    )
    received = [exchanged(block, "tensor", r) for r, block in enumerate(sent, 1)]

    head_weights = call(
        arrange_kernel,
        [((2 * out_width, 3 * HEAD_DIM), bf16)] * chip_count,
        *[after(weight, total) for weight in weights],
        far=6,
        scratch=[pltpu.SemaphoreType.DMA((6 * chip_count,))],
    )
    for d in range(1, chip_count - 1):
        out_weights.insert(d, exchanged(after(latent_out, total), "seq", 2 * d))
    total, *rest = lax.optimization_barrier((total, *head_weights, *out_weights))
    head_weights, out_weights = rest[:chip_count], rest[chip_count:]
    for share in received:
        total = total + share.astype(f32)
    latent_in = total.astype(bf16)

    gain = norm_gain[None, :]
    groups = [[0], list(range(1, min(3, tensor_count))), list(range(3, tensor_count))]
    groups = [group for group in groups if group]
    shares, arrived, latent_blocks = [], [], [latent_in]
    for g, group in enumerate(groups):
        blocks = [latent_in]
        if g:
            start = after(latent_in, *arrived, *shares[:chip_count]) if g > 1 else latent_in
            arrived = [exchanged(start, "tensor", r) for r in group]
            latent_blocks += arrived
            blocks = [after(block, *shares[:chip_count]) for block in arrived]
        height = len(group) * quarter
        share, *sent = call(
            functools.partial(project_kernel, len(group)),
            [((height + 8, 3 * HEAD_DIM), f32)]
            + [((height + 16, 3 * HEAD_DIM), bf16)] * (chip_count - 1),
            gain,
            *[piece for block in blocks for piece in (block, core_swapped(block))],
            *head_weights,
            scratch=[pltpu.VMEM((height, 2 * out_width), bf16)],
            flops=2 * height * 2 * out_width * 3 * HEAD_DIM * chip_count,
        )
        if g > 1:
            sent[2:] = [after(part, *shares[(g - 1) * chip_count + 1 :]) for part in sent[2:]]
        shares += [share] + [exchanged(part, "seq", 2 * d) for d, part in enumerate(sent, 1)]
    attended = call(
        functools.partial(attention_kernel, groups, chip_count, out_width * seq_count),
        [((quarter, HEAD_DIM), bf16)] * chip_count,
        *shares,
        scratch=[pltpu.VMEM((patch_count, HEAD_DIM), bf16)] * 4,
        flops=2 * patch_count * patch_count * HEAD_DIM,
    )

    pieces = []
    for d, block in enumerate(attended):
        moved = exchanged(block, "seq", 2 * d) if d else block
        pieces += [moved, core_swapped(moved)]
    total, *sent = call(
        functools.partial(latent_out_kernel, seq_count),
        [((quarter, out_width), bf16 if r else f32) for r in range(tensor_count)],
        *pieces,
        *out_weights,
        far=chip_count,
        scratch=[
            pltpu.VMEM((quarter, local_width), bf16),
            pltpu.VMEM((chip_count, local_width, out_width), bf16),
            pltpu.VMEM((patch_count, out_width), f32),
            pltpu.SemaphoreType.DMA((chip_count,)),
        ],
        flops=2 * quarter * local_width * out_width * chip_count,
    )
    received = [exchanged(block, "tensor", r) for r, block in enumerate(sent, 1)]

    residual = [latent_in]
    for d in range(1, chip_count):
        route = [
            ((2 * t + k) * tensor_count + t, (2 * (t ^ d) + k) * tensor_count + t)
            for t in range(tensor_count)
            for k in range(2)
        ]
        block = after(latent_blocks[d], *(received[:1] if d > 1 else [total]))
        residual.append(lax.ppermute(block, ("seq", "tensor"), route))
    same, crossed = call(
        final_kernel,
        [((patch_dev, out_width), bf16)] * 2,
        total,
        *residual,
        *received,
        scratch=[pltpu.VMEM((quarter, out_width), f32)],
    )
    crossed = core_swapped(crossed)
    return jnp.concatenate(
        [jnp.where(core == 0, same, crossed), jnp.where(core == 0, crossed, same)], axis=1
    )


def head_per_device(mesh, heads):
    seq_count, tensor_count = mesh.shape["seq"], mesh.shape["tensor"]
    return (
        heads == seq_count * tensor_count
        and seq_count == 2 * tensor_count
        and tensor_count & (tensor_count - 1) == 0
    )


def solution(mesh):
    specs = (
        P("seq", None),
        P("seq"),
        P(),
        P("seq", "tensor"),
        P("seq", "tensor"),
        P("seq", "tensor"),
        P("tensor", "seq"),
        P(),
        P("seq", "tensor"),
        P("seq", "tensor"),
        P("seq", "tensor"),
        P("tensor", "seq"),
    )

    def whole(*arrays):
        chosen = (
            per_device
            if head_per_device(mesh, arrays[3].shape[1] // HEAD_DIM)
            else per_device_gathered
        )
        return jax.shard_map(
            chosen, mesh=mesh, in_specs=specs, out_specs=P("seq", "tensor"), check_vma=False
        )(*arrays)

    return whole
```
